32 devices in a mesh: seq: 16 (over z, y, x), wsh: 2 (over core).
Axes of the slice: x: 2, y: 2, z: 4, core: 2. Of those that a mesh axis runs over, the one named last changes fastest.
Arguments:
- tokens: float32 [4, 1024, 1024], P('wsh', 'seq'), may hold values from -6 to 6
- doc_start: int32 [4, 1024], P('wsh', 'seq'), may hold values from 0 to 1023, as said below
- cotangent: float32 [4, 1024, 1024], P('wsh', 'seq'), may hold values from -6 to 6
- mix_gain: float32 [1024], replicated, may hold values from 0.5 to 1.5
- in_proj: bfloat16 [1024, 3072], P(None, 'wsh'), may hold values from -0.1875 to 0.1875
- conv_taps: float32 [3, 1024], replicated, may hold values from -3 to 3
- mix_proj: bfloat16 [1024, 1024], P(None, 'wsh'), may hold values from -0.1875 to 0.1875
- ffn_gain_a: float32 [1024], replicated, may hold values from 0.5 to 1.5
- gate_a: bfloat16 [1024, 4608], P(None, 'wsh'), may hold values from -0.1875 to 0.1875
- up_a: bfloat16 [1024, 4608], P(None, 'wsh'), may hold values from -0.1875 to 0.1875
- down_a: bfloat16 [4608, 1024], P(None, 'wsh'), may hold values from -0.09375 to 0.09375
- attn_gain: float32 [1024], replicated, may hold values from 0.5 to 1.5
- query_proj: bfloat16 [1024, 1024], P(None, 'wsh'), may hold values from -0.1875 to 0.1875
- key_proj: bfloat16 [1024, 512], P(None, 'wsh'), may hold values from -0.1875 to 0.1875
- value_proj: bfloat16 [1024, 512], P(None, 'wsh'), may hold values from -0.1875 to 0.1875
- attn_proj: bfloat16 [1024, 1024], P(None, 'wsh'), may hold values from -1 to 1
- query_gain: float32 [64], replicated, may hold values from 0.5 to 1.5
- key_gain: float32 [64], replicated, may hold values from 0.5 to 1.5
- ffn_gain_b: float32 [1024], replicated, may hold values from 0.5 to 1.5
- gate_b: bfloat16 [1024, 4608], P(None, 'wsh'), may hold values from -0.1875 to 0.1875
- up_b: bfloat16 [1024, 4608], P(None, 'wsh'), may hold values from -0.1875 to 0.1875
- down_b: bfloat16 [4608, 1024], P(None, 'wsh'), may hold values from -0.09375 to 0.09375
Outputs:
- output: float32 [4, 1024, 1024], P('wsh', 'seq')
- tokens_grad: float32 [4, 1024, 1024], P('wsh', 'seq')
- mix_gain_grad: float32 [1024], replicated
- in_proj_grad: float32 [1024, 3072], P('seq', 'wsh')
- conv_taps_grad: float32 [3, 1024], replicated
- mix_proj_grad: float32 [1024, 1024], P('seq', 'wsh')
- ffn_gain_a_grad: float32 [1024], replicated
- gate_a_grad: float32 [1024, 4608], P('seq', 'wsh')
- up_a_grad: float32 [1024, 4608], P('seq', 'wsh')
- down_a_grad: float32 [4608, 1024], P('wsh', 'seq')
- attn_gain_grad: float32 [1024], replicated
- query_proj_grad: float32 [1024, 1024], P('seq', 'wsh')
- key_proj_grad: float32 [1024, 512], P('seq', 'wsh')
- value_proj_grad: float32 [1024, 512], P('seq', 'wsh')
- attn_proj_grad: float32 [1024, 1024], P('seq', 'wsh')
- query_gain_grad: float32 [64], replicated
- key_gain_grad: float32 [64], replicated
- ffn_gain_b_grad: float32 [1024], replicated
- gate_b_grad: float32 [1024, 4608], P('seq', 'wsh')
- up_b_grad: float32 [1024, 4608], P('seq', 'wsh')
- down_b_grad: float32 [4608, 1024], P('wsh', 'seq')
The draws below stay inside these ranges and needn't reach their ends.
Inputs may be any that keep to these rules, and one draw needn't show every extreme that they name: `doc_start`: each entry is the position of the first token of its document: entries never fall along a sequence, each equals the one before it or its own position, and the first is 0. In each run of 2 consecutive sequences starting at sequence 0, one, which one varies, is a single document; in each of the others the last token begins a document of its own.
All inputs are finite; a program needn't handle non-finite values.
Results may differ from the reference program's by a relative error of at most 0.025.
Values may be sent and summed in bfloat16 or wider, within the bound.
No kernel may reach another device: no remote copies, remote signals or barrier semaphores. Data moves between devices by JAX's collectives and lax.ppermute only.
A program may use at most 640 MiB of HBM per device.

```python
import jax
import jax.numpy as jnp
from jax import lax

D = 1024
FF = 4608
HEADS = 16
KV_HEADS = 8
HEAD_DIM = 64
CONV_K = 3
STREAMS = 2
SEQS = 4
LEN = 1024


def draw_doc_start(key, part):
    key = jax.random.fold_in(key, 11)
    pick_key, cut_key = jax.random.split(key)
    groups_count = SEQS // STREAMS
    whole_doc = jax.random.randint(pick_key, (groups_count,), 0, STREAMS)
    places = jnp.arange(LEN, dtype=jnp.int32)
    cut_here = jax.random.randint(cut_key, (groups_count, STREAMS, LEN), 0, LEN) < 8
    cut_here = cut_here | (places == LEN - 1)[None, None, :]
    others = (jnp.arange(STREAMS, dtype=jnp.int32)[None, :] != whole_doc[:, None])[:, :, None]
    cut_here = cut_here & others | (places == 0)[None, None, :]
    start_marks = jnp.where(cut_here, places[None, None, :], 0)
    starts = lax.cummax(start_marks, axis=2)
    return starts.reshape(SEQS, LEN).astype(jnp.int32)


def block_levels(own_key, extent, cuts, low, top_value):
    loudness = 1.0
    for dim, blocks in cuts:
        steps = jax.random.uniform(jax.random.fold_in(jax.random.fold_in(own_key, 6), dim), (blocks,), jnp.float32, low / len(cuts), top_value / len(cuts))
        loudness = loudness * jnp.repeat(jnp.exp(steps), extent[dim] // blocks).reshape((-1,) + (1,) * (len(extent) - 1 - dim))
    return loudness


def gaussian(key, shape, width, reach, cuts=(), kind=jnp.bfloat16):
    values = width * jax.random.normal(key, shape, jnp.float32)
    if cuts:
        values = values * block_levels(key, shape, cuts, -0.22, 0.18)
    return jnp.clip(values, -reach, reach).astype(kind)


def setup_inputs(seed: int = 0) -> dict:
    key_of = jax.random.split(jax.random.key(seed), 23)
    return {
        "tokens": gaussian(key_of[0], (SEQS, LEN, D), 1.0, 6.0, ((0, 2), (1, 16)), jnp.float32),
        "doc_start": draw_doc_start(jax.random.fold_in(key_of[22], 71), 0),
        "cotangent": gaussian(key_of[2], (SEQS, LEN, D), 1.0, 6.0, ((0, 2), (1, 16)), jnp.float32),
        "mix_gain": jnp.clip(1.0 + 0.1 * jax.random.normal(key_of[3], (D,), jnp.float32), 0.5, 1.5),
        "in_proj": gaussian(key_of[4], (D, 3 * D), D ** -0.5, 0.1875, ((1, 2),)),
        "conv_taps": gaussian(key_of[5], (CONV_K, D), 0.6, 3.0, (), jnp.float32),
        "mix_proj": gaussian(key_of[6], (D, D), D ** -0.5, 0.1875, ((1, 2),)),
        "ffn_gain_a": jnp.clip(1.0 + 0.1 * jax.random.normal(key_of[7], (D,), jnp.float32), 0.5, 1.5),
        "gate_a": gaussian(key_of[8], (D, FF), D ** -0.5, 0.1875, ((1, 2),)),
        "up_a": gaussian(key_of[9], (D, FF), D ** -0.5, 0.1875, ((1, 2),)),
        "down_a": gaussian(key_of[10], (FF, D), FF ** -0.5, 0.09375, ((1, 2),)),
        "attn_gain": jnp.clip(1.0 + 0.1 * jax.random.normal(key_of[11], (D,), jnp.float32), 0.5, 1.5),
        "query_proj": gaussian(key_of[12], (D, D), D ** -0.5, 0.1875, ((1, 2),)),
        "key_proj": gaussian(key_of[13], (D, KV_HEADS * HEAD_DIM), D ** -0.5, 0.1875, ((1, 2),)),
        "value_proj": gaussian(key_of[14], (D, KV_HEADS * HEAD_DIM), D ** -0.5, 0.1875, ((1, 2),)),
        "attn_proj": gaussian(key_of[15], (D, D), (D // 32) ** -0.5, 1.0, ((1, 2),)),
        "query_gain": jnp.clip(1.0 + 0.1 * jax.random.normal(key_of[16], (HEAD_DIM,), jnp.float32), 0.5, 1.5),
        "key_gain": jnp.clip(1.0 + 0.1 * jax.random.normal(key_of[17], (HEAD_DIM,), jnp.float32), 0.5, 1.5),
        "ffn_gain_b": jnp.clip(1.0 + 0.1 * jax.random.normal(key_of[18], (D,), jnp.float32), 0.5, 1.5),
        "gate_b": gaussian(key_of[19], (D, FF), D ** -0.5, 0.1875, ((1, 2),)),
        "up_b": gaussian(key_of[20], (D, FF), D ** -0.5, 0.1875, ((1, 2),)),
        "down_b": gaussian(key_of[21], (FF, D), FF ** -0.5, 0.09375, ((1, 2),)),
    }


EPS = 1e-05
ROPE_BASE = 1000000.0
MASKED = -1e+30

@jax.custom_vjp
def low(v):
    return lax.optimization_barrier(v.astype(jnp.bfloat16)).astype(jnp.float32)

@jax.custom_vjp
def low_back(v):
    return v

def low_keep(v):
    return (low(v), None)

def low_pass(kept, grad):
    return (grad,)

def back_keep(v):
    return (v, None)

def back_low(kept, grad):
    return (low(grad),)
low.defvjp(low_keep, low_pass)
low_back.defvjp(back_keep, back_low)

def product(left, right):
    return jnp.dot(left, right, precision=lax.Precision.HIGHEST, preferred_element_type=jnp.float32)

def norm_rows(values, gain_vec):
    return values * lax.rsqrt(lax.optimization_barrier(jnp.mean(values * values, axis=-1, keepdims=True)) + EPS) * gain_vec

def rope_tables(positions):
    frequency = ROPE_BASE ** (-(jnp.arange(0, HEAD_DIM, 2, dtype=jnp.float32) / HEAD_DIM))
    angles = positions.astype(jnp.float32)[:, None] * frequency[None, :]
    angles = jnp.concatenate([angles, angles], axis=-1)
    return (jnp.cos(angles)[:, None, :], jnp.sin(angles)[:, None, :])

def rotate(values, cosine_part, sine_part):
    half_width = values.shape[-1] // 2
    turned = jnp.concatenate([-values[..., half_width:], values[..., :half_width]], axis=-1)
    return values * cosine_part + turned * sine_part

def convolve(gated, taps_now, starts, positions):
    padded = jnp.concatenate([jnp.zeros((CONV_K - 1, gated.shape[1]), gated.dtype), gated], axis=0)
    running = jnp.zeros_like(gated)
    for tap_index in range(CONV_K):
        offset = CONV_K - 1 - tap_index
        shifted = padded[tap_index:tap_index + gated.shape[0]]
        allowed = (positions - offset >= starts)[:, None]
        running = running + jnp.where(allowed, shifted, 0.0) * taps_now[tap_index]
    return running

def feed_forward(residual, gain_vec, gate_weight, up_weight, down_weight):
    hidden = low(norm_rows(residual, gain_vec))
    gate_val = low_back(product(hidden, gate_weight))
    up_val = low_back(product(hidden, up_weight))
    activated = low(jax.nn.silu(gate_val) * up_val)
    return residual + low_back(product(activated, down_weight))

def attend(queries, keys_now, values_now, starts, positions):
    length = queries.shape[0]
    block_rows = min(512, length)
    block_count = length // block_rows
    grouped = queries.reshape(block_count, block_rows, KV_HEADS, HEADS // KV_HEADS, HEAD_DIM)

    def one_block(inputs):
        query_block, start_block, place_block = inputs
        scores = jnp.einsum('qkgd,lkd->kgql', query_block, keys_now, precision=lax.Precision.HIGHEST) * HEAD_DIM ** (-0.5)
        scores = low_back(scores)
        allowed = (positions[None, :] >= start_block[:, None]) & (positions[None, :] <= place_block[:, None])
        scores = jnp.where(allowed, scores, MASKED)
        shares = low(jnp.exp(scores - jax.nn.logsumexp(scores, axis=-1, keepdims=True)))
        mixed = jnp.einsum('kgql,lkd->qkgd', shares, values_now, precision=lax.Precision.HIGHEST)
        return mixed.reshape(block_rows, HEADS * HEAD_DIM)
    blocks_out = lax.map(jax.checkpoint(one_block), (grouped, starts.reshape(block_count, block_rows), positions.reshape(block_count, block_rows)))
    return blocks_out.reshape(length, HEADS * HEAD_DIM)

def layers(weights, sequence, starts):
    mix_gain, in_proj, conv_taps, mix_proj, ffn_gain_a, gate_a, up_a, down_a, attn_gain, query_proj, key_proj, value_proj, attn_proj, query_gain, key_gain, ffn_gain_b, gate_b, up_b, down_b = weights
    length = sequence.shape[0]
    positions = jnp.arange(length, dtype=jnp.int32)
    hidden = low(norm_rows(sequence, mix_gain))
    projected = low_back(product(hidden, in_proj))
    b_part = projected[:, :D]
    c_part = projected[:, D:2 * D]
    x_part = projected[:, 2 * D:]
    mixed = convolve(b_part * x_part, conv_taps, starts, positions)
    residual = sequence + low_back(product(low(c_part * mixed), mix_proj))
    residual = feed_forward(residual, ffn_gain_a, gate_a, up_a, down_a)
    hidden = low(norm_rows(residual, attn_gain))
    queries = low_back(product(hidden, query_proj)).reshape(length, HEADS, HEAD_DIM)
    keys_now = low_back(product(hidden, key_proj)).reshape(length, KV_HEADS, HEAD_DIM)
    values_now = low(low_back(product(hidden, value_proj))).reshape(length, KV_HEADS, HEAD_DIM)
    cosine_part, sine_part = rope_tables(positions)
    queries = low(rotate(norm_rows(queries, query_gain), cosine_part, sine_part))
    keys_now = low(rotate(norm_rows(keys_now, key_gain), cosine_part, sine_part))
    attended = low(low_back(attend(queries, keys_now, values_now, starts, positions)))
    residual = residual + low_back(product(attended, attn_proj))
    return feed_forward(residual, ffn_gain_b, gate_b, up_b, down_b)

def reference(tokens, doc_start, cotangent, mix_gain, in_proj, conv_taps, mix_proj, ffn_gain_a, gate_a, up_a, down_a, attn_gain, query_proj, key_proj, value_proj, attn_proj, query_gain, key_gain, ffn_gain_b, gate_b, up_b, down_b):
    weights = tuple((weight_item.astype(jnp.float32) for weight_item in (mix_gain, in_proj, conv_taps, mix_proj, ffn_gain_a, gate_a, up_a, down_a, attn_gain, query_proj, key_proj, value_proj, attn_proj, query_gain, key_gain, ffn_gain_b, gate_b, up_b, down_b)))

    def per_sequence(totals, inputs):
        sequence, starts, incoming = inputs
        result, pullback = jax.vjp(lambda seq_tokens, weight_set: layers(weight_set, seq_tokens, starts), sequence, weights)
        grad_tokens, grad_weights = pullback(incoming)
        return (jax.tree.map(jnp.add, totals, grad_weights), (result, grad_tokens))
    zero_set = jax.tree.map(jnp.zeros_like, weights)
    totals, (output, tokens_grad) = lax.scan(per_sequence, zero_set, (tokens, doc_start, cotangent))
    return (output, tokens_grad, totals[0], totals[1], totals[2], totals[3], totals[4], totals[5], totals[6], totals[7], totals[8], totals[9], totals[10], totals[11], totals[12], totals[13], totals[14], totals[15], totals[16], totals[17], totals[18])
```

```python
from functools import partial
import math

import jax
import jax.numpy as jnp
from jax import lax
from jax.experimental import pallas as pl
from jax.experimental.pallas import tpu as pltpu
from jax.sharding import Mesh, PartitionSpec as P

EPS = 1e-05
ROPE_BASE = 1000000.0
MASKED = -1e30
START_PEAK = -1e25
SEQ = ("z", "y", "x")
EVERY = ("z", "y", "x", "wsh")
SWAP = [(0, 1), (1, 0)]
BF16 = jnp.bfloat16
F32 = jnp.float32
LANES = 128


def norm_rows(values, gain_vec):
    return values * lax.rsqrt(jnp.mean(values * values, axis=-1, keepdims=True) + EPS) * gain_vec


def product(left, right):
    return jnp.dot(left, right, preferred_element_type=F32)


def product_tn(left, right):
    return lax.dot_general(left, right, (((0,), (0,)), ((), ())), preferred_element_type=F32)


def product_nt(left, right):
    return lax.dot_general(left, right, (((1,), (1,)), ((), ())), preferred_element_type=F32)


def gated_unit(gate_val, up_val):
    return jax.nn.silu(gate_val) * up_val


def swap_cores(block):
    return lax.ppermute(block, "wsh", SWAP)


def gather_cores(block, axis=0):
    return lax.all_gather(block, "wsh", axis=axis, tiled=True)


def half_of(array, which, axis=0):
    size = array.shape[axis] // 2
    return lax.dynamic_slice_in_dim(array, which * size, size, axis)


def ordered(core, own, other):
    first = jnp.where(core == 0, own, other)
    second = jnp.where(core == 0, other, own)
    return jnp.concatenate([first, second], axis=-1)


def lane_of(shape):
    return lax.broadcasted_iota(jnp.int32, shape, 1)


def two_heads(block):
    return jnp.concatenate([block[:, :64], block[:, 64:]], axis=0)


def side_by_side(block):
    rows = block.shape[0] // 2
    return jnp.concatenate([block[:rows], block[rows:]], axis=1)


def places(meta_ref, starts_ref, rows):
    block = pl.program_id(0)
    starts = starts_ref[...]
    starts = jnp.concatenate([starts, starts], axis=0)
    row = lax.broadcasted_iota(jnp.int32, (2 * rows, 1), 0)
    row = jnp.where(row >= rows, row - rows, row)
    mine = meta_ref[pl.num_programs(0)] + block * rows + row
    return starts, mine


def sweep_bounds(meta_ref, rows, span):
    block = pl.program_id(0)
    first = meta_ref[block] // span
    last = (meta_ref[pl.num_programs(0)] + (block + 1) * rows + span - 1) // span
    return first, last


def attend_kernel(meta_ref, query_ref, kv_ref, starts_ref, low_ref, full_ref, log_ref, *, span, scale):
    rows = query_ref.shape[0]
    query = two_heads(query_ref[...])
    starts, mine = places(meta_ref, starts_ref, rows)

    def advance(index, carried):
        peak, total, mixed = carried
        kv_block = kv_ref[pl.ds(pl.multiple_of(index * span, span), span), :]
        scores = product_nt(query, kv_block[:, :64]) * scale
        place = index * span + lane_of((1, span))
        scores = jnp.where((place >= starts) & (place <= mine), scores, MASKED)
        fresh_peak = jnp.maximum(peak, jnp.max(scores, axis=1, keepdims=True))
        shares = jnp.exp(scores - fresh_peak)
        keep = jnp.exp(peak - fresh_peak)
        total = total * keep + jnp.sum(shares, axis=1, keepdims=True)
        mixed = mixed * keep + product(shares.astype(BF16), kv_block[:, 64:])
        return fresh_peak, total, mixed

    first, last = sweep_bounds(meta_ref, rows, span)
    peak, total, mixed = lax.fori_loop(
        first,
        last,
        advance,
        (
            jnp.full((2 * rows, 1), START_PEAK, F32),
            jnp.zeros((2 * rows, 1), F32),
            jnp.zeros((2 * rows, 64), F32),
        ),
    )
    attended = side_by_side(mixed / total)
    low_ref[...] = attended.astype(BF16)
    full_ref[...] = attended
    log_ref[...] = side_by_side(jnp.broadcast_to(peak + jnp.log(total), (2 * rows, 64)))


def attend_back_kernel(
    meta_ref, query_ref, kv_ref, starts_ref, grad_ref, full_ref, log_ref, dq_ref, dkv_ref, sums_ref, *, span, scale
):
    rows = query_ref.shape[0]
    query = two_heads(query_ref[...])
    grad = two_heads(grad_ref[...])
    attended = two_heads(full_ref[...])
    logs = two_heads(log_ref[...])[:, :1]
    delta = jnp.sum(grad.astype(F32) * attended, axis=1, keepdims=True)
    starts, mine = places(meta_ref, starts_ref, rows)

    @pl.when(pl.program_id(0) == 0)
    def _():
        sums_ref[...] = jnp.zeros_like(sums_ref)

    def advance(index, query_grad):
        window = pl.ds(pl.multiple_of(index * span, span), span)
        kv_block = kv_ref[window, :]
        key, value = kv_block[:, :64], kv_block[:, 64:]
        scores = product_nt(query, key) * scale
        place = index * span + lane_of((1, span))
        scores = jnp.where((place >= starts) & (place <= mine), scores, MASKED)
        shares = jnp.exp(scores - logs)
        grad_scores = (shares * (product_nt(grad, value) - delta)).astype(BF16)
        key_grad = product_tn(grad_scores, query) * scale
        value_grad = product_tn(shares.astype(BF16), grad)
        sums_ref[window, :] += jnp.concatenate([key_grad, value_grad], axis=1)
        return query_grad + product(grad_scores, key)

    first, last = sweep_bounds(meta_ref, rows, span)
    query_grad = lax.fori_loop(first, last, advance, jnp.zeros((2 * rows, 64), F32))
    dq_ref[...] = side_by_side(query_grad * scale).astype(BF16)

    @pl.when(pl.program_id(0) == pl.num_programs(0) - 1)
    def _():
        dkv_ref[...] = sums_ref[...].astype(BF16)


def attend_blocks(length):
    return math.gcd(256, length)


def rows_spec(rows, columns, column_block=0):
    return pl.BlockSpec((rows, columns), lambda index: (index, column_block))


def whole_spec(rows, columns, column_block=0):
    return pl.BlockSpec((rows, columns), lambda index: (0, column_block))


SCALARS = pl.BlockSpec(memory_space=pltpu.SMEM)


def attend(meta, packed, kv, kv_block, starts, scale):
    length, keys = packed.shape[0], kv.shape[0]
    rows = attend_blocks(length)
    return pl.pallas_call(
        partial(attend_kernel, span=attend_blocks(keys), scale=scale),
        grid=(length // rows,),
        in_specs=[SCALARS, rows_spec(rows, LANES), whole_spec(keys, LANES, kv_block), rows_spec(rows, 1)],
        out_specs=[rows_spec(rows, LANES)] * 3,
        out_shape=[
            jax.ShapeDtypeStruct((length, LANES), BF16),
            jax.ShapeDtypeStruct((length, LANES), F32),
            jax.ShapeDtypeStruct((length, LANES), F32),
        ],
        compiler_params=pltpu.CompilerParams(vmem_limit_bytes=32 << 20),
        cost_estimate=pl.CostEstimate(flops=4 * length * keys * 64, bytes_accessed=2 << 20, transcendentals=length * keys),
    )(meta, packed, kv, starts)


def attend_back(meta, packed, kv, kv_block, starts, grad, full, logs, scale):
    length, keys = packed.shape[0], kv.shape[0]
    rows = attend_blocks(length)
    return pl.pallas_call(
        partial(attend_back_kernel, span=attend_blocks(keys), scale=scale),
        grid=(length // rows,),
        in_specs=[SCALARS, rows_spec(rows, LANES), whole_spec(keys, LANES, kv_block), rows_spec(rows, 1)]
        + [rows_spec(rows, LANES)] * 3,
        out_specs=[rows_spec(rows, LANES), whole_spec(keys, LANES)],
        out_shape=[jax.ShapeDtypeStruct((length, LANES), BF16), jax.ShapeDtypeStruct((keys, LANES), BF16)],
        scratch_shapes=[pltpu.VMEM((keys, LANES), F32)],
        compiler_params=pltpu.CompilerParams(vmem_limit_bytes=32 << 20),
        cost_estimate=pl.CostEstimate(flops=10 * length * keys * 64, bytes_accessed=3 << 20, transcendentals=length * keys),
    )(meta, packed, kv, starts, grad, full, logs)


def head_means(values):
    low_lanes = lane_of(values.shape) < 64
    low_mean = jnp.sum(jnp.where(low_lanes, values, 0.0), axis=1, keepdims=True) * (1.0 / 64)
    high_mean = jnp.sum(jnp.where(low_lanes, 0.0, values), axis=1, keepdims=True) * (1.0 / 64)
    return jnp.where(low_lanes, low_mean, high_mean)


def turn(values, sign):
    lower = (lane_of(values.shape) % 64) < 32
    return jnp.where(lower, -sign * pltpu.roll(values, LANES - 32, 1), sign * pltpu.roll(values, 32, 1))


def head_forward(raw, gain, cosine, sine):
    unit = raw * lax.rsqrt(head_means(raw * raw) + EPS) * gain
    return (unit * cosine + turn(unit, 1.0) * sine).astype(BF16)


def head_backward(raw, gain, cosine, sine, grad):
    back = grad * cosine + turn(grad * sine, -1.0)
    scale = lax.rsqrt(head_means(raw * raw) + EPS)
    gain_term = jnp.sum(back * raw * scale, axis=0, keepdims=True)
    back = back * gain
    raw_grad = back * scale - raw * (scale * scale * scale) * head_means(back * raw)
    return raw_grad.astype(BF16), gain_term


def heads_kernel(query_ref, key_ref, value_ref, cos_ref, sin_ref, query_gain_ref, key_gain_ref, out_ref):
    rows = out_ref.shape[1]
    groups = key_ref.shape[1] // 64
    sequences = query_ref.shape[0] // rows
    cosine, sine = cos_ref[...], sin_ref[...]
    for place in range(sequences):
        span = pl.ds(place * rows, rows)
        for pair in range(groups // 2):
            lanes = pl.ds(pair * LANES, LANES)
            key = head_forward(key_ref[span, lanes], key_gain_ref[...], cosine, sine)
            value = value_ref[span, lanes].astype(BF16)
            for side in range(2):
                group = 2 * pair + side
                query = head_forward(
                    query_ref[span, pl.ds(group * LANES, LANES)], query_gain_ref[...], cosine, sine
                )
                half = slice(64 * side, 64 * side + 64)
                out_ref[place * groups + group, :, 0:LANES] = query
                out_ref[place * groups + group, :, LANES : 2 * LANES] = jnp.concatenate(
                    [key[:, half], value[:, half]], axis=1
                )


def heads_back_kernel(
    grad_ref,
    query_ref,
    key_ref,
    cos_ref,
    sin_ref,
    query_gain_ref,
    key_gain_ref,
    dq_ref,
    dk_ref,
    dv_ref,
    query_term_ref,
    key_term_ref,
):
    rows = grad_ref.shape[1]
    groups = key_ref.shape[1] // 64
    sequences = query_ref.shape[0] // rows
    cosine, sine = cos_ref[...], sin_ref[...]
    query_term = jnp.zeros((1, LANES), F32)
    key_term = jnp.zeros((1, LANES), F32)
    for place in range(sequences):
        span = pl.ds(place * rows, rows)
        for pair in range(groups // 2):
            lanes = pl.ds(pair * LANES, LANES)
            sides = [grad_ref[place * groups + 2 * pair + side, :, LANES : 2 * LANES] for side in range(2)]
            key_grad = jnp.concatenate([sides[0][:, :64], sides[1][:, :64]], axis=1).astype(F32)
            dv_ref[span, lanes] = jnp.concatenate([sides[0][:, 64:], sides[1][:, 64:]], axis=1)
            low, term = head_backward(key_ref[span, lanes], key_gain_ref[...], cosine, sine, key_grad)
            dk_ref[span, lanes] = low
            key_term = key_term + term
            for side in range(2):
                group = 2 * pair + side
                wide = pl.ds(group * LANES, LANES)
                query_grad = grad_ref[place * groups + group, :, 0:LANES].astype(F32)
                low, term = head_backward(query_ref[span, wide], query_gain_ref[...], cosine, sine, query_grad)
                dq_ref[span, wide] = low
                query_term = query_term + term
    query_term_ref[...] = query_term
    key_term_ref[...] = key_term


def heads_forward(query, key, value, tables, query_gain, key_gain, rows):
    groups = key.shape[1] // 64
    blocks = query.shape[0] // rows * groups
    return pl.pallas_call(
        heads_kernel,
        out_shape=jax.ShapeDtypeStruct((blocks, rows, 2 * LANES), BF16),
        compiler_params=pltpu.CompilerParams(vmem_limit_bytes=32 << 20),
    )(query, key, value, *tables, query_gain, key_gain)


def heads_backward(grad, query, key, tables, query_gain, key_gain):
    return pl.pallas_call(
        heads_back_kernel,
        out_shape=[
            jax.ShapeDtypeStruct(query.shape, BF16),
            jax.ShapeDtypeStruct(key.shape, BF16),
            jax.ShapeDtypeStruct(key.shape, BF16),
            jax.ShapeDtypeStruct((1, LANES), F32),
            jax.ShapeDtypeStruct((1, LANES), F32),
        ],
        compiler_params=pltpu.CompilerParams(vmem_limit_bytes=32 << 20),
    )(grad, query, key, *tables, query_gain, key_gain)


class Reducer:
    def __init__(self):
        self.sizes = {name: lax.axis_size(name) for name in SEQ}
        self.paired = self.sizes["x"] == 2 and self.sizes["y"] == 2

    def exchange(self, block, axis):
        return lax.ppermute(block, axis, SWAP)

    def pick(self, columns, axis, which):
        owners = [self.sizes[name] for name in SEQ]
        shaped = columns.reshape(*owners, -1, columns.shape[-1])
        picked = lax.dynamic_index_in_dim(shaped, which, SEQ.index(axis), keepdims=False)
        return picked.reshape(-1, columns.shape[-1])

    def share_left(self, left, axis):
        turned = left.T
        if not self.paired:
            return turned
        place = lax.axis_index(axis)
        own = self.pick(turned, axis, place)
        return own, self.exchange(self.pick(turned, axis, 1 - place), axis)

    def share_right(self, right, axis):
        return (right, self.exchange(right, axis)) if self.paired else right

    def total(self, left, right, axis):
        if not self.paired:
            whole = product(left, right).astype(BF16)
            return lax.psum_scatter(whole, SEQ, scatter_dimension=0, tiled=True).astype(F32)
        other = "y" if axis == "x" else "x"
        place = lax.axis_index(other)

        def part(which):
            sums = 0.0
            for columns, values in zip(left, right):
                shaped = columns.reshape(self.sizes["z"], 2, -1, columns.shape[-1])
                picked = lax.dynamic_index_in_dim(shaped, which, 1, keepdims=False)
                sums = sums + product(picked.reshape(-1, columns.shape[-1]), values)
            return sums

        arrived = self.exchange(part(1 - place).astype(BF16), other)
        summed = (part(place) + arrived.astype(F32)).astype(BF16)
        return lax.psum_scatter(summed, "z", scatter_dimension=0, tiled=True).astype(F32)


def shards(
    tokens,
    doc_start,
    cotangent,
    mix_gain,
    in_proj,
    conv_taps,
    mix_proj,
    ffn_gain_a,
    gate_a,
    up_a,
    down_a,
    attn_gain,
    query_proj,
    key_proj,
    value_proj,
    attn_proj,
    query_gain,
    key_gain,
    ffn_gain_b,
    gate_b,
    up_b,
    down_b,
):
    streams, seq_rows, width = tokens.shape
    core = lax.axis_index("wsh")
    sequences = streams * lax.axis_size("wsh")
    token_count = streams * seq_rows
    head_width = query_gain.shape[0]
    groups = key_proj.shape[1] // head_width
    score_scale = head_width ** (-0.5)
    margin = conv_taps.shape[0] - 1
    half_width = width // 2
    chips = lax.axis_size(SEQ)
    chip = lax.axis_index(SEQ)
    positions = chip * seq_rows + jnp.arange(seq_rows, dtype=jnp.int32)
    reducer = Reducer()

    frequency = ROPE_BASE ** (-(jnp.arange(0, head_width, 2, dtype=F32) / head_width))
    angles = positions.astype(F32)[:, None] * jnp.tile(frequency, 4)[None, :]
    tables = (jnp.cos(angles), jnp.sin(angles))
    query_gain_row = jnp.tile(query_gain, 2)[None, :]
    key_gain_row = jnp.tile(key_gain, 2)[None, :]

    def split_rows(weight):
        return half_of(weight, core), swap_cores(half_of(weight, 1 - core))

    def out_product(left, pieces):
        return ordered(core, product(left, pieces[0]), product(left, pieces[1]))

    def out_product_back(grad, pieces):
        own = half_of(grad, core, 1)
        other = half_of(grad, 1 - core, 1)
        return product_nt(own, pieces[0]) + product_nt(other, pieces[1])

    def sum_cores(partial_rows):
        return half_of(partial_rows, core) + swap_cores(half_of(partial_rows, 1 - core))

    starts_here = gather_cores(doc_start)
    in_low, in_mid, in_high = (in_proj[:, index * half_width : (index + 1) * half_width] for index in range(3))
    in_mid = swap_cores(in_mid)
    mix_pieces = split_rows(mix_proj)
    down_a_pieces = split_rows(down_a)
    attn_pieces = split_rows(attn_proj)
    down_b_pieces = split_rows(down_b)

    flat_tokens = tokens.reshape(token_count, width)
    low_one = gather_cores(norm_rows(flat_tokens, mix_gain).astype(BF16))
    part_low = product(low_one, in_low)
    part_mid = product(low_one, in_mid)
    part_high = product(low_one, in_high)
    factor = jnp.where(core == 0, part_low, part_high)
    c_part = jnp.where(core == 0, part_high, part_low)
    gated = (part_mid * factor).reshape(sequences, seq_rows, half_width)
    edge_rows = lax.ppermute(gated[:, seq_rows - margin :, :], SEQ, [(i, i + 1) for i in range(chips - 1)])
    extended = jnp.concatenate([edge_rows, gated], axis=1)
    taps_here = half_of(conv_taps, core, 1)

    def convolve(extended_rows, taps_now):
        running = jnp.zeros_like(extended_rows[:, margin:])
        for tap_index in range(margin + 1):
            offset = margin - tap_index
            shifted = extended_rows[:, tap_index : tap_index + seq_rows]
            allowed = (positions[None, :] - offset >= starts_here)[:, :, None]
            running = running + jnp.where(allowed, shifted, 0.0) * taps_now[tap_index]
        return running

    mixed_conv = convolve(extended, taps_here).reshape(-1, half_width)
    mixer_low = (c_part * mixed_conv).astype(BF16)
    resid_one = flat_tokens + sum_cores(out_product(mixer_low, mix_pieces))

    def ffn_forward(residual, gain_vec, gate_weight, up_weight, down_pieces):
        hidden_low = gather_cores(norm_rows(residual, gain_vec).astype(BF16))
        gate_val = product(hidden_low, gate_weight)
        up_val = product(hidden_low, up_weight)
        act_low = gated_unit(gate_val, up_val).astype(BF16)
        result = residual + sum_cores(out_product(act_low, down_pieces))
        return result, (hidden_low, gate_val, up_val, act_low)

    resid_two, saved_a = ffn_forward(resid_one, ffn_gain_a, gate_a, up_a, down_a_pieces)

    low_three = gather_cores(norm_rows(resid_two, attn_gain).astype(BF16))
    query_raw = product(low_three, query_proj)
    key_raw = product(low_three, key_proj)
    value_raw = product(low_three, value_proj)
    packed = heads_forward(query_raw, key_raw, value_raw, tables, query_gain_row, key_gain_row, seq_rows)

    team = SEQ if chips == sequences * groups else ("y", "x")
    rest = () if team == SEQ else ("z",)
    to_heads = partial(lax.all_to_all, axis_name=team, split_axis=0, concat_axis=0, tiled=True)
    packed = to_heads(packed).reshape(-1, 2 * LANES)
    length = packed.shape[0]
    team_starts = lax.all_gather(starts_here, team, axis=1, tiled=True)
    own_starts = lax.dynamic_index_in_dim(team_starts, lax.axis_index(team) // groups, 0, keepdims=False)
    first_place = lax.axis_index(rest) * length if rest else 0
    meta = jnp.append(own_starts[:: attend_blocks(length)], first_place).astype(jnp.int32)
    own_starts = own_starts[:, None]
    if rest:
        kv, kv_block = lax.all_gather(packed[:, LANES:], rest, axis=0, tiled=True), 0
    else:
        kv, kv_block = packed, 1
    attended_low, attended_full, logs = attend(meta, packed, kv, kv_block, own_starts, score_scale)

    def from_heads(block):
        back = to_heads(block.reshape(sequences * groups, seq_rows, -1))
        back = back.reshape(sequences, groups, seq_rows, -1)
        return jnp.transpose(back, (0, 2, 1, 3)).reshape(sequences * seq_rows, -1)

    attn_low = from_heads(attended_low)
    resid_three = resid_two + sum_cores(out_product(attn_low, attn_pieces))
    output, saved_b = ffn_forward(resid_three, ffn_gain_b, gate_b, up_b, down_b_pieces)

    def ffn_backward(residual, gain_vec, saved, gate_weight, up_weight, down_pieces, grad_after, axis):
        hidden_low, gate_val, up_val, act_low = saved
        other = "y" if axis == "x" else "x"
        grad_low = gather_cores(grad_after.astype(BF16))
        grad_act = out_product_back(grad_low, down_pieces)
        _, pull_unit = jax.vjp(gated_unit, gate_val, up_val)
        grad_gate_val, grad_up_val = pull_unit(grad_act)
        gate_low = grad_gate_val.astype(BF16)
        up_low = grad_up_val.astype(BF16)
        grad_hidden = sum_cores(product_nt(gate_low, gate_weight) + product_nt(up_low, up_weight))
        _, pull_norm = jax.vjp(norm_rows, residual, gain_vec)
        grad_resid, grad_gain = pull_norm(grad_hidden)
        left = reducer.share_left(hidden_low, axis)
        grad_gate = reducer.total(left, reducer.share_right(gate_low, axis), axis)
        grad_up = reducer.total(left, reducer.share_right(up_low, axis), axis)
        down_left = reducer.share_left(grad_low, other)
        grad_down = reducer.total(down_left, reducer.share_right(act_low, other), other)
        return grad_after + grad_resid, grad_gate, grad_up, grad_down.T, grad_gain

    grad_out = cotangent.reshape(token_count, width)
    grad_three, grad_gate_b, grad_up_b, grad_down_b, grad_gain_b = ffn_backward(
        resid_three, ffn_gain_b, saved_b, gate_b, up_b, down_b_pieces, grad_out, "x"
    )
    grad_attn_low = gather_cores(grad_three.astype(BF16))
    grad_heads_low = out_product_back(grad_attn_low, attn_pieces).astype(BF16)
    grad_heads = jnp.transpose(
        grad_heads_low.reshape(sequences, seq_rows, groups, LANES), (0, 2, 1, 3)
    ).reshape(sequences * groups, seq_rows, LANES)
    grad_heads = to_heads(grad_heads).reshape(length, LANES)
    query_grads, kv_grads = attend_back(
        meta, packed, kv, kv_block, own_starts, grad_heads, attended_full, logs, score_scale
    )
    if rest:
        kv_grads = lax.psum_scatter(kv_grads, rest, scatter_dimension=0, tiled=True)
    packed_grads = jnp.concatenate([query_grads, kv_grads], axis=1)
    packed_grads = to_heads(packed_grads.reshape(sequences * groups, seq_rows, 2 * LANES))
    query_back, key_back, value_back, query_term, key_term = heads_backward(
        packed_grads, query_raw, key_raw, tables, query_gain_row, key_gain_row
    )
    grad_hidden_three = sum_cores(
        product_nt(query_back, query_proj) + product_nt(key_back, key_proj) + product_nt(value_back, value_proj)
    )
    _, pull_three = jax.vjp(norm_rows, resid_two, attn_gain)
    grad_resid_three, grad_attn_gain = pull_three(grad_hidden_three)
    grad_two = grad_three + grad_resid_three

    attn_left = reducer.share_left(gather_cores(attn_low, 1), "y")
    grad_attn = reducer.total(attn_left, reducer.share_right(half_of(grad_attn_low, core, 1), "y"), "y")
    qkv_back = jnp.concatenate([query_back, key_back, value_back], axis=1)
    qkv_left = reducer.share_left(low_three, "y")
    grad_qkv = reducer.total(qkv_left, reducer.share_right(qkv_back, "y"), "y")

    grad_one, grad_gate_a, grad_up_a, grad_down_a, grad_gain_a = ffn_backward(
        resid_one, ffn_gain_a, saved_a, gate_a, up_a, down_a_pieces, grad_two, "y"
    )
    grad_mix_low = gather_cores(grad_one.astype(BF16))
    grad_mixer = out_product_back(grad_mix_low, mix_pieces)
    grad_c_part = grad_mixer * mixed_conv
    grad_conv = (grad_mixer * c_part).reshape(sequences, seq_rows, half_width)
    _, pull_conv = jax.vjp(convolve, extended, taps_here)
    grad_extended, grad_taps = pull_conv(grad_conv)
    returned = lax.ppermute(grad_extended[:, :margin, :], SEQ, [(i + 1, i) for i in range(chips - 1)])
    grad_gated = grad_extended[:, margin:, :] + jnp.concatenate(
        [jnp.zeros((sequences, seq_rows - margin, half_width), F32), returned], axis=1
    )
    grad_gated = grad_gated.reshape(-1, half_width)
    grad_factor = grad_gated * part_mid
    mid_low = (grad_gated * factor).astype(BF16)
    low_low = jnp.where(core == 0, grad_factor, grad_c_part).astype(BF16)
    high_low = jnp.where(core == 0, grad_c_part, grad_factor).astype(BF16)
    grad_hidden_one = sum_cores(
        product_nt(low_low, in_low) + product_nt(mid_low, in_mid) + product_nt(high_low, in_high)
    )
    _, pull_one = jax.vjp(norm_rows, flat_tokens, mix_gain)
    grad_tokens_norm, grad_mix_gain = pull_one(grad_hidden_one)
    tokens_grad = (grad_one + grad_tokens_norm).reshape(streams, seq_rows, width)

    mix_left = reducer.share_left(gather_cores(mixer_low, 1), "x")
    grad_mix = reducer.total(mix_left, reducer.share_right(half_of(grad_mix_low, core, 1), "x"), "x")
    proj_back = jnp.concatenate([low_low, swap_cores(mid_low), high_low], axis=1)
    in_left = reducer.share_left(low_one, "x")
    grad_in = reducer.total(in_left, reducer.share_right(proj_back, "x"), "x")

    grad_taps = lax.dynamic_update_slice_in_dim(jnp.zeros_like(conv_taps), grad_taps, core * half_width, 1)
    small = jnp.concatenate(
        [
            grad_mix_gain,
            grad_taps.reshape(-1),
            grad_gain_a,
            grad_attn_gain,
            grad_gain_b,
            query_term[0],
            key_term[0],
        ]
    )
    small = lax.psum(small, EVERY)
    taps_end = width + conv_taps.size
    heads_at = taps_end + 3 * width

    def head_gain(offset):
        both = small[offset : offset + LANES]
        return both[:head_width] + both[head_width:]

    query_columns, key_columns = query_proj.shape[1], key_proj.shape[1]
    return (
        output.reshape(streams, seq_rows, width),
        tokens_grad,
        small[:width],
        grad_in,
        small[width:taps_end].reshape(conv_taps.shape),
        grad_mix,
        small[taps_end : taps_end + width],
        grad_gate_a,
        grad_up_a,
        grad_down_a,
        small[taps_end + width : taps_end + 2 * width],
        grad_qkv[:, :query_columns],
        grad_qkv[:, query_columns : query_columns + key_columns],
        grad_qkv[:, query_columns + key_columns :],
        grad_attn,
        head_gain(heads_at),
        head_gain(heads_at + LANES),
        small[taps_end + 2 * width : taps_end + 3 * width],
        grad_gate_b,
        grad_up_b,
        grad_down_b,
    )


def chip_grid(chips):
    along_z = math.gcd(4, chips)
    side = math.isqrt(chips // along_z)
    return along_z, chips // along_z // side, side


def solution(mesh):
    cores = mesh.shape["wsh"]
    grid = Mesh(mesh.devices.reshape(*chip_grid(mesh.shape["seq"]), cores), EVERY)
    tokens_spec = P("wsh", SEQ, None)
    columns = P(None, "wsh")
    grads = P(SEQ, "wsh")
    in_specs = (
        tokens_spec,
        P("wsh", SEQ),
        tokens_spec,
        P(),
        columns,
        P(),
        columns,
        P(),
        columns,
        columns,
        columns,
        P(),
        columns,
        columns,
        columns,
        columns,
        P(),
        P(),
        P(),
        columns,
        columns,
        columns,
    )
    out_specs = (
        tokens_spec,
        tokens_spec,
        P(),
        grads,
        P(),
        grads,
        P(),
        grads,
        grads,
        P("wsh", SEQ),
        P(),
        grads,
        grads,
        grads,
        grads,
        P(),
        P(),
        P(),
        grads,
        grads,
        P("wsh", SEQ),
    )
    return jax.shard_map(shards, mesh=grid, in_specs=in_specs, out_specs=out_specs, check_vma=False)
```

```python
from functools import partial
import math

import jax
import jax.numpy as jnp
from jax import lax
from jax.experimental import pallas as pl
from jax.experimental.pallas import tpu as pltpu
from jax.sharding import Mesh, PartitionSpec as P

EPS = 1e-05
ROPE_BASE = 1000000.0
MASKED = -1e30
START_PEAK = -1e25
SEQ = ("zh", "zl", "y", "x")
EVERY = SEQ + ("wsh",)
SWAP = [(0, 1), (1, 0)]
BF16 = jnp.bfloat16
F32 = jnp.float32
LANES = 128


def norm_rows(values, gain_vec):
    return values * lax.rsqrt(jnp.mean(values * values, axis=-1, keepdims=True) + EPS) * gain_vec


def product(left, right):
    return jnp.dot(left, right, preferred_element_type=F32)


def product_tn(left, right):
    return lax.dot_general(left, right, (((0,), (0,)), ((), ())), preferred_element_type=F32)


def product_nt(left, right):
    return lax.dot_general(left, right, (((1,), (1,)), ((), ())), preferred_element_type=F32)


def gated_unit(gate_val, up_val):
    return jax.nn.silu(gate_val) * up_val


def swap_cores(block):
    return lax.ppermute(block, "wsh", SWAP)


def gather_cores(block, axis=0):
    return lax.all_gather(block, "wsh", axis=axis, tiled=True)


def half_of(array, which, axis=0):
    size = array.shape[axis] // 2
    return lax.dynamic_slice_in_dim(array, which * size, size, axis)


def ordered(core, own, other):
    first = jnp.where(core == 0, own, other)
    second = jnp.where(core == 0, other, own)
    return jnp.concatenate([first, second], axis=-1)


def lane_of(shape):
    return lax.broadcasted_iota(jnp.int32, shape, 1)


def two_heads(block):
    return jnp.concatenate([block[:, :64], block[:, 64:]], axis=0)


def side_by_side(block):
    rows = block.shape[0] // 2
    return jnp.concatenate([block[:rows], block[rows:]], axis=1)


EXTRA = 16


def flat(block):
    return block[:, : block.shape[1] - EXTRA].reshape(-1, block.shape[2])


def places(packed_ref, offset):
    chips, padded, _ = packed_ref.shape
    rows = padded - EXTRA
    coded = packed_ref[:, rows, :].astype(F32)
    starts = coded[:, :64] * 64.0 + coded[:, 64:]
    diagonal = lax.broadcasted_iota(jnp.int32, (rows, rows), 0) == lane_of((rows, rows))
    columns = [
        jnp.sum(jnp.where(diagonal, starts[chip : chip + 1], 0.0), axis=1, keepdims=True) for chip in range(chips)
    ]
    starts = jnp.concatenate(columns * 2, axis=0).astype(jnp.int32)
    row = lax.broadcasted_iota(jnp.int32, (2 * chips * rows, 1), 0)
    row = jnp.where(row >= chips * rows, row - chips * rows, row)
    return starts, offset + pl.program_id(0) * chips * rows + row


def first_place(rest, length):
    return lax.axis_index(rest) * length if rest else 0


def kv_window(kv_ref, index, chips):
    return flat(kv_ref[pl.ds(index * chips, chips)])


def attend_kernel(packed_ref, kv_ref, low_ref, full_ref, log_ref, *, rest, span, scale):
    rows = low_ref.shape[0]
    offset = first_place(rest, rows * pl.num_programs(0))
    query = two_heads(flat(packed_ref[...]))
    starts, mine = places(packed_ref, offset)

    def advance(index, carried):
        peak, total, mixed = carried
        kv_block = kv_window(kv_ref, index, packed_ref.shape[0])
        scores = product_nt(query, kv_block[:, :64]) * scale
        place = index * span + lane_of((1, span))
        scores = jnp.where((place >= starts) & (place <= mine), scores, MASKED)
        fresh_peak = jnp.maximum(peak, jnp.max(scores, axis=1, keepdims=True))
        shares = jnp.exp(scores - fresh_peak)
        keep = jnp.exp(peak - fresh_peak)
        total = total * keep + jnp.sum(shares, axis=1, keepdims=True)
        mixed = mixed * keep + product(shares.astype(BF16), kv_block[:, 64:])
        return fresh_peak, total, mixed

    last = (offset + (pl.program_id(0) + 1) * rows) // span
    peak, total, mixed = lax.fori_loop(
        0,
        last,
        advance,
        (
            jnp.full((2 * rows, 1), START_PEAK, F32),
            jnp.zeros((2 * rows, 1), F32),
            jnp.zeros((2 * rows, 64), F32),
        ),
    )
    attended = side_by_side(mixed / total)
    low_ref[...] = attended.astype(BF16)
    full_ref[...] = attended
    log_ref[...] = side_by_side(jnp.broadcast_to(peak + jnp.log(total), (2 * rows, 64)))


def attend_back_kernel(packed_ref, kv_ref, grad_ref, full_ref, log_ref, dq_ref, dkv_ref, sums_ref, *, rest, span, scale):
    rows = grad_ref.shape[0]
    offset = first_place(rest, rows * pl.num_programs(0))
    query = two_heads(flat(packed_ref[...]))
    grad = two_heads(grad_ref[...])
    attended = two_heads(full_ref[...])
    logs = two_heads(log_ref[...])[:, :1]
    delta = jnp.sum(grad.astype(F32) * attended, axis=1, keepdims=True)
    starts, mine = places(packed_ref, offset)

    @pl.when(pl.program_id(0) == 0)
    def _():
        sums_ref[...] = jnp.zeros_like(sums_ref)

    def advance(index, query_grad):
        window = pl.ds(pl.multiple_of(index * span, span), span)
        kv_block = kv_window(kv_ref, index, packed_ref.shape[0])
        key, value = kv_block[:, :64], kv_block[:, 64:]
        scores = product_nt(query, key) * scale
        place = index * span + lane_of((1, span))
        scores = jnp.where((place >= starts) & (place <= mine), scores, MASKED)
        shares = jnp.exp(scores - logs)
        grad_scores = (shares * (product_nt(grad, value) - delta)).astype(BF16)
        key_grad = product_tn(grad_scores, query) * scale
        value_grad = product_tn(shares.astype(BF16), grad)
        sums_ref[window, :] += jnp.concatenate([key_grad, value_grad], axis=1)
        return query_grad + product(grad_scores, key)

    last = (offset + (pl.program_id(0) + 1) * rows) // span
    query_grad = lax.fori_loop(0, last, advance, jnp.zeros((2 * rows, 64), F32))
    dq_ref[...] = side_by_side(query_grad * scale).astype(BF16)

    @pl.when(pl.program_id(0) == pl.num_programs(0) - 1)
    def _():
        dkv_ref[...] = sums_ref[...].astype(BF16)


def rows_spec(rows, columns, column_block=0):
    return pl.BlockSpec((rows, columns), lambda index: (index, column_block))


def whole_spec(rows, columns, column_block=0):
    return pl.BlockSpec((rows, columns), lambda index: (0, column_block))


def attend_specs(packed, kv, kv_block):
    chips, padded, _ = packed.shape
    per_step = max(1, 256 // (padded - EXTRA))
    packed_spec = pl.BlockSpec((per_step, padded, LANES), lambda index: (index, 0, 0))
    kv_spec = pl.BlockSpec((kv.shape[0], padded, LANES), lambda index: (0, 0, kv_block))
    return chips // per_step, per_step * (padded - EXTRA), [packed_spec, kv_spec]


def attend(packed, kv, kv_block, rest, scale):
    steps, rows, specs = attend_specs(packed, kv, kv_block)
    length, keys = steps * rows, kv.shape[0] * (kv.shape[1] - EXTRA)
    return pl.pallas_call(
        partial(attend_kernel, rest=rest, span=rows, scale=scale),
        grid=(steps,),
        in_specs=specs,
        out_specs=[rows_spec(rows, LANES)] * 3,
        out_shape=[
            jax.ShapeDtypeStruct((length, LANES), BF16),
            jax.ShapeDtypeStruct((length, LANES), F32),
            jax.ShapeDtypeStruct((length, LANES), F32),
        ],
        compiler_params=pltpu.CompilerParams(vmem_limit_bytes=24 << 20),
        cost_estimate=pl.CostEstimate(flops=4 * length * keys * 64, bytes_accessed=2 << 20, transcendentals=length * keys),
    )(packed, kv)


def attend_back(packed, kv, kv_block, rest, grad, full, logs, scale):
    steps, rows, specs = attend_specs(packed, kv, kv_block)
    length, keys = steps * rows, kv.shape[0] * (kv.shape[1] - EXTRA)
    return pl.pallas_call(
        partial(attend_back_kernel, rest=rest, span=rows, scale=scale),
        grid=(steps,),
        in_specs=specs + [rows_spec(rows, LANES)] * 3,
        out_specs=[rows_spec(rows, LANES), whole_spec(keys, LANES)],
        out_shape=[jax.ShapeDtypeStruct((length, LANES), BF16), jax.ShapeDtypeStruct((keys, LANES), BF16)],
        scratch_shapes=[pltpu.VMEM((keys, LANES), F32)],
        compiler_params=pltpu.CompilerParams(vmem_limit_bytes=24 << 20),
        cost_estimate=pl.CostEstimate(flops=10 * length * keys * 64, bytes_accessed=3 << 20, transcendentals=length * keys),
    )(packed, kv, grad, full, logs)


def heads_grad_kernel(own_ref, other_ref, own_piece_ref, other_piece_ref, out_ref):
    sums = product_nt(own_ref[...], own_piece_ref[...]) + product_nt(other_ref[...], other_piece_ref[...])
    out_ref[...] = sums.astype(BF16).reshape(out_ref.shape)


def heads_grad(own, other, pieces, sequences):
    tokens, columns = own.shape
    groups = pieces[0].shape[0] // LANES
    piece_spec = pl.BlockSpec((LANES, columns), lambda index: (index, 0))
    rows = tokens // sequences
    return pl.pallas_call(
        heads_grad_kernel,
        grid=(groups,),
        in_specs=[whole_spec(tokens, columns)] * 2 + [piece_spec] * 2,
        out_specs=pl.BlockSpec((sequences, rows, LANES), lambda index: (index, 0, 0)),
        out_shape=jax.ShapeDtypeStruct((groups * sequences, rows, LANES), BF16),
        compiler_params=pltpu.CompilerParams(vmem_limit_bytes=16 << 20),
    )(own, other, *pieces)


def head_means(values):
    low_lanes = lane_of(values.shape) < 64
    low_mean = jnp.sum(jnp.where(low_lanes, values, 0.0), axis=1, keepdims=True) * (1.0 / 64)
    high_mean = jnp.sum(jnp.where(low_lanes, 0.0, values), axis=1, keepdims=True) * (1.0 / 64)
    return jnp.where(low_lanes, low_mean, high_mean)


def turn(values, sign):
    lower = (lane_of(values.shape) % 64) < 32
    return jnp.where(lower, -sign * pltpu.roll(values, LANES - 32, 1), sign * pltpu.roll(values, 32, 1))


def head_forward(raw, gain, cosine, sine):
    unit = raw * lax.rsqrt(head_means(raw * raw) + EPS) * gain
    return (unit * cosine + turn(unit, 1.0) * sine).astype(BF16)


def head_backward(raw, gain, cosine, sine, grad):
    back = grad * cosine + turn(grad * sine, -1.0)
    scale = lax.rsqrt(head_means(raw * raw) + EPS)
    gain_term = jnp.sum(back * raw * scale, axis=0, keepdims=True)
    back = back * gain
    raw_grad = back * scale - raw * (scale * scale * scale) * head_means(back * raw)
    return raw_grad.astype(BF16), gain_term


def heads_kernel(query_ref, key_ref, value_ref, starts_ref, cos_ref, sin_ref, query_gain_ref, key_gain_ref, out_ref):
    rows = out_ref.shape[1] - EXTRA
    groups = key_ref.shape[1] // 64
    sequences = query_ref.shape[0] // rows
    cosine, sine = cos_ref[...], sin_ref[...]
    for place in range(sequences):
        span = pl.ds(place * rows, rows)
        starts = jnp.broadcast_to(starts_ref[place : place + 1], (EXTRA, LANES)).astype(BF16)
        for pair in range(groups // 2):
            lanes = pl.ds(pair * LANES, LANES)
            key = head_forward(key_ref[span, lanes], key_gain_ref[...], cosine, sine)
            value = value_ref[span, lanes].astype(BF16)
            for side in range(2):
                group = 2 * pair + side
                query = head_forward(
                    query_ref[span, pl.ds(group * LANES, LANES)], query_gain_ref[...], cosine, sine
                )
                half = slice(64 * side, 64 * side + 64)
                block = group * sequences + place
                out_ref[block, :rows, 0:LANES] = query
                out_ref[block, :rows, LANES : 2 * LANES] = jnp.concatenate([key[:, half], value[:, half]], axis=1)
                out_ref[block, rows:, 0:LANES] = starts
                out_ref[block, rows:, LANES : 2 * LANES] = starts


def heads_back_kernel(
    grad_ref,
    query_ref,
    key_ref,
    cos_ref,
    sin_ref,
    query_gain_ref,
    key_gain_ref,
    dq_ref,
    dk_ref,
    dv_ref,
    query_term_ref,
    key_term_ref,
):
    rows = grad_ref.shape[1]
    groups = key_ref.shape[1] // 64
    sequences = query_ref.shape[0] // rows
    cosine, sine = cos_ref[...], sin_ref[...]
    query_term = jnp.zeros((1, LANES), F32)
    key_term = jnp.zeros((1, LANES), F32)
    for place in range(sequences):
        span = pl.ds(place * rows, rows)
        for pair in range(groups // 2):
            lanes = pl.ds(pair * LANES, LANES)
            sides = [grad_ref[(2 * pair + side) * sequences + place, :, LANES : 2 * LANES] for side in range(2)]
            key_grad = jnp.concatenate([sides[0][:, :64], sides[1][:, :64]], axis=1).astype(F32)
            dv_ref[span, lanes] = jnp.concatenate([sides[0][:, 64:], sides[1][:, 64:]], axis=1)
            low, term = head_backward(key_ref[span, lanes], key_gain_ref[...], cosine, sine, key_grad)
            dk_ref[span, lanes] = low
            key_term = key_term + term
            for side in range(2):
                group = 2 * pair + side
                wide = pl.ds(group * LANES, LANES)
                query_grad = grad_ref[group * sequences + place, :, 0:LANES].astype(F32)
                low, term = head_backward(query_ref[span, wide], query_gain_ref[...], cosine, sine, query_grad)
                dq_ref[span, wide] = low
                query_term = query_term + term
    query_term_ref[...] = query_term
    key_term_ref[...] = key_term


def heads_forward(query, key, value, starts, tables, query_gain, key_gain):
    rows = starts.shape[1]
    blocks = starts.shape[0] * (key.shape[1] // 64)
    coded = jnp.concatenate([starts // 64, starts % 64], axis=1).astype(F32)
    return pl.pallas_call(
        heads_kernel,
        out_shape=jax.ShapeDtypeStruct((blocks, rows + EXTRA, 2 * LANES), BF16),
        compiler_params=pltpu.CompilerParams(vmem_limit_bytes=32 << 20),
    )(query, key, value, coded, *tables, query_gain, key_gain)


def heads_backward(grad, query, key, tables, query_gain, key_gain):
    return pl.pallas_call(
        heads_back_kernel,
        out_shape=[
            jax.ShapeDtypeStruct(query.shape, BF16),
            jax.ShapeDtypeStruct(key.shape, BF16),
            jax.ShapeDtypeStruct(key.shape, BF16),
            jax.ShapeDtypeStruct((1, LANES), F32),
            jax.ShapeDtypeStruct((1, LANES), F32),
        ],
        compiler_params=pltpu.CompilerParams(vmem_limit_bytes=32 << 20),
    )(grad, query, key, *tables, query_gain, key_gain)


def at_place(pieces, place):
    return jnp.where(place == 0, pieces[0], pieces[1])


def quarters(block, dim, core):
    size = block.shape[dim] // 4
    pieces = [lax.slice_in_dim(block, index * size, (index + 1) * size, axis=dim) for index in range(4)]
    return [
        pieces[0],
        jnp.where(core == 0, pieces[2], pieces[1]),
        jnp.where(core == 0, pieces[1], pieces[2]),
        pieces[3],
    ]


def places_here():
    core, x, y = lax.axis_index("wsh"), lax.axis_index("x"), lax.axis_index("y")
    return jnp.where(core == 0, x, y), jnp.where(core == 0, y, x)


def ffn_grad_kernel(meta_ref, *refs):
    hidden, grads = refs[:5], refs[5:10]
    keep_ref, far_ref, last_ref, act_ref, act_far_ref, act_last_ref = refs[10:16]
    outs = refs[16:]
    rows = keep_ref.shape[0]
    core, place = lax.axis_index("wsh"), places_here()[1]

    def tokens_of(left_refs):
        own, near, across, last, last_far = (left_ref[...] for left_ref in left_refs)
        halves = jnp.where(core == 0, last, last_far), jnp.where(core == 0, last_far, last)
        return own, near, across, jnp.concatenate(halves, axis=0)

    def lanes(block):
        pieces = quarters(block, 1, core)
        return jnp.concatenate([at_place(pieces[:2], place), at_place(pieces[2:], place)], axis=1)

    def total(lefts, own_ref, near_ref, pair_ref):
        sums = product_tn(lefts[0], own_ref[...]) + product_tn(lefts[1], near_ref[...])
        return sums + product_tn(lefts[2], pair_ref[:rows]) + product_tn(lefts[3], pair_ref[rows:])

    units = total(tokens_of(hidden), keep_ref, far_ref, last_ref).astype(BF16)
    downs = total([lanes(block) for block in tokens_of(grads)], act_ref, act_far_ref, act_last_ref).astype(BF16)
    unit_rows = units.shape[0]
    step, steps = pl.program_id(0), pl.num_programs(0)

    for place, out_ref in enumerate(outs):

        @pl.when(step * len(outs) // steps == place)
        def _(out_ref=out_ref):
            out_ref[:unit_rows] = units
            out_ref[unit_rows:] = downs


def ffn_grad_rows(hidden, grads, units, acts, whole):
    first, second = places_here()
    zl = lax.axis_index("zl")
    tokens, width = hidden[0].shape
    columns = units[2].shape[1]
    order = (0, 1, 2, 3) if whole else (1 - zl, 3 - zl, zl, 2 + zl)
    meta = jnp.stack([jnp.asarray(value, jnp.int32) for value in (*order, second, first)])

    def left_spec(block):
        return pl.BlockSpec((block.shape[0], width // 4), lambda index, meta_ref: (0, meta_ref[index]))

    def half_spec(position):
        return pl.BlockSpec((tokens, columns), lambda index, meta_ref: (0, meta_ref[position]))

    def full_spec(rows):
        return pl.BlockSpec((rows, columns), lambda index, meta_ref: (0, 0))

    out_rows = width // 4 + width // 8
    outs = 1 if whole else 2
    steps = 4 // outs

    def out_spec(place):
        return pl.BlockSpec((out_rows, columns), lambda index, meta_ref: (jnp.clip(index - place * steps, 0, steps - 1), 0))

    return pl.pallas_call(
        ffn_grad_kernel,
        grid_spec=pltpu.PrefetchScalarGridSpec(
            num_scalar_prefetch=1,
            grid=(4,),
            in_specs=[left_spec(block) for block in (*hidden, *grads)]
            + [half_spec(4), half_spec(4), full_spec(2 * tokens), half_spec(5), full_spec(tokens), full_spec(2 * tokens)],
            out_specs=[out_spec(place) for place in range(outs)],
        ),
        out_shape=[jax.ShapeDtypeStruct((steps * out_rows, columns), BF16)] * outs,
        compiler_params=pltpu.CompilerParams(vmem_limit_bytes=30 << 20),
        cost_estimate=pl.CostEstimate(
            flops=8 * tokens * 4 * out_rows * columns, bytes_accessed=14 << 20, transcendentals=0
        ),
    )(meta, *hidden, *grads, *units, *acts)


def row_kernel(a_ref, a_far_ref, b_ref, b_far_ref, right_ref, right_far_ref, send_ref, keep_ref, *, cut):
    core, (first, second) = lax.axis_index("wsh"), places_here()
    for left_ref, left_far_ref, span in ((a_ref, a_far_ref, slice(0, cut)), (b_ref, b_far_ref, slice(cut, None))):
        sums = product_tn(left_ref[...], right_ref[:, span]) + product_tn(left_far_ref[...], right_far_ref[:, span])
        pieces = quarters(sums, 0, core)
        pieces = [at_place(pieces[0::2], first), at_place(pieces[1::2], first)]
        keep_ref[:, span] = at_place(pieces, second).astype(BF16)
        send_ref[:, span] = at_place(pieces[::-1], second).astype(BF16)


def row_grad_rows(lefts, rights, cut):
    (a, a_far), (b, b_far) = lefts
    tokens, width = a.shape
    columns = rights[0].shape[1]
    out_rows = width // 16
    left_spec = pl.BlockSpec((tokens, width // 4), lambda index: (0, index))
    return pl.pallas_call(
        partial(row_kernel, cut=cut),
        grid=(4,),
        in_specs=[left_spec] * 4 + [whole_spec(tokens, columns)] * 2,
        out_specs=[rows_spec(out_rows, columns)] * 2,
        out_shape=[jax.ShapeDtypeStruct((4 * out_rows, columns), BF16)] * 2,
        compiler_params=pltpu.CompilerParams(vmem_limit_bytes=20 << 20),
        cost_estimate=pl.CostEstimate(flops=4 * tokens * width * columns, bytes_accessed=6 << 20, transcendentals=0),
    )(a, a_far, b, b_far, *rights)


def trade(block, axis):
    return lax.ppermute(block, axis, SWAP)


def trade_mirrored(block, stage):
    route = []
    for index in range(32):
        along_x = (index % 2 == 0) == (stage == 1)
        route.append((index, index ^ (2 if along_x else 4)))
    return lax.ppermute(block, EVERY, route)


def rows_at(blocks, axis, which):
    return lax.dynamic_index_in_dim(blocks, which, axis, keepdims=False)


def add_low(kept, arrived):
    return (kept.astype(F32) + arrived.astype(F32)).astype(BF16)


def tie(*values):
    return lax.optimization_barrier(values)


def sum_everywhere(vector, between):
    devices = lax.axis_size(EVERY)
    piece = -(-vector.size // (devices * LANES)) * LANES
    padded = jnp.pad(vector, (0, devices * piece - vector.size)).reshape(devices, 1, piece)
    turn_over = partial(lax.all_to_all, axis_name=EVERY, split_axis=0, concat_axis=0, tiled=True)
    own = between(jnp.sum(turn_over(padded), axis=0, keepdims=True))
    return turn_over(jnp.broadcast_to(own, (devices, 1, piece))).reshape(-1)


def mirrored_rows(shard, core):
    return jnp.stack(quarters(shard, 0, core)).reshape(2, 2, -1, shard.shape[1])


class AlongZ:
    def z_start(self, main, send, keep):
        main, send, keep = tie(main, send, keep)
        self.part = keep, trade(send, "zl")
        return main

    def z_second(self, main):
        keep, arrived = self.part
        main, arrived = tie(main, arrived)
        summed = add_low(keep, arrived).reshape(2, -1, keep.shape[-1])
        here = lax.axis_index("zh")
        send, keep = rows_at(summed, 0, 1 - here), rows_at(summed, 0, here)
        main, send, keep = tie(main, send, keep)
        self.part = keep, trade(send, "zh")
        return main

    def z_done(self, main):
        keep, arrived = self.part
        main, arrived = tie(main, arrived)
        self.part = keep, arrived
        return main


class FourChips:
    def __init__(self, own):
        self.own, self.near = own, trade_mirrored(own, 1)

    def second(self, main):
        main, near = tie(main, self.near)
        across = swap_cores(near)
        half = half_of(across, lax.axis_index("wsh"))
        main, half = tie(main, half)
        self.near, self.across, self.last = near, across, trade_mirrored(half, 1)
        return main

    def third(self, main):
        main, last = tie(main, self.last)
        self.blocks = self.own, self.near, self.across, last, swap_cores(last)
        return main


class FfnGrads(AlongZ):
    def __init__(self, offload):
        self.core, self.places, self.offload = lax.axis_index("wsh"), places_here(), offload

    def hidden_known(self, hidden):
        self.hidden = FourChips(hidden)

    def act_known(self, act):
        self.act = act
        self.act_far = trade_mirrored(half_of(act, 1 - self.places[0], 1), 1)

    def grad_known(self, grad):
        self.grad = FourChips(grad)

    def units_known(self, gate_low, up_low):
        place = self.places[0]
        self.keep = at_place((gate_low, up_low), place)
        self.far = trade_mirrored(at_place((up_low, gate_low), place), 1)

    def hidden_second(self, main):
        return self.hidden.second(main)

    def hidden_third(self, main):
        return self.hidden.third(main)

    def grad_second(self, main):
        return self.grad.second(main)

    def grad_third(self, main):
        return self.grad.third(main)

    def act_second(self, main):
        main, self.act_far = tie(main, self.act_far)
        main, send = tie(main, jnp.concatenate([half_of(self.act, self.places[0], 1), self.act_far], axis=0))
        self.act_last = trade_mirrored(send, 2)
        return main

    def act_in(self, main):
        main, self.act_last = tie(main, self.act_last)
        return main

    def units_in(self, main):
        main, self.last = tie(main, self.last)
        return main

    def units_second(self, main):
        main, self.far = tie(main, self.far)
        other = 1 - self.places[1]
        main, send = tie(main, jnp.concatenate([half_of(self.keep, other, 1), half_of(self.far, other, 1)], axis=0))
        self.last = trade_mirrored(send, 2)
        return main

    def multiply(self, main):
        main, last, act_last = tie(main, self.last, self.act_last)
        sums = ffn_grad_rows(
            self.hidden.blocks,
            self.grad.blocks,
            (self.keep, self.far, last),
            (self.act, self.act_far, act_last),
            self.offload,
        )
        if not self.offload:
            return self.z_start(main, *sums)
        main, sums = tie(main, *sums)
        self.rows = lax.psum_scatter(sums, ("zh", "zl"), scatter_dimension=0, tiled=True)
        return main

    def landed(self, main):
        main, self.rows = tie(main, self.rows)
        return main

    def finish(self):
        first, second = self.places
        rows = self.rows if self.offload else add_low(*self.part)
        unit_rows = rows.shape[0] // 3 * 2
        units = jnp.stack(quarters(rows[:unit_rows], 0, self.core)).reshape(2, 2, -1, rows.shape[1])
        downs = rows[unit_rows:].reshape(2, -1, rows.shape[1])
        far = trade_mirrored(rows_at(units, 1, 1 - second), 2)
        units = ordered(second, rows_at(units, 1, second), far)
        columns = units.shape[2]
        own, far = (
            jnp.concatenate([rows_at(units, 0, which), rows_at(downs, 0, which)], axis=1)
            for which in (first, 1 - first)
        )
        far = trade_mirrored(far, 1).astype(F32)
        own = own.astype(F32)
        gate = at_place((own[:, :columns], far[:, :columns]), first)
        up = at_place((far[:, :columns], own[:, :columns]), first)
        return gate, up, ordered(first, own[:, columns:], far[:, columns:])


class RowGrads(AlongZ):
    def __init__(self):
        self.lefts = [None, None]

    def left_known(self, index, left):
        self.lefts[index] = left, trade_mirrored(left, 1)

    def rights_known(self, first, second):
        self.cut = first.shape[1]
        right = jnp.concatenate([first, second], axis=1)
        self.rights = right, trade_mirrored(right, 1)

    def left_in(self, main):
        main, self.lefts = tie(main, self.lefts)
        return main

    def multiply(self, main):
        main, far, lefts = tie(main, self.rights[1], self.lefts)
        main, (send, keep) = tie(main, row_grad_rows(lefts, (self.rights[0], far), self.cut))
        self.part = keep, trade_mirrored(send, 2)
        return main

    def pair_done(self, main):
        keep, arrived = self.part
        main, arrived = tie(main, arrived)
        summed = add_low(keep, arrived).reshape(2, 2, -1, keep.shape[-1])
        here = lax.axis_index("zl")
        send, keep = (rows_at(summed, 1, which).reshape(-1, keep.shape[-1]) for which in (1 - here, here))
        return self.z_start(main, send, keep)

    def finish(self):
        keep, arrived = self.part
        summed = keep.astype(F32) + arrived.astype(F32)
        return summed[:, : self.cut], summed[:, self.cut :]


def plain_grad(left, right):
    return lax.psum_scatter(product_tn(left, right).astype(BF16), SEQ, scatter_dimension=0, tiled=True).astype(F32)


class PlainFfnGrads:
    def __init__(self, offload):
        pass

    def hidden_known(self, hidden):
        self.hidden = hidden

    def act_known(self, act):
        self.act = act

    def grad_known(self, grad):
        self.grad = grad

    def units_known(self, gate_low, up_low):
        self.units = gate_low, up_low

    def finish(self):
        gate, up = (plain_grad(self.hidden, unit) for unit in self.units)
        return gate, up, plain_grad(self.grad, self.act)


class PlainRowGrads:
    def __init__(self):
        self.lefts = [None, None]

    def left_known(self, index, left):
        self.lefts[index] = left

    def rights_known(self, *rights):
        self.rights = rights

    def finish(self):
        return tuple(plain_grad(left, right) for left, right in zip(self.lefts, self.rights))


def shards(
    tokens,
    doc_start,
    cotangent,
    mix_gain,
    in_proj,
    conv_taps,
    mix_proj,
    ffn_gain_a,
    gate_a,
    up_a,
    down_a,
    attn_gain,
    query_proj,
    key_proj,
    value_proj,
    attn_proj,
    query_gain,
    key_gain,
    ffn_gain_b,
    gate_b,
    up_b,
    down_b,
):
    streams, seq_rows, width = tokens.shape
    core = lax.axis_index("wsh")
    sequences = streams * lax.axis_size("wsh")
    token_count = streams * seq_rows
    head_width = query_gain.shape[0]
    groups = key_proj.shape[1] // head_width
    score_scale = head_width ** (-0.5)
    margin = conv_taps.shape[0] - 1
    half_width = width // 2
    chips = lax.axis_size(SEQ)
    chip = lax.axis_index(SEQ)
    positions = chip * seq_rows + jnp.arange(seq_rows, dtype=jnp.int32)
    paired = all(lax.axis_size(name) == 2 for name in SEQ)
    ffn_kind, rows_kind = (FfnGrads, RowGrads) if paired else (PlainFfnGrads, PlainRowGrads)
    ffn_a, ffn_b, mixer_rows, attn_rows = ffn_kind(False), ffn_kind(True), rows_kind(), rows_kind()

    def step(main, *events):
        if paired:
            for owner, name in events:
                main = getattr(owner, name)(main)
        return main

    frequency = ROPE_BASE ** (-(jnp.arange(0, head_width, 2, dtype=F32) / head_width))
    angles = positions.astype(F32)[:, None] * jnp.tile(frequency, 4)[None, :]
    tables = (jnp.cos(angles), jnp.sin(angles))
    query_gain_row = jnp.tile(query_gain, 2)[None, :]
    key_gain_row = jnp.tile(key_gain, 2)[None, :]

    def split_rows(weight, sent):
        return half_of(weight, core), half_of(swap_cores(sent), core)

    def out_product(left, pieces):
        return ordered(core, product(left, pieces[0]), product(left, pieces[1]))

    def out_product_back(grad, pieces):
        own = half_of(grad, core, 1)
        other = half_of(grad, 1 - core, 1)
        return product_nt(own, pieces[0]) + product_nt(other, pieces[1])

    def sum_cores(partial_rows):
        return half_of(partial_rows, core) + swap_cores(half_of(partial_rows, 1 - core))

    starts_far = swap_cores(doc_start)
    starts_here = jnp.concatenate(
        [jnp.where(core == 0, doc_start, starts_far), jnp.where(core == 0, starts_far, doc_start)], axis=0
    )
    in_far = swap_cores(in_proj)
    in_low, in_high = in_proj[:, :half_width], in_proj[:, 2 * half_width :]
    in_mid = in_far[:, half_width : 2 * half_width]

    grad_out = cotangent.reshape(token_count, width)
    down_low_b = gather_cores(grad_out.astype(BF16))
    flat_tokens = tokens.reshape(token_count, width)
    low_one = gather_cores(norm_rows(flat_tokens, mix_gain).astype(BF16))
    low_one, mix_far, down_a_far = tie(low_one, mix_proj, down_a)
    mix_pieces = split_rows(mix_proj, mix_far)
    down_a_pieces = split_rows(down_a, down_a_far)
    part_low = product(low_one, in_low)
    part_mid = product(low_one, in_mid)
    part_high = product(low_one, in_high)
    factor = jnp.where(core == 0, part_low, part_high)
    c_part = jnp.where(core == 0, part_high, part_low)
    gated = (part_mid * factor).reshape(sequences, seq_rows, half_width)
    edge_rows = lax.ppermute(gated[:, seq_rows - margin :, :], SEQ, [(i, i + 1) for i in range(chips - 1)])
    extended = jnp.concatenate([edge_rows, gated], axis=1)
    taps_here = half_of(conv_taps, core, 1)

    def convolve(extended_rows, taps_now):
        running = jnp.zeros_like(extended_rows[:, margin:])
        for tap_index in range(margin + 1):
            offset = margin - tap_index
            shifted = extended_rows[:, tap_index : tap_index + seq_rows]
            allowed = (positions[None, :] - offset >= starts_here)[:, :, None]
            running = running + jnp.where(allowed, shifted, 0.0) * taps_now[tap_index]
        return running

    mixed_conv = convolve(extended, taps_here).reshape(-1, half_width)
    mixer_low = (c_part * mixed_conv).astype(BF16)
    mixer_rows.left_known(1, low_one)
    resid_one = flat_tokens + sum_cores(out_product(mixer_low, mix_pieces))

    def ffn_units(grads, residual, gain_vec, gate_weight, up_weight):
        hidden_low = gather_cores(norm_rows(residual, gain_vec).astype(BF16))
        grads.hidden_known(hidden_low)
        gate_val = product(hidden_low, gate_weight)
        up_val = product(hidden_low, up_weight)
        act_low = gated_unit(gate_val, up_val).astype(BF16)
        grads.act_known(act_low)
        return gate_val, up_val, act_low

    gate_val_a, up_val_a, act_low_a = ffn_units(ffn_a, resid_one, ffn_gain_a, gate_a, up_a)
    resid_two = resid_one + sum_cores(out_product(act_low_a, down_a_pieces))

    low_three = gather_cores(norm_rows(resid_two, attn_gain).astype(BF16))
    low_three, attn_far, down_b_far = tie(low_three, attn_proj, down_b)
    attn_pieces = split_rows(attn_proj, attn_far)
    down_b_pieces = split_rows(down_b, down_b_far)
    attn_rows.left_known(1, low_three)
    query_raw = product(low_three, query_proj)
    key_raw = product(low_three, key_proj)
    value_raw = product(low_three, value_proj)
    packed = heads_forward(query_raw, key_raw, value_raw, starts_here, tables, query_gain_row, key_gain_row)

    team = SEQ if chips == sequences * groups else ("y", "x")
    rest = () if team == SEQ else ("zh", "zl")
    to_heads = partial(lax.all_to_all, axis_name=team, split_axis=0, concat_axis=0, tiled=True)
    packed = to_heads(packed)
    length = packed.shape[0] * seq_rows
    mixer_whole = gather_cores(mixer_low, 1)
    packed, mixer_whole, down_low_b = tie(packed, mixer_whole, down_low_b)
    packed = step(packed, (ffn_a, "hidden_second"))
    mixer_rows.left_known(0, mixer_whole)
    ffn_b.grad_known(down_low_b)
    kv, kv_block = (lax.all_gather(packed[:, :, LANES:], rest, axis=0, tiled=True), 0) if rest else (packed, 1)
    attended_low, attended_full, logs = attend(packed, kv, kv_block, rest, score_scale)

    def from_heads(block):
        back = to_heads(block.reshape(sequences * groups, seq_rows, -1))
        back = back.reshape(groups, sequences, seq_rows, -1)
        return jnp.transpose(back, (1, 2, 0, 3)).reshape(sequences * seq_rows, -1)

    attended_low = step(attended_low, (ffn_a, "act_second"))
    attn_low = from_heads(attended_low)
    grad_act_b = out_product_back(down_low_b, down_b_pieces)
    attn_low, grad_act_b = tie(attn_low, grad_act_b)
    attn_low = step(attn_low, (ffn_a, "hidden_third"), (ffn_b, "grad_second"))
    resid_three = resid_two + sum_cores(out_product(attn_low, attn_pieces))
    gate_val_b, up_val_b, act_low_b = ffn_units(ffn_b, resid_three, ffn_gain_b, gate_b, up_b)

    def units_back(gate_val, up_val, grad_act):
        _, pull_unit = jax.vjp(gated_unit, gate_val, up_val)
        grad_gate_val, grad_up_val = pull_unit(grad_act)
        return grad_gate_val.astype(BF16), grad_up_val.astype(BF16)

    def norm_back(residual, gain_vec, partial_grad, grad_after):
        _, pull_norm = jax.vjp(norm_rows, residual, gain_vec)
        grad_resid, grad_gain = pull_norm(sum_cores(partial_grad))
        return grad_after + grad_resid, grad_gain

    gate_low, up_low = units_back(gate_val_b, up_val_b, grad_act_b)
    ffn_b.units_known(gate_low, up_low)
    grad_three, grad_gain_b = norm_back(
        resid_three, ffn_gain_b, product_nt(gate_low, gate_b) + product_nt(up_low, up_b), grad_out
    )
    grad_attn_low = gather_cores(grad_three.astype(BF16))
    grad_heads = heads_grad(
        half_of(grad_attn_low, core, 1), half_of(grad_attn_low, 1 - core, 1), attn_pieces, sequences
    )
    grad_heads = step(
        grad_heads, (ffn_b, "grad_third"), (ffn_b, "units_second"), (ffn_b, "act_second"), (ffn_b, "hidden_second")
    )
    grad_heads = to_heads(grad_heads).reshape(length, LANES)
    attn_whole = gather_cores(attn_low, 1)
    grad_heads, attn_whole = tie(grad_heads, attn_whole)
    attn_rows.left_known(0, attn_whole)
    grad_heads = step(grad_heads, (ffn_a, "act_in"))
    query_grads, kv_grads = attend_back(packed, kv, kv_block, rest, grad_heads, attended_full, logs, score_scale)
    if rest:
        kv_grads = lax.psum_scatter(kv_grads, rest, scatter_dimension=0, tiled=True)
    query_grads = step(query_grads, (ffn_b, "hidden_third"))
    packed_grads = jnp.concatenate([query_grads, kv_grads], axis=1)
    packed_grads = to_heads(packed_grads.reshape(sequences * groups, seq_rows, 2 * LANES))
    packed_grads = step(packed_grads, (ffn_b, "multiply"), (attn_rows, "left_in"))
    query_back, key_back, value_back, query_term, key_term = heads_backward(
        packed_grads, query_raw, key_raw, tables, query_gain_row, key_gain_row
    )
    attn_rows.rights_known(
        half_of(grad_attn_low, core, 1), jnp.concatenate([query_back, key_back, value_back], axis=1)
    )
    grad_two, grad_attn_gain = norm_back(
        resid_two,
        attn_gain,
        product_nt(query_back, query_proj) + product_nt(key_back, key_proj) + product_nt(value_back, value_proj),
        grad_three,
    )

    down_low_a = gather_cores(grad_two.astype(BF16))
    gate_low, up_low = units_back(gate_val_a, up_val_a, out_product_back(down_low_a, down_a_pieces))
    ffn_a.units_known(gate_low, up_low)
    gate_low, down_low_a = tie(gate_low, down_low_a)
    ffn_a.grad_known(down_low_a)
    grad_one, grad_gain_a = norm_back(
        resid_one, ffn_gain_a, product_nt(gate_low, gate_a) + product_nt(up_low, up_a), grad_two
    )
    grad_mix_low = gather_cores(grad_one.astype(BF16))
    grad_mixer = out_product_back(grad_mix_low, mix_pieces)
    grad_mixer = step(grad_mixer, (attn_rows, "multiply"), (ffn_a, "units_second"), (ffn_a, "grad_second"))
    grad_c_part = grad_mixer * mixed_conv
    grad_conv = (grad_mixer * c_part).reshape(sequences, seq_rows, half_width)
    _, pull_conv = jax.vjp(convolve, extended, taps_here)
    grad_extended, grad_taps = pull_conv(grad_conv)
    returned = lax.ppermute(grad_extended[:, :margin, :], SEQ, [(i + 1, i) for i in range(chips - 1)])
    grad_gated = grad_extended[:, margin:, :] + jnp.concatenate(
        [jnp.zeros((sequences, seq_rows - margin, half_width), F32), returned], axis=1
    )
    grad_gated = grad_gated.reshape(-1, half_width)
    grad_gated = step(grad_gated, (ffn_a, "units_in"), (attn_rows, "pair_done"))
    grad_factor = grad_gated * part_mid
    mid_low = (grad_gated * factor).astype(BF16)
    low_low = jnp.where(core == 0, grad_factor, grad_c_part).astype(BF16)
    high_low = jnp.where(core == 0, grad_c_part, grad_factor).astype(BF16)
    mixer_rows.rights_known(
        half_of(grad_mix_low, core, 1), jnp.concatenate([low_low, swap_cores(mid_low), high_low], axis=1)
    )
    low_low = step(low_low, (ffn_a, "grad_third"), (ffn_a, "multiply"), (attn_rows, "z_second"), (ffn_b, "landed"))
    partial_one = product_nt(low_low, in_low) + product_nt(mid_low, in_mid) + product_nt(high_low, in_high)
    partial_one = step(partial_one, (mixer_rows, "multiply"))
    grad_tokens, grad_mix_gain = norm_back(flat_tokens, mix_gain, partial_one, grad_one)
    tokens_grad = grad_tokens.reshape(streams, seq_rows, width)
    grad_taps = lax.dynamic_update_slice_in_dim(jnp.zeros_like(conv_taps), grad_taps, core * half_width, 1)
    small = jnp.concatenate(
        [
            grad_mix_gain,
            grad_taps.reshape(-1),
            grad_gain_a,
            grad_attn_gain,
            grad_gain_b,
            query_term[0],
            key_term[0],
        ]
    )
    small = step(small, (mixer_rows, "pair_done"), (ffn_a, "z_second"), (mixer_rows, "z_second"), (attn_rows, "z_done"))
    act_low_b, small = tie(act_low_b, small)
    output = resid_three + sum_cores(out_product(act_low_b, down_b_pieces))
    done_b, done_attn = ffn_b.finish(), attn_rows.finish()

    def between(own):
        nonlocal output, done_b, done_attn
        own, output, done_b, done_attn = tie(own, output, done_b, done_attn)
        return step(own, (ffn_a, "z_done"), (mixer_rows, "z_done"))

    small = sum_everywhere(small, between)
    taps_end = width + conv_taps.size
    heads_at = taps_end + 3 * width

    def head_gain(offset):
        both = small[offset : offset + LANES]
        return both[:head_width] + both[head_width:]

    gate_a_grad, up_a_grad, down_a_grad = ffn_a.finish()
    gate_b_grad, up_b_grad, down_b_grad = done_b
    mix_grad, proj_grad = mixer_rows.finish()
    attn_grad, qkv_grad = done_attn
    query_columns, key_columns = query_proj.shape[1], key_proj.shape[1]
    return (
        output.reshape(streams, seq_rows, width),
        tokens_grad,
        small[:width],
        proj_grad,
        small[width:taps_end].reshape(conv_taps.shape),
        mix_grad,
        small[taps_end : taps_end + width],
        gate_a_grad,
        up_a_grad,
        down_a_grad.T,
        small[taps_end + width : taps_end + 2 * width],
        qkv_grad[:, :query_columns],
        qkv_grad[:, query_columns : query_columns + key_columns],
        qkv_grad[:, query_columns + key_columns :],
        attn_grad,
        head_gain(heads_at),
        head_gain(heads_at + LANES),
        small[taps_end + 2 * width : taps_end + 3 * width],
        gate_b_grad,
        up_b_grad,
        down_b_grad.T,
    )


def chip_grid(chips):
    along_z = math.gcd(4, chips)
    side = math.isqrt(chips // along_z)
    return along_z // 2, 2, chips // along_z // side, side


def solution(mesh):
    cores = mesh.shape["wsh"]
    grid = Mesh(mesh.devices.reshape(*chip_grid(mesh.shape["seq"]), cores), EVERY)
    tokens_spec = P("wsh", SEQ, None)
    columns = P(None, "wsh")
    grads = P(SEQ, "wsh")
    in_specs = (
        tokens_spec,
        P("wsh", SEQ),
        tokens_spec,
        P(),
        columns,
        P(),
        columns,
        P(),
        columns,
        columns,
        columns,
        P(),
        columns,
        columns,
        columns,
        columns,
        P(),
        P(),
        P(),
        columns,
        columns,
        columns,
    )
    out_specs = (
        tokens_spec,
        tokens_spec,
        P(),
        grads,
        P(),
        grads,
        P(),
        grads,
        grads,
        P("wsh", SEQ),
        P(),
        grads,
        grads,
        grads,
        grads,
        P(),
        P(),
        P(),
        grads,
        grads,
        P("wsh", SEQ),
    )
    return jax.shard_map(shards, mesh=grid, in_specs=in_specs, out_specs=out_specs, check_vma=False)
```

```python
from functools import partial
import math

import jax
import jax.numpy as jnp
from jax import lax
from jax.experimental import pallas as pl
from jax.experimental.pallas import tpu as pltpu
from jax.sharding import Mesh, PartitionSpec as P

EPS = 1e-05
ROPE_BASE = 1000000.0
MASKED = -1e30
START_PEAK = -1e25
SEQ = ("zh", "zl", "y", "x")
EVERY = SEQ + ("wsh",)
SWAP = [(0, 1), (1, 0)]
BF16 = jnp.bfloat16
F32 = jnp.float32
LANES = 128


def norm_rows(values, gain_vec):
    return values * lax.rsqrt(jnp.mean(values * values, axis=-1, keepdims=True) + EPS) * gain_vec


def product(left, right):
    return jnp.dot(left, right, preferred_element_type=F32)


def product_tn(left, right):
    return lax.dot_general(left, right, (((0,), (0,)), ((), ())), preferred_element_type=F32)


def product_nt(left, right):
    return lax.dot_general(left, right, (((1,), (1,)), ((), ())), preferred_element_type=F32)


def gated_unit(gate_val, up_val):
    return jax.nn.silu(gate_val) * up_val


def swap_cores(block):
    return lax.ppermute(block, "wsh", SWAP)


def gather_cores(block, axis=0):
    return lax.all_gather(block, "wsh", axis=axis, tiled=True)


def half_of(array, which, axis=0):
    size = array.shape[axis] // 2
    return lax.dynamic_slice_in_dim(array, which * size, size, axis)


def ordered(core, own, other):
    first = jnp.where(core == 0, own, other)
    second = jnp.where(core == 0, other, own)
    return jnp.concatenate([first, second], axis=-1)


def lane_of(shape):
    return lax.broadcasted_iota(jnp.int32, shape, 1)


def two_heads(block):
    return jnp.concatenate([block[:, :64], block[:, 64:]], axis=0)


def side_by_side(block):
    rows = block.shape[0] // 2
    return jnp.concatenate([block[:rows], block[rows:]], axis=1)


EXTRA = 16


def flat(block):
    return block[:, : block.shape[1] - EXTRA].reshape(-1, block.shape[2])


def places(packed_ref, offset):
    chips, padded, _ = packed_ref.shape
    rows = padded - EXTRA
    coded = packed_ref[:, rows, :].astype(F32)
    starts = coded[:, :64] * 64.0 + coded[:, 64:]
    diagonal = lax.broadcasted_iota(jnp.int32, (rows, rows), 0) == lane_of((rows, rows))
    columns = [
        jnp.sum(jnp.where(diagonal, starts[chip : chip + 1], 0.0), axis=1, keepdims=True) for chip in range(chips)
    ]
    starts = jnp.concatenate(columns * 2, axis=0).astype(jnp.int32)
    row = lax.broadcasted_iota(jnp.int32, (2 * chips * rows, 1), 0)
    row = jnp.where(row >= chips * rows, row - chips * rows, row)
    return starts, offset + pl.program_id(0) * chips * rows + row


def first_place(rest, length):
    return lax.axis_index(rest) * length if rest else 0


def lay_out(kv_ref, flat_ref):
    rows = kv_ref.shape[1] - EXTRA

    @pl.when(pl.program_id(0) == 0)
    def _():
        for chip in range(kv_ref.shape[0]):
            flat_ref[chip * rows : (chip + 1) * rows] = kv_ref[chip, :rows]


def attend_kernel(packed_ref, kv_ref, low_ref, full_ref, log_ref, flat_ref, *, rest, span, scale):
    lay_out(kv_ref, flat_ref)
    rows = low_ref.shape[0]
    offset = first_place(rest, rows * pl.num_programs(0))
    query = two_heads(flat(packed_ref[...]))
    starts, mine = places(packed_ref, offset)

    def advance(index, carried):
        peak, total, mixed = carried
        kv_block = flat_ref[pl.ds(pl.multiple_of(index * span, span), span), :]
        scores = product_nt(query, kv_block[:, :64]) * scale
        place = index * span + lane_of((1, span))
        scores = jnp.where((place >= starts) & (place <= mine), scores, MASKED)
        fresh_peak = jnp.maximum(peak, jnp.max(scores, axis=1, keepdims=True))
        shares = jnp.exp(scores - fresh_peak)
        keep = jnp.exp(peak - fresh_peak)
        total = total * keep + jnp.sum(shares, axis=1, keepdims=True)
        mixed = mixed * keep + product(shares.astype(BF16), kv_block[:, 64:])
        return fresh_peak, total, mixed

    last = (offset + (pl.program_id(0) + 1) * rows) // span
    peak, total, mixed = lax.fori_loop(
        0,
        last,
        advance,
        (
            jnp.full((2 * rows, 1), START_PEAK, F32),
            jnp.zeros((2 * rows, 1), F32),
            jnp.zeros((2 * rows, 64), F32),
        ),
    )
    attended = side_by_side(mixed / total)
    low_ref[...] = attended.astype(BF16)
    full_ref[...] = attended
    log_ref[...] = side_by_side(jnp.broadcast_to(peak + jnp.log(total), (2 * rows, 64)))


def attend_back_kernel(packed_ref, kv_ref, grad_ref, full_ref, log_ref, dq_ref, dkv_ref, sums_ref, flat_ref, *, rest, span, scale):
    lay_out(kv_ref, flat_ref)
    rows = grad_ref.shape[0]
    offset = first_place(rest, rows * pl.num_programs(0))
    query = two_heads(flat(packed_ref[...]))
    grad = two_heads(grad_ref[...])
    attended = two_heads(full_ref[...])
    logs = two_heads(log_ref[...])[:, :1]
    delta = jnp.sum(grad.astype(F32) * attended, axis=1, keepdims=True)
    starts, mine = places(packed_ref, offset)

    @pl.when(pl.program_id(0) == 0)
    def _():
        sums_ref[...] = jnp.zeros_like(sums_ref)

    def advance(index, query_grad):
        window = pl.ds(pl.multiple_of(index * span, span), span)
        kv_block = flat_ref[window, :]
        key, value = kv_block[:, :64], kv_block[:, 64:]
        scores = product_nt(query, key) * scale
        place = index * span + lane_of((1, span))
        scores = jnp.where((place >= starts) & (place <= mine), scores, MASKED)
        shares = jnp.exp(scores - logs)
        grad_scores = (shares * (product_nt(grad, value) - delta)).astype(BF16)
        key_grad = product_tn(grad_scores, query) * scale
        value_grad = product_tn(shares.astype(BF16), grad)
        sums_ref[window, :] += jnp.concatenate([key_grad, value_grad], axis=1)
        return query_grad + product(grad_scores, key)

    last = (offset + (pl.program_id(0) + 1) * rows) // span
    query_grad = lax.fori_loop(0, last, advance, jnp.zeros((2 * rows, 64), F32))
    dq_ref[...] = side_by_side(query_grad * scale).astype(BF16)

    @pl.when(pl.program_id(0) == pl.num_programs(0) - 1)
    def _():
        dkv_ref[...] = sums_ref[...].astype(BF16)


def rows_spec(rows, columns, column_block=0):
    return pl.BlockSpec((rows, columns), lambda index: (index, column_block))


def whole_spec(rows, columns, column_block=0):
    return pl.BlockSpec((rows, columns), lambda index: (0, column_block))


def attend_specs(packed, kv, kv_block):
    chips, padded, _ = packed.shape
    per_step = max(1, 256 // (padded - EXTRA))
    packed_spec = pl.BlockSpec((per_step, padded, LANES), lambda index: (index, 0, 0))
    kv_spec = pl.BlockSpec((kv.shape[0], padded, LANES), lambda index: (0, 0, kv_block))
    return chips // per_step, per_step * (padded - EXTRA), [packed_spec, kv_spec]


def attend(packed, kv, kv_block, rest, scale):
    steps, rows, specs = attend_specs(packed, kv, kv_block)
    length, keys = steps * rows, kv.shape[0] * (kv.shape[1] - EXTRA)
    return pl.pallas_call(
        partial(attend_kernel, rest=rest, span=rows, scale=scale),
        grid=(steps,),
        in_specs=specs,
        out_specs=[rows_spec(rows, LANES)] * 3,
        out_shape=[
            jax.ShapeDtypeStruct((length, LANES), BF16),
            jax.ShapeDtypeStruct((length, LANES), F32),
            jax.ShapeDtypeStruct((length, LANES), F32),
        ],
        scratch_shapes=[pltpu.VMEM((keys, LANES), BF16)],
        compiler_params=pltpu.CompilerParams(vmem_limit_bytes=24 << 20),
        cost_estimate=pl.CostEstimate(flops=4 * length * keys * 64, bytes_accessed=2 << 20, transcendentals=length * keys),
    )(packed, kv)


def attend_back(packed, kv, kv_block, rest, grad, full, logs, scale):
    steps, rows, specs = attend_specs(packed, kv, kv_block)
    length, keys = steps * rows, kv.shape[0] * (kv.shape[1] - EXTRA)
    return pl.pallas_call(
        partial(attend_back_kernel, rest=rest, span=rows, scale=scale),
        grid=(steps,),
        in_specs=specs + [rows_spec(rows, LANES)] * 3,
        out_specs=[rows_spec(rows, LANES), whole_spec(keys, LANES)],
        out_shape=[jax.ShapeDtypeStruct((length, LANES), BF16), jax.ShapeDtypeStruct((keys, LANES), BF16)],
        scratch_shapes=[pltpu.VMEM((keys, LANES), F32), pltpu.VMEM((keys, LANES), BF16)],
        compiler_params=pltpu.CompilerParams(vmem_limit_bytes=24 << 20),
        cost_estimate=pl.CostEstimate(flops=10 * length * keys * 64, bytes_accessed=3 << 20, transcendentals=length * keys),
    )(packed, kv, grad, full, logs)


def heads_grad_kernel(own_ref, other_ref, own_piece_ref, other_piece_ref, out_ref):
    sums = product_nt(own_ref[...], own_piece_ref[...]) + product_nt(other_ref[...], other_piece_ref[...])
    out_ref[...] = sums.astype(BF16).reshape(out_ref.shape)


def heads_grad(own, other, pieces, sequences):
    tokens, columns = own.shape
    groups = pieces[0].shape[0] // LANES
    piece_spec = pl.BlockSpec((LANES, columns), lambda index: (index, 0))
    rows = tokens // sequences
    return pl.pallas_call(
        heads_grad_kernel,
        grid=(groups,),
        in_specs=[whole_spec(tokens, columns)] * 2 + [piece_spec] * 2,
        out_specs=pl.BlockSpec((sequences, rows, LANES), lambda index: (index, 0, 0)),
        out_shape=jax.ShapeDtypeStruct((groups * sequences, rows, LANES), BF16),
        compiler_params=pltpu.CompilerParams(vmem_limit_bytes=16 << 20),
    )(own, other, *pieces)


def head_means(values):
    low_lanes = lane_of(values.shape) < 64
    low_mean = jnp.sum(jnp.where(low_lanes, values, 0.0), axis=1, keepdims=True) * (1.0 / 64)
    high_mean = jnp.sum(jnp.where(low_lanes, 0.0, values), axis=1, keepdims=True) * (1.0 / 64)
    return jnp.where(low_lanes, low_mean, high_mean)


def turn(values, sign):
    lower = (lane_of(values.shape) % 64) < 32
    return jnp.where(lower, -sign * pltpu.roll(values, LANES - 32, 1), sign * pltpu.roll(values, 32, 1))


def head_forward(raw, gain, cosine, sine):
    unit = raw * lax.rsqrt(head_means(raw * raw) + EPS) * gain
    return (unit * cosine + turn(unit, 1.0) * sine).astype(BF16)


def head_backward(raw, gain, cosine, sine, grad):
    back = grad * cosine + turn(grad * sine, -1.0)
    scale = lax.rsqrt(head_means(raw * raw) + EPS)
    gain_term = jnp.sum(back * raw * scale, axis=0, keepdims=True)
    back = back * gain
    raw_grad = back * scale - raw * (scale * scale * scale) * head_means(back * raw)
    return raw_grad.astype(BF16), gain_term


def heads_kernel(query_ref, key_ref, value_ref, starts_ref, cos_ref, sin_ref, query_gain_ref, key_gain_ref, out_ref):
    rows = out_ref.shape[1] - EXTRA
    groups = key_ref.shape[1] // 64
    sequences = query_ref.shape[0] // rows
    cosine, sine = cos_ref[...], sin_ref[...]
    for place in range(sequences):
        span = pl.ds(place * rows, rows)
        starts = jnp.broadcast_to(starts_ref[place : place + 1], (EXTRA, LANES)).astype(BF16)
        for pair in range(groups // 2):
            lanes = pl.ds(pair * LANES, LANES)
            key = head_forward(key_ref[span, lanes], key_gain_ref[...], cosine, sine)
            value = value_ref[span, lanes].astype(BF16)
            for side in range(2):
                group = 2 * pair + side
                query = head_forward(
                    query_ref[span, pl.ds(group * LANES, LANES)], query_gain_ref[...], cosine, sine
                )
                half = slice(64 * side, 64 * side + 64)
                block = group * sequences + place
                out_ref[block, :rows, 0:LANES] = query
                out_ref[block, :rows, LANES : 2 * LANES] = jnp.concatenate([key[:, half], value[:, half]], axis=1)
                out_ref[block, rows:, 0:LANES] = starts
                out_ref[block, rows:, LANES : 2 * LANES] = starts


def heads_back_kernel(
    grad_ref,
    query_ref,
    key_ref,
    cos_ref,
    sin_ref,
    query_gain_ref,
    key_gain_ref,
    dq_ref,
    dk_ref,
    dv_ref,
    query_term_ref,
    key_term_ref,
):
    rows = grad_ref.shape[1]
    groups = key_ref.shape[1] // 64
    sequences = query_ref.shape[0] // rows
    cosine, sine = cos_ref[...], sin_ref[...]
    query_term = jnp.zeros((1, LANES), F32)
    key_term = jnp.zeros((1, LANES), F32)
    for place in range(sequences):
        span = pl.ds(place * rows, rows)
        for pair in range(groups // 2):
            lanes = pl.ds(pair * LANES, LANES)
            sides = [grad_ref[(2 * pair + side) * sequences + place, :, LANES : 2 * LANES] for side in range(2)]
            key_grad = jnp.concatenate([sides[0][:, :64], sides[1][:, :64]], axis=1).astype(F32)
            dv_ref[span, lanes] = jnp.concatenate([sides[0][:, 64:], sides[1][:, 64:]], axis=1)
            low, term = head_backward(key_ref[span, lanes], key_gain_ref[...], cosine, sine, key_grad)
            dk_ref[span, lanes] = low
            key_term = key_term + term
            for side in range(2):
                group = 2 * pair + side
                wide = pl.ds(group * LANES, LANES)
                query_grad = grad_ref[group * sequences + place, :, 0:LANES].astype(F32)
                low, term = head_backward(query_ref[span, wide], query_gain_ref[...], cosine, sine, query_grad)
                dq_ref[span, wide] = low
                query_term = query_term + term
    query_term_ref[...] = query_term
    key_term_ref[...] = key_term


def heads_forward(query, key, value, starts, tables, query_gain, key_gain):
    rows = starts.shape[1]
    blocks = starts.shape[0] * (key.shape[1] // 64)
    coded = jnp.concatenate([starts // 64, starts % 64], axis=1).astype(F32)
    return pl.pallas_call(
        heads_kernel,
        out_shape=jax.ShapeDtypeStruct((blocks, rows + EXTRA, 2 * LANES), BF16),
        compiler_params=pltpu.CompilerParams(vmem_limit_bytes=32 << 20),
    )(query, key, value, coded, *tables, query_gain, key_gain)


def heads_backward(grad, query, key, tables, query_gain, key_gain):
    return pl.pallas_call(
        heads_back_kernel,
        out_shape=[
            jax.ShapeDtypeStruct(query.shape, BF16),
            jax.ShapeDtypeStruct(key.shape, BF16),
            jax.ShapeDtypeStruct(key.shape, BF16),
            jax.ShapeDtypeStruct((1, LANES), F32),
            jax.ShapeDtypeStruct((1, LANES), F32),
        ],
        compiler_params=pltpu.CompilerParams(vmem_limit_bytes=32 << 20),
    )(grad, query, key, *tables, query_gain, key_gain)


def at_place(pieces, place):
    return jnp.where(place == 0, pieces[0], pieces[1])


def quarters(block, dim, core):
    size = block.shape[dim] // 4
    pieces = [lax.slice_in_dim(block, index * size, (index + 1) * size, axis=dim) for index in range(4)]
    return [
        pieces[0],
        jnp.where(core == 0, pieces[2], pieces[1]),
        jnp.where(core == 0, pieces[1], pieces[2]),
        pieces[3],
    ]


def places_here():
    core, x, y = lax.axis_index("wsh"), lax.axis_index("x"), lax.axis_index("y")
    return jnp.where(core == 0, x, y), jnp.where(core == 0, y, x)


def ffn_grad_kernel(meta_ref, *refs):
    hidden, grads = refs[:5], refs[5:10]
    keep_ref, far_ref, last_ref, act_ref, act_far_ref, act_last_ref = refs[10:16]
    outs = refs[16:]
    rows = keep_ref.shape[0]
    core, place = lax.axis_index("wsh"), places_here()[1]

    def tokens_of(left_refs):
        own, near, across, last, last_far = (left_ref[...] for left_ref in left_refs)
        halves = jnp.where(core == 0, last, last_far), jnp.where(core == 0, last_far, last)
        return own, near, across, jnp.concatenate(halves, axis=0)

    def lanes(block):
        pieces = quarters(block, 1, core)
        return jnp.concatenate([at_place(pieces[:2], place), at_place(pieces[2:], place)], axis=1)

    def total(lefts, own_ref, near_ref, pair_ref):
        sums = product_tn(lefts[0], own_ref[...]) + product_tn(lefts[1], near_ref[...])
        return sums + product_tn(lefts[2], pair_ref[:rows]) + product_tn(lefts[3], pair_ref[rows:])

    units = total(tokens_of(hidden), keep_ref, far_ref, last_ref).astype(BF16)
    downs = total([lanes(block) for block in tokens_of(grads)], act_ref, act_far_ref, act_last_ref).astype(BF16)
    unit_rows = units.shape[0]
    step, steps = pl.program_id(0), pl.num_programs(0)

    for place, out_ref in enumerate(outs):

        @pl.when(step * len(outs) // steps == place)
        def _(out_ref=out_ref):
            out_ref[:unit_rows] = units
            out_ref[unit_rows:] = downs


def ffn_grad_rows(hidden, grads, units, acts, whole):
    first, second = places_here()
    zl = lax.axis_index("zl")
    tokens, width = hidden[0].shape
    columns = units[2].shape[1]
    order = (0, 1, 2, 3) if whole else (1 - zl, 3 - zl, zl, 2 + zl)
    meta = jnp.stack([jnp.asarray(value, jnp.int32) for value in (*order, second, first)])

    def left_spec(block):
        return pl.BlockSpec((block.shape[0], width // 4), lambda index, meta_ref: (0, meta_ref[index]))

    def half_spec(position):
        return pl.BlockSpec((tokens, columns), lambda index, meta_ref: (0, meta_ref[position]))

    def full_spec(rows):
        return pl.BlockSpec((rows, columns), lambda index, meta_ref: (0, 0))

    out_rows = width // 4 + width // 8
    outs = 1 if whole else 2
    steps = 4 // outs

    def out_spec(place):
        return pl.BlockSpec((out_rows, columns), lambda index, meta_ref: (jnp.clip(index - place * steps, 0, steps - 1), 0))

    return pl.pallas_call(
        ffn_grad_kernel,
        grid_spec=pltpu.PrefetchScalarGridSpec(
            num_scalar_prefetch=1,
            grid=(4,),
            in_specs=[left_spec(block) for block in (*hidden, *grads)]
            + [half_spec(4), half_spec(4), full_spec(2 * tokens), half_spec(5), full_spec(tokens), full_spec(2 * tokens)],
            out_specs=[out_spec(place) for place in range(outs)],
        ),
        out_shape=[jax.ShapeDtypeStruct((steps * out_rows, columns), BF16)] * outs,
        compiler_params=pltpu.CompilerParams(vmem_limit_bytes=48 << 20),
        cost_estimate=pl.CostEstimate(
            flops=8 * tokens * 4 * out_rows * columns, bytes_accessed=14 << 20, transcendentals=0
        ),
    )(meta, *hidden, *grads, *units, *acts)


def row_kernel(a_ref, a_far_ref, b_ref, b_far_ref, right_ref, right_far_ref, send_ref, keep_ref, *, cut):
    core, (first, second) = lax.axis_index("wsh"), places_here()
    for left_ref, left_far_ref, span in ((a_ref, a_far_ref, slice(0, cut)), (b_ref, b_far_ref, slice(cut, None))):
        sums = product_tn(left_ref[...], right_ref[:, span]) + product_tn(left_far_ref[...], right_far_ref[:, span])
        pieces = quarters(sums, 0, core)
        pieces = [at_place(pieces[0::2], first), at_place(pieces[1::2], first)]
        keep_ref[:, span] = at_place(pieces, second).astype(BF16)
        send_ref[:, span] = at_place(pieces[::-1], second).astype(BF16)


def row_grad_rows(lefts, rights, cut):
    (a, a_far), (b, b_far) = lefts
    tokens, width = a.shape
    columns = rights[0].shape[1]
    out_rows = width // 16
    left_spec = pl.BlockSpec((tokens, width // 4), lambda index: (0, index))
    return pl.pallas_call(
        partial(row_kernel, cut=cut),
        grid=(4,),
        in_specs=[left_spec] * 4 + [whole_spec(tokens, columns)] * 2,
        out_specs=[rows_spec(out_rows, columns)] * 2,
        out_shape=[jax.ShapeDtypeStruct((4 * out_rows, columns), BF16)] * 2,
        compiler_params=pltpu.CompilerParams(vmem_limit_bytes=20 << 20),
        cost_estimate=pl.CostEstimate(flops=4 * tokens * width * columns, bytes_accessed=6 << 20, transcendentals=0),
    )(a, a_far, b, b_far, *rights)


def trade(block, axis):
    return lax.ppermute(block, axis, SWAP)


def trade_mirrored(block, stage):
    route = []
    for index in range(32):
        along_x = (index % 2 == 0) == (stage == 1)
        route.append((index, index ^ (2 if along_x else 4)))
    return lax.ppermute(block, EVERY, route)


def rows_at(blocks, axis, which):
    return lax.dynamic_index_in_dim(blocks, which, axis, keepdims=False)


def add_low(kept, arrived):
    return (kept.astype(F32) + arrived.astype(F32)).astype(BF16)


def tie(*values):
    return lax.optimization_barrier(values)


def sum_everywhere(vector):
    devices = lax.axis_size(EVERY)
    piece = -(-vector.size // (devices * LANES)) * LANES
    padded = jnp.pad(vector, (0, devices * piece - vector.size)).reshape(devices, 1, piece)
    turn_over = partial(lax.all_to_all, axis_name=EVERY, split_axis=0, concat_axis=0, tiled=True)
    own = jnp.sum(turn_over(padded), axis=0, keepdims=True)
    return turn_over(jnp.broadcast_to(own, (devices, 1, piece))).reshape(-1)


def mirrored_rows(shard, core):
    return jnp.stack(quarters(shard, 0, core)).reshape(2, 2, -1, shard.shape[1])


class AlongZ:
    def z_start(self, main, send, keep):
        main, send, keep = tie(main, send, keep)
        self.part = keep, trade(send, "zl")
        return main

    def z_second(self, main):
        keep, arrived = self.part
        main, arrived = tie(main, arrived)
        summed = add_low(keep, arrived).reshape(2, -1, keep.shape[-1])
        here = lax.axis_index("zh")
        send, keep = rows_at(summed, 0, 1 - here), rows_at(summed, 0, here)
        main, send, keep = tie(main, send, keep)
        self.part = keep, trade(send, "zh")
        return main

    def z_done(self, main):
        keep, arrived = self.part
        main, arrived = tie(main, arrived)
        self.part = keep, arrived
        return main


class FourChips:
    def __init__(self, own):
        self.own, self.near = own, trade_mirrored(own, 1)

    def second(self, main):
        main, near = tie(main, self.near)
        across = swap_cores(near)
        half = half_of(across, lax.axis_index("wsh"))
        main, half = tie(main, half)
        self.near, self.across, self.last = near, across, trade_mirrored(half, 1)
        return main

    def third(self, main):
        main, last = tie(main, self.last)
        self.blocks = self.own, self.near, self.across, last, swap_cores(last)
        return main


class FfnGrads(AlongZ):
    def __init__(self, offload):
        self.core, self.places, self.offload = lax.axis_index("wsh"), places_here(), offload

    def hidden_known(self, hidden):
        self.hidden = FourChips(hidden)

    def act_known(self, act):
        self.act = act
        self.act_far = trade_mirrored(half_of(act, 1 - self.places[0], 1), 1)

    def grad_known(self, grad):
        self.grad = FourChips(grad)

    def units_known(self, gate_low, up_low):
        place = self.places[0]
        self.keep = at_place((gate_low, up_low), place)
        self.far = trade_mirrored(at_place((up_low, gate_low), place), 1)

    def hidden_second(self, main):
        return self.hidden.second(main)

    def hidden_third(self, main):
        return self.hidden.third(main)

    def grad_second(self, main):
        return self.grad.second(main)

    def grad_third(self, main):
        return self.grad.third(main)

    def act_second(self, main):
        main, self.act_far = tie(main, self.act_far)
        main, send = tie(main, jnp.concatenate([half_of(self.act, self.places[0], 1), self.act_far], axis=0))
        self.act_last = trade_mirrored(send, 2)
        return main

    def act_in(self, main):
        main, self.act_last = tie(main, self.act_last)
        return main

    def units_in(self, main):
        main, self.last = tie(main, self.last)
        return main

    def units_second(self, main):
        main, self.far = tie(main, self.far)
        other = 1 - self.places[1]
        main, send = tie(main, jnp.concatenate([half_of(self.keep, other, 1), half_of(self.far, other, 1)], axis=0))
        self.last = trade_mirrored(send, 2)
        return main

    def multiply(self, main):
        main, last, act_last = tie(main, self.last, self.act_last)
        sums = ffn_grad_rows(
            self.hidden.blocks,
            self.grad.blocks,
            (self.keep, self.far, last),
            (self.act, self.act_far, act_last),
            self.offload,
        )
        if not self.offload:
            return self.z_start(main, *sums)
        main, sums = tie(main, *sums)
        self.rows = lax.psum_scatter(sums, ("zh", "zl"), scatter_dimension=0, tiled=True)
        return main

    def landed(self, main):
        main, self.rows = tie(main, self.rows)
        return main

    def fix_first(self, main):
        second = self.places[1]
        rows = self.rows if self.offload else add_low(*self.part)
        unit_rows = rows.shape[0] // 3 * 2
        units = jnp.stack(quarters(rows[:unit_rows], 0, self.core)).reshape(2, 2, -1, rows.shape[1])
        main, send = tie(main, rows_at(units, 1, 1 - second))
        self.units, self.downs = rows_at(units, 1, second), rows[unit_rows:].reshape(2, -1, rows.shape[1])
        self.units_far = trade_mirrored(send, 2)
        return main

    def fix_second(self, main):
        first, second = self.places
        main, far = tie(main, self.units_far)
        units = ordered(second, self.units, far)
        self.own, send = (
            jnp.concatenate([rows_at(units, 0, which), rows_at(self.downs, 0, which)], axis=1)
            for which in (first, 1 - first)
        )
        main, send = tie(main, send)
        self.far = trade_mirrored(send, 1)
        return main

    def fix_in(self, main):
        main, self.far = tie(main, self.far)
        return main

    def finish(self):
        first = self.places[0]
        own, far = self.own.astype(F32), self.far.astype(F32)
        columns = own.shape[1] // 3 * 2
        gate = at_place((own[:, :columns], far[:, :columns]), first)
        up = at_place((far[:, :columns], own[:, :columns]), first)
        return gate, up, ordered(first, own[:, columns:], far[:, columns:])


class RowGrads(AlongZ):
    def __init__(self):
        self.lefts = [None, None]

    def left_known(self, index, left):
        self.lefts[index] = left, trade_mirrored(left, 1)

    def rights_known(self, first, second):
        self.cut = first.shape[1]
        right = jnp.concatenate([first, second], axis=1)
        self.rights = right, trade_mirrored(right, 1)

    def first_left_in(self, main):
        main, self.lefts[0] = tie(main, self.lefts[0])
        return main

    def second_left_in(self, main):
        main, self.lefts[1] = tie(main, self.lefts[1])
        return main

    def multiply(self, main):
        main, far, lefts = tie(main, self.rights[1], self.lefts)
        main, (send, keep) = tie(main, row_grad_rows(lefts, (self.rights[0], far), self.cut))
        self.part = keep, trade_mirrored(send, 2)
        return main

    def pair_done(self, main):
        keep, arrived = self.part
        main, arrived = tie(main, arrived)
        summed = add_low(keep, arrived).reshape(2, 2, -1, keep.shape[-1])
        here = lax.axis_index("zl")
        send, keep = (rows_at(summed, 1, which).reshape(-1, keep.shape[-1]) for which in (1 - here, here))
        return self.z_start(main, send, keep)

    def finish(self):
        keep, arrived = self.part
        summed = keep.astype(F32) + arrived.astype(F32)
        return summed[:, : self.cut], summed[:, self.cut :]


def plain_grad(left, right):
    return lax.psum_scatter(product_tn(left, right).astype(BF16), SEQ, scatter_dimension=0, tiled=True).astype(F32)


class PlainFfnGrads:
    def __init__(self, offload):
        pass

    def hidden_known(self, hidden):
        self.hidden = hidden

    def act_known(self, act):
        self.act = act

    def grad_known(self, grad):
        self.grad = grad

    def units_known(self, gate_low, up_low):
        self.units = gate_low, up_low

    def finish(self):
        gate, up = (plain_grad(self.hidden, unit) for unit in self.units)
        return gate, up, plain_grad(self.grad, self.act)


class PlainRowGrads:
    def __init__(self):
        self.lefts = [None, None]

    def left_known(self, index, left):
        self.lefts[index] = left

    def rights_known(self, *rights):
        self.rights = rights

    def finish(self):
        return tuple(plain_grad(left, right) for left, right in zip(self.lefts, self.rights))


def shards(
    tokens,
    doc_start,
    cotangent,
    mix_gain,
    in_proj,
    conv_taps,
    mix_proj,
    ffn_gain_a,
    gate_a,
    up_a,
    down_a,
    attn_gain,
    query_proj,
    key_proj,
    value_proj,
    attn_proj,
    query_gain,
    key_gain,
    ffn_gain_b,
    gate_b,
    up_b,
    down_b,
):
    streams, seq_rows, width = tokens.shape
    core = lax.axis_index("wsh")
    sequences = streams * lax.axis_size("wsh")
    token_count = streams * seq_rows
    head_width = query_gain.shape[0]
    groups = key_proj.shape[1] // head_width
    score_scale = head_width ** (-0.5)
    margin = conv_taps.shape[0] - 1
    half_width = width // 2
    chips = lax.axis_size(SEQ)
    chip = lax.axis_index(SEQ)
    positions = chip * seq_rows + jnp.arange(seq_rows, dtype=jnp.int32)
    paired = all(lax.axis_size(name) == 2 for name in SEQ)
    ffn_kind, rows_kind = (FfnGrads, RowGrads) if paired else (PlainFfnGrads, PlainRowGrads)
    ffn_a, ffn_b, mixer_rows, attn_rows = ffn_kind(True), ffn_kind(True), rows_kind(), rows_kind()

    def step(main, *events):
        if paired:
            for owner, name in events:
                main = getattr(owner, name)(main)
        return main

    frequency = ROPE_BASE ** (-(jnp.arange(0, head_width, 2, dtype=F32) / head_width))
    angles = positions.astype(F32)[:, None] * jnp.tile(frequency, 4)[None, :]
    tables = (jnp.cos(angles), jnp.sin(angles))
    query_gain_row = jnp.tile(query_gain, 2)[None, :]
    key_gain_row = jnp.tile(key_gain, 2)[None, :]

    def split_rows(weight, sent):
        return half_of(weight, core), half_of(swap_cores(sent), core)

    def out_product(left, pieces):
        return ordered(core, product(left, pieces[0]), product(left, pieces[1]))

    def out_product_back(grad, pieces):
        own = half_of(grad, core, 1)
        other = half_of(grad, 1 - core, 1)
        return product_nt(own, pieces[0]) + product_nt(other, pieces[1])

    def sum_cores(partial_rows):
        return half_of(partial_rows, core) + swap_cores(half_of(partial_rows, 1 - core))

    starts_far = swap_cores(doc_start)
    starts_here = jnp.concatenate(
        [jnp.where(core == 0, doc_start, starts_far), jnp.where(core == 0, starts_far, doc_start)], axis=0
    )
    in_far = swap_cores(in_proj)
    in_low, in_high = in_proj[:, :half_width], in_proj[:, 2 * half_width :]
    in_mid = in_far[:, half_width : 2 * half_width]

    grad_out = cotangent.reshape(token_count, width)
    down_low_b = gather_cores(grad_out.astype(BF16))
    flat_tokens = tokens.reshape(token_count, width)
    low_one = gather_cores(norm_rows(flat_tokens, mix_gain).astype(BF16))
    low_one, mix_far, down_a_far = tie(low_one, mix_proj, down_a)
    mix_pieces = split_rows(mix_proj, mix_far)
    down_a_pieces = split_rows(down_a, down_a_far)
    part_low = product(low_one, in_low)
    part_mid = product(low_one, in_mid)
    part_high = product(low_one, in_high)
    factor = jnp.where(core == 0, part_low, part_high)
    c_part = jnp.where(core == 0, part_high, part_low)
    gated = (part_mid * factor).reshape(sequences, seq_rows, half_width)
    edge_rows = lax.ppermute(gated[:, seq_rows - margin :, :], SEQ, [(i, i + 1) for i in range(chips - 1)])
    extended = jnp.concatenate([edge_rows, gated], axis=1)
    taps_here = half_of(conv_taps, core, 1)

    def convolve(extended_rows, taps_now):
        running = jnp.zeros_like(extended_rows[:, margin:])
        for tap_index in range(margin + 1):
            offset = margin - tap_index
            shifted = extended_rows[:, tap_index : tap_index + seq_rows]
            allowed = (positions[None, :] - offset >= starts_here)[:, :, None]
            running = running + jnp.where(allowed, shifted, 0.0) * taps_now[tap_index]
        return running

    mixed_conv = convolve(extended, taps_here).reshape(-1, half_width)
    mixer_low = (c_part * mixed_conv).astype(BF16)
    mixer_rows.left_known(1, low_one)
    resid_one = flat_tokens + sum_cores(out_product(mixer_low, mix_pieces))

    def ffn_units(grads, residual, gain_vec, gate_weight, up_weight):
        hidden_low = gather_cores(norm_rows(residual, gain_vec).astype(BF16))
        grads.hidden_known(hidden_low)
        gate_val = product(hidden_low, gate_weight)
        up_val = product(hidden_low, up_weight)
        act_low = gated_unit(gate_val, up_val).astype(BF16)
        grads.act_known(act_low)
        return gate_val, up_val, act_low

    gate_val_a, up_val_a, act_low_a = ffn_units(ffn_a, resid_one, ffn_gain_a, gate_a, up_a)
    resid_two = resid_one + sum_cores(out_product(act_low_a, down_a_pieces))

    low_three = gather_cores(norm_rows(resid_two, attn_gain).astype(BF16))
    low_three, attn_far, down_b_far = tie(low_three, attn_proj, down_b)
    attn_pieces = split_rows(attn_proj, attn_far)
    down_b_pieces = split_rows(down_b, down_b_far)
    attn_rows.left_known(1, low_three)
    query_raw = product(low_three, query_proj)
    key_raw = product(low_three, key_proj)
    value_raw = product(low_three, value_proj)
    packed = heads_forward(query_raw, key_raw, value_raw, starts_here, tables, query_gain_row, key_gain_row)

    team = SEQ if chips == sequences * groups else ("y", "x")
    rest = () if team == SEQ else ("zh", "zl")
    to_heads = partial(lax.all_to_all, axis_name=team, split_axis=0, concat_axis=0, tiled=True)
    packed = to_heads(packed)
    length = packed.shape[0] * seq_rows
    mixer_whole = gather_cores(mixer_low, 1)
    packed, mixer_whole, down_low_b = tie(packed, mixer_whole, down_low_b)
    packed = step(packed, (ffn_a, "hidden_second"))
    mixer_rows.left_known(0, mixer_whole)
    ffn_b.grad_known(down_low_b)
    kv, kv_block = (lax.all_gather(packed[:, :, LANES:], rest, axis=0, tiled=True), 0) if rest else (packed, 1)
    attended_low, attended_full, logs = attend(packed, kv, kv_block, rest, score_scale)

    def from_heads(block):
        back = to_heads(block.reshape(sequences * groups, seq_rows, -1))
        back = back.reshape(groups, sequences, seq_rows, -1)
        return jnp.transpose(back, (1, 2, 0, 3)).reshape(sequences * seq_rows, -1)

    attended_low = step(attended_low, (ffn_a, "act_second"), (ffn_b, "grad_second"))
    attn_low = from_heads(attended_low)
    grad_act_b = out_product_back(down_low_b, down_b_pieces)
    attn_low, grad_act_b = tie(attn_low, grad_act_b)
    attn_low = step(
        attn_low,
        (ffn_a, "hidden_third"),
        (mixer_rows, "second_left_in"),
    )
    resid_three = resid_two + sum_cores(out_product(attn_low, attn_pieces))
    gate_val_b, up_val_b, act_low_b = ffn_units(ffn_b, resid_three, ffn_gain_b, gate_b, up_b)

    def units_back(gate_val, up_val, grad_act):
        _, pull_unit = jax.vjp(gated_unit, gate_val, up_val)
        grad_gate_val, grad_up_val = pull_unit(grad_act)
        return grad_gate_val.astype(BF16), grad_up_val.astype(BF16)

    def norm_back(residual, gain_vec, partial_grad, grad_after):
        _, pull_norm = jax.vjp(norm_rows, residual, gain_vec)
        grad_resid, grad_gain = pull_norm(sum_cores(partial_grad))
        return grad_after + grad_resid, grad_gain

    gate_low, up_low = units_back(gate_val_b, up_val_b, grad_act_b)
    ffn_b.units_known(gate_low, up_low)
    gate_low = step(gate_low, (ffn_b, "grad_third"), (attn_rows, "second_left_in"), (mixer_rows, "first_left_in"))
    grad_three, grad_gain_b = norm_back(
        resid_three, ffn_gain_b, product_nt(gate_low, gate_b) + product_nt(up_low, up_b), grad_out
    )
    grad_attn_low = gather_cores(grad_three.astype(BF16))
    grad_heads = heads_grad(
        half_of(grad_attn_low, core, 1), half_of(grad_attn_low, 1 - core, 1), attn_pieces, sequences
    )
    grad_heads = to_heads(grad_heads).reshape(length, LANES)
    attn_whole = gather_cores(attn_low, 1)
    grad_heads, attn_whole = tie(grad_heads, attn_whole)
    attn_rows.left_known(0, attn_whole)
    grad_heads = step(
        grad_heads, (ffn_a, "act_in"), (ffn_b, "units_second"), (ffn_b, "act_second"), (ffn_b, "hidden_second")
    )
    query_grads, kv_grads = attend_back(packed, kv, kv_block, rest, grad_heads, attended_full, logs, score_scale)
    if rest:
        kv_grads = lax.psum_scatter(kv_grads, rest, scatter_dimension=0, tiled=True)
    query_grads = step(query_grads, (ffn_b, "units_in"), (ffn_b, "hidden_third"))
    packed_grads = jnp.concatenate([query_grads, kv_grads], axis=1)
    packed_grads = to_heads(packed_grads.reshape(sequences * groups, seq_rows, 2 * LANES))
    packed_grads = step(packed_grads, (ffn_b, "act_in"), (attn_rows, "first_left_in"))
    query_back, key_back, value_back, query_term, key_term = heads_backward(
        packed_grads, query_raw, key_raw, tables, query_gain_row, key_gain_row
    )
    attn_rows.rights_known(
        half_of(grad_attn_low, core, 1), jnp.concatenate([query_back, key_back, value_back], axis=1)
    )
    grad_two, grad_attn_gain = norm_back(
        resid_two,
        attn_gain,
        product_nt(query_back, query_proj) + product_nt(key_back, key_proj) + product_nt(value_back, value_proj),
        grad_three,
    )

    grad_two = step(grad_two, (ffn_b, "multiply"))
    down_low_a = gather_cores(grad_two.astype(BF16))
    gate_low, up_low = units_back(gate_val_a, up_val_a, out_product_back(down_low_a, down_a_pieces))
    ffn_a.units_known(gate_low, up_low)
    gate_low, down_low_a = tie(gate_low, down_low_a)
    ffn_a.grad_known(down_low_a)
    grad_one, grad_gain_a = norm_back(
        resid_one, ffn_gain_a, product_nt(gate_low, gate_a) + product_nt(up_low, up_a), grad_two
    )
    grad_mix_low = gather_cores(grad_one.astype(BF16))
    grad_mixer = out_product_back(grad_mix_low, mix_pieces)
    grad_mixer = step(grad_mixer, (attn_rows, "multiply"), (ffn_a, "units_second"), (ffn_a, "grad_second"))
    grad_c_part = grad_mixer * mixed_conv
    grad_conv = (grad_mixer * c_part).reshape(sequences, seq_rows, half_width)
    _, pull_conv = jax.vjp(convolve, extended, taps_here)
    grad_extended, grad_taps = pull_conv(grad_conv)
    returned = lax.ppermute(grad_extended[:, :margin, :], SEQ, [(i + 1, i) for i in range(chips - 1)])
    grad_gated = grad_extended[:, margin:, :] + jnp.concatenate(
        [jnp.zeros((sequences, seq_rows - margin, half_width), F32), returned], axis=1
    )
    grad_gated = grad_gated.reshape(-1, half_width)
    grad_gated = step(grad_gated, (ffn_a, "units_in"), (ffn_a, "grad_third"), (ffn_a, "multiply"))
    grad_factor = grad_gated * part_mid
    mid_low = (grad_gated * factor).astype(BF16)
    low_low = jnp.where(core == 0, grad_factor, grad_c_part).astype(BF16)
    high_low = jnp.where(core == 0, grad_c_part, grad_factor).astype(BF16)
    mixer_rows.rights_known(
        half_of(grad_mix_low, core, 1), jnp.concatenate([low_low, swap_cores(mid_low), high_low], axis=1)
    )
    low_low = step(low_low, (attn_rows, "pair_done"), (ffn_b, "landed"))
    partial_one = product_nt(low_low, in_low) + product_nt(mid_low, in_mid) + product_nt(high_low, in_high)
    partial_one = step(partial_one, (mixer_rows, "multiply"), (attn_rows, "z_second"))
    grad_tokens, grad_mix_gain = norm_back(flat_tokens, mix_gain, partial_one, grad_one)
    tokens_grad = grad_tokens.reshape(streams, seq_rows, width)
    grad_taps = lax.dynamic_update_slice_in_dim(jnp.zeros_like(conv_taps), grad_taps, core * half_width, 1)
    small = jnp.concatenate(
        [
            grad_mix_gain,
            grad_taps.reshape(-1),
            grad_gain_a,
            grad_attn_gain,
            grad_gain_b,
            query_term[0],
            key_term[0],
        ]
    )
    small = step(small, (ffn_b, "fix_first"), (mixer_rows, "pair_done"), (ffn_b, "fix_second"))
    act_low_b, small = tie(act_low_b, small)
    output = resid_three + sum_cores(out_product(act_low_b, down_b_pieces))
    done_b = ffn_b.finish()

    small = sum_everywhere(small)
    small, output, done_b = tie(small, output, done_b)
    small = step(
        small,
        (ffn_a, "landed"),
        (ffn_a, "fix_first"),
        (mixer_rows, "z_second"),
        (ffn_a, "fix_second"),
        (ffn_a, "fix_in"),
        (attn_rows, "z_done"),
        (mixer_rows, "z_done"),
    )
    taps_end = width + conv_taps.size
    heads_at = taps_end + 3 * width

    def head_gain(offset):
        both = small[offset : offset + LANES]
        return both[:head_width] + both[head_width:]

    gate_a_grad, up_a_grad, down_a_grad = ffn_a.finish()
    gate_b_grad, up_b_grad, down_b_grad = done_b
    mix_grad, proj_grad = mixer_rows.finish()
    attn_grad, qkv_grad = attn_rows.finish()
    query_columns, key_columns = query_proj.shape[1], key_proj.shape[1]
    return (
        output.reshape(streams, seq_rows, width),
        tokens_grad,
        small[:width],
        proj_grad,
        small[width:taps_end].reshape(conv_taps.shape),
        mix_grad,
        small[taps_end : taps_end + width],
        gate_a_grad,
        up_a_grad,
        down_a_grad.T,
        small[taps_end + width : taps_end + 2 * width],
        qkv_grad[:, :query_columns],
        qkv_grad[:, query_columns : query_columns + key_columns],
        qkv_grad[:, query_columns + key_columns :],
        attn_grad,
        head_gain(heads_at),
        head_gain(heads_at + LANES),
        small[taps_end + 2 * width : taps_end + 3 * width],
        gate_b_grad,
        up_b_grad,
        down_b_grad.T,
    )


def chip_grid(chips):
    along_z = math.gcd(4, chips)
    side = math.isqrt(chips // along_z)
    return along_z // 2, 2, chips // along_z // side, side


def solution(mesh):
    cores = mesh.shape["wsh"]
    grid = Mesh(mesh.devices.reshape(*chip_grid(mesh.shape["seq"]), cores), EVERY)
    tokens_spec = P("wsh", SEQ, None)
    columns = P(None, "wsh")
    grads = P(SEQ, "wsh")
    in_specs = (
        tokens_spec,
        P("wsh", SEQ),
        tokens_spec,
        P(),
        columns,
        P(),
        columns,
        P(),
        columns,
        columns,
        columns,
        P(),
        columns,
        columns,
        columns,
        columns,
        P(),
        P(),
        P(),
        columns,
        columns,
        columns,
    )
    out_specs = (
        tokens_spec,
        tokens_spec,
        P(),
        grads,
        P(),
        grads,
        P(),
        grads,
        grads,
        P("wsh", SEQ),
        P(),
        grads,
        grads,
        grads,
        grads,
        P(),
        P(),
        P(),
        grads,
        grads,
        P("wsh", SEQ),
    )
    return jax.shard_map(shards, mesh=grid, in_specs=in_specs, out_specs=out_specs, check_vma=False)
```

```python
from functools import partial
import math

import jax
import jax.numpy as jnp
from jax import lax
from jax.experimental import pallas as pl
from jax.experimental.pallas import tpu as pltpu
from jax.sharding import Mesh, PartitionSpec as P

EPS = 1e-05
ROPE_BASE = 1000000.0
MASKED = -1e30
START_PEAK = -1e25
SEQ = ("zh", "zl", "y", "x")
EVERY = SEQ + ("wsh",)
SWAP = [(0, 1), (1, 0)]
BF16 = jnp.bfloat16
F32 = jnp.float32
LANES = 128


def norm_rows(values, gain_vec):
    return values * lax.rsqrt(jnp.mean(values * values, axis=-1, keepdims=True) + EPS) * gain_vec


def product(left, right):
    return jnp.dot(left, right, preferred_element_type=F32)


def product_tn(left, right):
    return lax.dot_general(left, right, (((0,), (0,)), ((), ())), preferred_element_type=F32)


def product_nt(left, right):
    return lax.dot_general(left, right, (((1,), (1,)), ((), ())), preferred_element_type=F32)


def gated_unit(gate_val, up_val):
    return jax.nn.silu(gate_val) * up_val


def swap_cores(block):
    return lax.ppermute(block, "wsh", SWAP)


def gather_cores(block, axis=0):
    return lax.all_gather(block, "wsh", axis=axis, tiled=True)


def half_of(array, which, axis=0):
    size = array.shape[axis] // 2
    return lax.dynamic_slice_in_dim(array, which * size, size, axis)


def ordered(core, own, other):
    first = jnp.where(core == 0, own, other)
    second = jnp.where(core == 0, other, own)
    return jnp.concatenate([first, second], axis=-1)


def lane_of(shape):
    return lax.broadcasted_iota(jnp.int32, shape, 1)


def two_heads(block):
    return jnp.concatenate([block[:, :64], block[:, 64:]], axis=0)


def side_by_side(block):
    rows = block.shape[0] // 2
    return jnp.concatenate([block[:rows], block[rows:]], axis=1)


EXTRA = 16


def flat(block):
    return block[:, : block.shape[1] - EXTRA].reshape(-1, block.shape[2])


def places(packed_ref, offset):
    chips, padded, _ = packed_ref.shape
    rows = padded - EXTRA
    coded = packed_ref[:, rows, :].astype(F32)
    starts = coded[:, :64] * 64.0 + coded[:, 64:]
    diagonal = lax.broadcasted_iota(jnp.int32, (rows, rows), 0) == lane_of((rows, rows))
    columns = [
        jnp.sum(jnp.where(diagonal, starts[chip : chip + 1], 0.0), axis=1, keepdims=True) for chip in range(chips)
    ]
    starts = jnp.concatenate(columns * 2, axis=0).astype(jnp.int32)
    row = lax.broadcasted_iota(jnp.int32, (2 * chips * rows, 1), 0)
    row = jnp.where(row >= chips * rows, row - chips * rows, row)
    return starts, offset + pl.program_id(0) * chips * rows + row


def first_place(rest, length):
    return lax.axis_index(rest) * length if rest else 0


def lay_out(kv_ref, flat_ref):
    rows = kv_ref.shape[1] - EXTRA

    @pl.when(pl.program_id(0) == 0)
    def _():
        for chip in range(kv_ref.shape[0]):
            flat_ref[chip * rows : (chip + 1) * rows] = kv_ref[chip, :rows]


def attend_kernel(packed_ref, kv_ref, low_ref, full_ref, log_ref, flat_ref, *, rest, span, scale):
    lay_out(kv_ref, flat_ref)
    rows = low_ref.shape[0]
    offset = first_place(rest, rows * pl.num_programs(0))
    query = two_heads(flat(packed_ref[...]))
    starts, mine = places(packed_ref, offset)

    def advance(index, carried):
        peak, total, mixed = carried
        kv_block = flat_ref[pl.ds(pl.multiple_of(index * span, span), span), :]
        scores = product_nt(query, kv_block[:, :64]) * scale
        place = index * span + lane_of((1, span))
        scores = jnp.where((place >= starts) & (place <= mine), scores, MASKED)
        fresh_peak = jnp.maximum(peak, jnp.max(scores, axis=1, keepdims=True))
        shares = jnp.exp(scores - fresh_peak)
        keep = jnp.exp(peak - fresh_peak)
        total = total * keep + jnp.sum(shares, axis=1, keepdims=True)
        mixed = mixed * keep + product(shares.astype(BF16), kv_block[:, 64:])
        return fresh_peak, total, mixed

    last = (offset + (pl.program_id(0) + 1) * rows) // span
    peak, total, mixed = lax.fori_loop(
        0,
        last,
        advance,
        (
            jnp.full((2 * rows, 1), START_PEAK, F32),
            jnp.zeros((2 * rows, 1), F32),
            jnp.zeros((2 * rows, 64), F32),
        ),
    )
    attended = side_by_side(mixed / total)
    low_ref[...] = attended.astype(BF16)
    full_ref[...] = attended
    log_ref[...] = side_by_side(jnp.broadcast_to(peak + jnp.log(total), (2 * rows, 64)))


def attend_back_kernel(packed_ref, kv_ref, grad_ref, full_ref, log_ref, dq_ref, dkv_ref, sums_ref, flat_ref, *, rest, span, scale):
    lay_out(kv_ref, flat_ref)
    rows = grad_ref.shape[0]
    offset = first_place(rest, rows * pl.num_programs(0))
    query = two_heads(flat(packed_ref[...]))
    grad = two_heads(grad_ref[...])
    attended = two_heads(full_ref[...])
    logs = two_heads(log_ref[...])[:, :1]
    delta = jnp.sum(grad.astype(F32) * attended, axis=1, keepdims=True)
    starts, mine = places(packed_ref, offset)

    @pl.when(pl.program_id(0) == 0)
    def _():
        sums_ref[...] = jnp.zeros_like(sums_ref)

    def advance(index, query_grad):
        window = pl.ds(pl.multiple_of(index * span, span), span)
        kv_block = flat_ref[window, :]
        key, value = kv_block[:, :64], kv_block[:, 64:]
        scores = product_nt(query, key) * scale
        place = index * span + lane_of((1, span))
        scores = jnp.where((place >= starts) & (place <= mine), scores, MASKED)
        shares = jnp.exp(scores - logs)
        grad_scores = (shares * (product_nt(grad, value) - delta)).astype(BF16)
        key_grad = product_tn(grad_scores, query) * scale
        value_grad = product_tn(shares.astype(BF16), grad)
        sums_ref[window, :] += jnp.concatenate([key_grad, value_grad], axis=1)
        return query_grad + product(grad_scores, key)

    last = (offset + (pl.program_id(0) + 1) * rows) // span
    query_grad = lax.fori_loop(0, last, advance, jnp.zeros((2 * rows, 64), F32))
    dq_ref[...] = side_by_side(query_grad * scale).astype(BF16)

    @pl.when(pl.program_id(0) == pl.num_programs(0) - 1)
    def _():
        dkv_ref[...] = sums_ref[...].astype(BF16)


def rows_spec(rows, columns, column_block=0):
    return pl.BlockSpec((rows, columns), lambda index: (index, column_block))


def whole_spec(rows, columns, column_block=0):
    return pl.BlockSpec((rows, columns), lambda index: (0, column_block))


def attend_specs(packed, kv, kv_block):
    chips, padded, _ = packed.shape
    per_step = max(1, 256 // (padded - EXTRA))
    packed_spec = pl.BlockSpec((per_step, padded, LANES), lambda index: (index, 0, 0))
    kv_spec = pl.BlockSpec((kv.shape[0], padded, LANES), lambda index: (0, 0, kv_block))
    return chips // per_step, per_step * (padded - EXTRA), [packed_spec, kv_spec]


def attend(packed, kv, kv_block, rest, scale):
    steps, rows, specs = attend_specs(packed, kv, kv_block)
    length, keys = steps * rows, kv.shape[0] * (kv.shape[1] - EXTRA)
    return pl.pallas_call(
        partial(attend_kernel, rest=rest, span=rows, scale=scale),
        grid=(steps,),
        in_specs=specs,
        out_specs=[rows_spec(rows, LANES)] * 3,
        out_shape=[
            jax.ShapeDtypeStruct((length, LANES), BF16),
            jax.ShapeDtypeStruct((length, LANES), F32),
            jax.ShapeDtypeStruct((length, LANES), F32),
        ],
        scratch_shapes=[pltpu.VMEM((keys, LANES), BF16)],
        compiler_params=pltpu.CompilerParams(vmem_limit_bytes=24 << 20),
        cost_estimate=pl.CostEstimate(flops=4 * length * keys * 64, bytes_accessed=2 << 20, transcendentals=length * keys),
    )(packed, kv)


def attend_back(packed, kv, kv_block, rest, grad, full, logs, scale):
    steps, rows, specs = attend_specs(packed, kv, kv_block)
    length, keys = steps * rows, kv.shape[0] * (kv.shape[1] - EXTRA)
    return pl.pallas_call(
        partial(attend_back_kernel, rest=rest, span=rows, scale=scale),
        grid=(steps,),
        in_specs=specs + [rows_spec(rows, LANES)] * 3,
        out_specs=[rows_spec(rows, LANES), whole_spec(keys, LANES)],
        out_shape=[jax.ShapeDtypeStruct((length, LANES), BF16), jax.ShapeDtypeStruct((keys, LANES), BF16)],
        scratch_shapes=[pltpu.VMEM((keys, LANES), F32), pltpu.VMEM((keys, LANES), BF16)],
        compiler_params=pltpu.CompilerParams(vmem_limit_bytes=24 << 20),
        cost_estimate=pl.CostEstimate(flops=10 * length * keys * 64, bytes_accessed=3 << 20, transcendentals=length * keys),
    )(packed, kv, grad, full, logs)


def causal_blocks(packed_ref, scale):
    chips, padded, _ = packed_ref.shape
    rows = padded - EXTRA
    per_block = 256 // rows
    blocks = []
    for first in range(0, chips, per_block):
        packed = packed_ref[first : first + per_block]
        whole = flat(packed)
        coded = packed[:, rows, :LANES].astype(F32)
        starts = coded[:, :64] * 64.0 + coded[:, 64:]
        starts = jnp.concatenate([starts[chip : chip + 1] for chip in range(per_block)] * 2, axis=1)
        place = lane_of((1, 512)) % 256 + first * rows
        query = two_heads(whole[:, :LANES])
        query = (query.astype(F32) * scale).astype(BF16)
        blocks.append((query, whole[:, 128:192], whole[:, 192:], starts.astype(jnp.int32), place))
    return blocks


def causal_shares(blocks, index):
    query, _, _, starts, mine = blocks[index]
    scores = []
    for other in range(index + 1):
        key = blocks[other][1]
        place = lax.broadcasted_iota(jnp.int32, (256, 1), 0) + other * 256
        allowed = place >= starts
        if other == index:
            allowed = allowed & (place <= mine)
        scores.append(jnp.where(allowed, product_nt(key, query), MASKED))
    peak = jnp.max(scores[0], axis=0, keepdims=True)
    for block in scores[1:]:
        peak = jnp.maximum(peak, jnp.max(block, axis=0, keepdims=True))
    shares = [jnp.exp(block - peak) for block in scores]
    total = sum(jnp.sum(block, axis=0, keepdims=True) for block in shares)
    return shares, 1.0 / total


def causal_kernel(packed_ref, low_ref, *, scale):
    blocks = causal_blocks(packed_ref, scale)
    for index in range(len(blocks)):
        shares, inverse = causal_shares(blocks, index)
        mixed = 0.0
        for other, block in enumerate(shares):
            mixed = mixed + product_tn(blocks[other][2], block.astype(BF16))
        attended = (mixed * inverse).T
        low_ref[index * 256 : (index + 1) * 256] = side_by_side(attended).astype(BF16)


def causal_back_kernel(packed_ref, grad_ref, dq_ref, dkv_ref, sums_ref, *, scale):
    blocks = causal_blocks(packed_ref, scale)
    for index in range(len(blocks)):
        here = slice(index * 256, (index + 1) * 256)
        query = blocks[index][0]
        grad = two_heads(grad_ref[here])
        shares, inverse = causal_shares(blocks, index)
        shares = [block * inverse for block in shares]
        grad_shares = [product_nt(blocks[other][2], grad) for other in range(index + 1)]
        delta = sum(
            jnp.sum(share * grad_share, axis=0, keepdims=True) for share, grad_share in zip(shares, grad_shares)
        )
        query_grad = 0.0
        for other, (share, grad_share) in enumerate(zip(shares, grad_shares)):
            grad_scores = (share * (grad_share - delta)).astype(BF16)
            query_grad = query_grad + product_tn(blocks[other][1], grad_scores)
            parts = jnp.concatenate([product(grad_scores, query), product(share.astype(BF16), grad)], axis=1)
            there = slice(other * 256, (other + 1) * 256)
            if other == index:
                sums_ref[there] = parts
            else:
                sums_ref[there] += parts
        dq_ref[here] = side_by_side((query_grad * scale).T).astype(BF16)
    dkv_ref[...] = sums_ref[...].astype(BF16)


def causal(packed, scale):
    length = packed.shape[0] * (packed.shape[1] - EXTRA)
    return pl.pallas_call(
        partial(causal_kernel, scale=scale),
        out_shape=jax.ShapeDtypeStruct((length, LANES), BF16),
        compiler_params=pltpu.CompilerParams(vmem_limit_bytes=32 << 20),
        cost_estimate=pl.CostEstimate(flops=2 * length * length * 128, bytes_accessed=2 << 20, transcendentals=length * length),
    )(packed)


def causal_back(packed, grad, scale):
    length = grad.shape[0]
    return pl.pallas_call(
        partial(causal_back_kernel, scale=scale),
        out_shape=[jax.ShapeDtypeStruct((length, LANES), BF16)] * 2,
        scratch_shapes=[pltpu.VMEM((length, LANES), F32)],
        compiler_params=pltpu.CompilerParams(vmem_limit_bytes=32 << 20),
        cost_estimate=pl.CostEstimate(flops=5 * length * length * 128, bytes_accessed=3 << 20, transcendentals=length * length),
    )(packed, grad)


def heads_grad_kernel(own_ref, other_ref, own_piece_ref, other_piece_ref, out_ref):
    sums = product_nt(own_ref[...], own_piece_ref[...]) + product_nt(other_ref[...], other_piece_ref[...])
    out_ref[...] = sums.astype(BF16).reshape(out_ref.shape)


def heads_grad(own, other, pieces, sequences):
    tokens, columns = own.shape
    groups = pieces[0].shape[0] // LANES
    piece_spec = pl.BlockSpec((LANES, columns), lambda index: (index, 0))
    rows = tokens // sequences
    return pl.pallas_call(
        heads_grad_kernel,
        grid=(groups,),
        in_specs=[whole_spec(tokens, columns)] * 2 + [piece_spec] * 2,
        out_specs=pl.BlockSpec((sequences, rows, LANES), lambda index: (index, 0, 0)),
        out_shape=jax.ShapeDtypeStruct((groups * sequences, rows, LANES), BF16),
        compiler_params=pltpu.CompilerParams(vmem_limit_bytes=16 << 20),
    )(own, other, *pieces)


def head_means(values):
    low_lanes = lane_of(values.shape) < 64
    low_mean = jnp.sum(jnp.where(low_lanes, values, 0.0), axis=1, keepdims=True) * (1.0 / 64)
    high_mean = jnp.sum(jnp.where(low_lanes, 0.0, values), axis=1, keepdims=True) * (1.0 / 64)
    return jnp.where(low_lanes, low_mean, high_mean)


def turn(values, sign):
    lower = (lane_of(values.shape) % 64) < 32
    return jnp.where(lower, -sign * pltpu.roll(values, LANES - 32, 1), sign * pltpu.roll(values, 32, 1))


def head_forward(raw, gain, cosine, sine):
    unit = raw * lax.rsqrt(head_means(raw * raw) + EPS) * gain
    return (unit * cosine + turn(unit, 1.0) * sine).astype(BF16)


def head_backward(raw, gain, cosine, sine, grad):
    back = grad * cosine + turn(grad * sine, -1.0)
    scale = lax.rsqrt(head_means(raw * raw) + EPS)
    gain_term = jnp.sum(back * raw * scale, axis=0, keepdims=True)
    back = back * gain
    raw_grad = back * scale - raw * (scale * scale * scale) * head_means(back * raw)
    return raw_grad.astype(BF16), gain_term


def heads_kernel(query_ref, key_ref, value_ref, starts_ref, cos_ref, sin_ref, query_gain_ref, key_gain_ref, out_ref):
    rows = out_ref.shape[1] - EXTRA
    groups = key_ref.shape[1] // 64
    sequences = query_ref.shape[0] // rows
    cosine, sine = cos_ref[...], sin_ref[...]
    for place in range(sequences):
        span = pl.ds(place * rows, rows)
        starts = jnp.broadcast_to(starts_ref[place : place + 1], (EXTRA, LANES)).astype(BF16)
        for pair in range(groups // 2):
            lanes = pl.ds(pair * LANES, LANES)
            key = head_forward(key_ref[span, lanes], key_gain_ref[...], cosine, sine)
            value = value_ref[span, lanes].astype(BF16)
            for side in range(2):
                group = 2 * pair + side
                query = head_forward(
                    query_ref[span, pl.ds(group * LANES, LANES)], query_gain_ref[...], cosine, sine
                )
                half = slice(64 * side, 64 * side + 64)
                block = group * sequences + place
                out_ref[block, :rows, 0:LANES] = query
                out_ref[block, :rows, LANES : 2 * LANES] = jnp.concatenate([key[:, half], value[:, half]], axis=1)
                out_ref[block, rows:, 0:LANES] = starts
                out_ref[block, rows:, LANES : 2 * LANES] = starts


def heads_back_kernel(
    grad_ref,
    query_ref,
    key_ref,
    cos_ref,
    sin_ref,
    query_gain_ref,
    key_gain_ref,
    dq_ref,
    dk_ref,
    dv_ref,
    query_term_ref,
    key_term_ref,
):
    rows = grad_ref.shape[1]
    groups = key_ref.shape[1] // 64
    sequences = query_ref.shape[0] // rows
    cosine, sine = cos_ref[...], sin_ref[...]
    query_term = jnp.zeros((1, LANES), F32)
    key_term = jnp.zeros((1, LANES), F32)
    for place in range(sequences):
        span = pl.ds(place * rows, rows)
        for pair in range(groups // 2):
            lanes = pl.ds(pair * LANES, LANES)
            sides = [grad_ref[(2 * pair + side) * sequences + place, :, LANES : 2 * LANES] for side in range(2)]
            key_grad = jnp.concatenate([sides[0][:, :64], sides[1][:, :64]], axis=1).astype(F32)
            dv_ref[span, lanes] = jnp.concatenate([sides[0][:, 64:], sides[1][:, 64:]], axis=1)
            low, term = head_backward(key_ref[span, lanes], key_gain_ref[...], cosine, sine, key_grad)
            dk_ref[span, lanes] = low
            key_term = key_term + term
            for side in range(2):
                group = 2 * pair + side
                wide = pl.ds(group * LANES, LANES)
                query_grad = grad_ref[group * sequences + place, :, 0:LANES].astype(F32)
                low, term = head_backward(query_ref[span, wide], query_gain_ref[...], cosine, sine, query_grad)
                dq_ref[span, wide] = low
                query_term = query_term + term
    query_term_ref[...] = query_term
    key_term_ref[...] = key_term


def heads_forward(query, key, value, starts, tables, query_gain, key_gain):
    rows = starts.shape[1]
    blocks = starts.shape[0] * (key.shape[1] // 64)
    coded = jnp.concatenate([starts // 64, starts % 64], axis=1).astype(F32)
    return pl.pallas_call(
        heads_kernel,
        out_shape=jax.ShapeDtypeStruct((blocks, rows + EXTRA, 2 * LANES), BF16),
        compiler_params=pltpu.CompilerParams(vmem_limit_bytes=32 << 20),
    )(query, key, value, coded, *tables, query_gain, key_gain)


def heads_backward(grad, query, key, tables, query_gain, key_gain):
    return pl.pallas_call(
        heads_back_kernel,
        out_shape=[
            jax.ShapeDtypeStruct(query.shape, BF16),
            jax.ShapeDtypeStruct(key.shape, BF16),
            jax.ShapeDtypeStruct(key.shape, BF16),
            jax.ShapeDtypeStruct((1, LANES), F32),
            jax.ShapeDtypeStruct((1, LANES), F32),
        ],
        compiler_params=pltpu.CompilerParams(vmem_limit_bytes=32 << 20),
    )(grad, query, key, *tables, query_gain, key_gain)


def at_place(pieces, place):
    return jnp.where(place == 0, pieces[0], pieces[1])


def quarters(block, dim, core):
    size = block.shape[dim] // 4
    pieces = [lax.slice_in_dim(block, index * size, (index + 1) * size, axis=dim) for index in range(4)]
    return [
        pieces[0],
        jnp.where(core == 0, pieces[2], pieces[1]),
        jnp.where(core == 0, pieces[1], pieces[2]),
        pieces[3],
    ]


def places_here():
    core, x, y = lax.axis_index("wsh"), lax.axis_index("x"), lax.axis_index("y")
    return jnp.where(core == 0, x, y), jnp.where(core == 0, y, x)


def ffn_grad_kernel(meta_ref, *refs):
    hidden, grads = refs[:5], refs[5:10]
    keep_ref, far_ref, last_ref, act_ref, act_far_ref, act_last_ref = refs[10:16]
    outs = refs[16:]
    rows = keep_ref.shape[0]
    core, place = lax.axis_index("wsh"), places_here()[1]

    def tokens_of(left_refs):
        own, near, across, last, last_far = (left_ref[...] for left_ref in left_refs)
        halves = jnp.where(core == 0, last, last_far), jnp.where(core == 0, last_far, last)
        return own, near, across, jnp.concatenate(halves, axis=0)

    def lanes(block):
        pieces = quarters(block, 1, core)
        return jnp.concatenate([at_place(pieces[:2], place), at_place(pieces[2:], place)], axis=1)

    def total(lefts, own_ref, near_ref, pair_ref):
        sums = product_tn(lefts[0], own_ref[...]) + product_tn(lefts[1], near_ref[...])
        return sums + product_tn(lefts[2], pair_ref[:rows]) + product_tn(lefts[3], pair_ref[rows:])

    units = total(tokens_of(hidden), keep_ref, far_ref, last_ref).astype(BF16)
    downs = total([lanes(block) for block in tokens_of(grads)], act_ref, act_far_ref, act_last_ref).astype(BF16)
    unit_rows = units.shape[0]
    step, steps = pl.program_id(0), pl.num_programs(0)

    for place, out_ref in enumerate(outs):

        @pl.when(step * len(outs) // steps == place)
        def _(out_ref=out_ref):
            out_ref[:unit_rows] = units
            out_ref[unit_rows:] = downs


def ffn_grad_rows(hidden, grads, units, acts, whole):
    first, second = places_here()
    zl = lax.axis_index("zl")
    tokens, width = hidden[0].shape
    columns = units[2].shape[1]
    order = (0, 1, 2, 3) if whole else (1 - zl, 3 - zl, zl, 2 + zl)
    meta = jnp.stack([jnp.asarray(value, jnp.int32) for value in (*order, second, first)])

    def left_spec(block):
        return pl.BlockSpec((block.shape[0], width // 4), lambda index, meta_ref: (0, meta_ref[index]))

    def half_spec(position):
        return pl.BlockSpec((tokens, columns), lambda index, meta_ref: (0, meta_ref[position]))

    def full_spec(rows):
        return pl.BlockSpec((rows, columns), lambda index, meta_ref: (0, 0))

    out_rows = width // 4 + width // 8
    outs = 1 if whole else 2
    steps = 4 // outs

    def out_spec(place):
        return pl.BlockSpec((out_rows, columns), lambda index, meta_ref: (jnp.clip(index - place * steps, 0, steps - 1), 0))

    return pl.pallas_call(
        ffn_grad_kernel,
        grid_spec=pltpu.PrefetchScalarGridSpec(
            num_scalar_prefetch=1,
            grid=(4,),
            in_specs=[left_spec(block) for block in (*hidden, *grads)]
            + [half_spec(4), half_spec(4), full_spec(2 * tokens), half_spec(5), full_spec(tokens), full_spec(2 * tokens)],
            out_specs=[out_spec(place) for place in range(outs)],
        ),
        out_shape=[jax.ShapeDtypeStruct((steps * out_rows, columns), BF16)] * outs,
        compiler_params=pltpu.CompilerParams(vmem_limit_bytes=58 << 20),
        cost_estimate=pl.CostEstimate(
            flops=8 * tokens * 4 * out_rows * columns, bytes_accessed=14 << 20, transcendentals=0
        ),
    )(meta, *hidden, *grads, *units, *acts)


def row_kernel(a_ref, a_far_ref, b_ref, b_far_ref, right_ref, right_far_ref, send_ref, keep_ref, *, cut):
    core, (first, second) = lax.axis_index("wsh"), places_here()
    for left_ref, left_far_ref, span in ((a_ref, a_far_ref, slice(0, cut)), (b_ref, b_far_ref, slice(cut, None))):
        sums = product_tn(left_ref[...], right_ref[:, span]) + product_tn(left_far_ref[...], right_far_ref[:, span])
        pieces = quarters(sums, 0, core)
        pieces = [at_place(pieces[0::2], first), at_place(pieces[1::2], first)]
        keep_ref[:, span] = at_place(pieces, second).astype(BF16)
        send_ref[:, span] = at_place(pieces[::-1], second).astype(BF16)


def row_grad_rows(lefts, rights, cut):
    (a, a_far), (b, b_far) = lefts
    tokens, width = a.shape
    columns = rights[0].shape[1]
    out_rows = width // 16
    left_spec = pl.BlockSpec((tokens, width // 4), lambda index: (0, index))
    return pl.pallas_call(
        partial(row_kernel, cut=cut),
        grid=(4,),
        in_specs=[left_spec] * 4 + [whole_spec(tokens, columns)] * 2,
        out_specs=[rows_spec(out_rows, columns)] * 2,
        out_shape=[jax.ShapeDtypeStruct((4 * out_rows, columns), BF16)] * 2,
        compiler_params=pltpu.CompilerParams(vmem_limit_bytes=20 << 20),
        cost_estimate=pl.CostEstimate(flops=4 * tokens * width * columns, bytes_accessed=6 << 20, transcendentals=0),
    )(a, a_far, b, b_far, *rights)


def trade(block, axis):
    return lax.ppermute(block, axis, SWAP)


def trade_mirrored(block, stage):
    route = []
    for index in range(32):
        along_x = (index % 2 == 0) == (stage == 1)
        route.append((index, index ^ (2 if along_x else 4)))
    return lax.ppermute(block, EVERY, route)


def rows_at(blocks, axis, which):
    return lax.dynamic_index_in_dim(blocks, which, axis, keepdims=False)


def add_low(kept, arrived):
    return (kept.astype(F32) + arrived.astype(F32)).astype(BF16)


def tie(*values):
    return lax.optimization_barrier(values)


def sum_everywhere(vector, between):
    devices = lax.axis_size(EVERY)
    piece = -(-vector.size // (devices * LANES)) * LANES
    padded = jnp.pad(vector, (0, devices * piece - vector.size)).reshape(devices, 1, piece)
    turn_over = partial(lax.all_to_all, axis_name=EVERY, split_axis=0, concat_axis=0, tiled=True)
    own = between(jnp.sum(turn_over(padded), axis=0, keepdims=True))
    return turn_over(jnp.broadcast_to(own, (devices, 1, piece))).reshape(-1)


def mirrored_rows(shard, core):
    return jnp.stack(quarters(shard, 0, core)).reshape(2, 2, -1, shard.shape[1])


class AlongZ:
    def z_start(self, main, send, keep):
        main, send, keep = tie(main, send, keep)
        self.part = keep, trade(send, "zl")
        return main

    def z_second(self, main):
        keep, arrived = self.part
        main, arrived = tie(main, arrived)
        summed = add_low(keep, arrived).reshape(2, -1, keep.shape[-1])
        here = lax.axis_index("zh")
        send, keep = rows_at(summed, 0, 1 - here), rows_at(summed, 0, here)
        main, send, keep = tie(main, send, keep)
        self.part = keep, trade(send, "zh")
        return main

    def z_done(self, main):
        keep, arrived = self.part
        main, arrived = tie(main, arrived)
        self.part = keep, arrived
        return main


class FourChips:
    def __init__(self, own):
        self.own, self.near = own, trade_mirrored(own, 1)

    def second(self, main):
        main, near = tie(main, self.near)
        across = swap_cores(near)
        half = half_of(across, lax.axis_index("wsh"))
        main, half = tie(main, half)
        self.near, self.across, self.last = near, across, trade_mirrored(half, 1)
        return main

    def third(self, main):
        main, last = tie(main, self.last)
        self.blocks = self.own, self.near, self.across, last, swap_cores(last)
        return main


class FfnGrads(AlongZ):
    def __init__(self, offload):
        self.core, self.places, self.offload = lax.axis_index("wsh"), places_here(), offload

    def hidden_known(self, hidden):
        self.hidden = FourChips(hidden)

    def act_known(self, act):
        self.act = act
        self.act_far = trade_mirrored(half_of(act, 1 - self.places[0], 1), 1)

    def grad_known(self, grad):
        self.grad = FourChips(grad)

    def units_known(self, gate_low, up_low):
        place = self.places[0]
        self.keep = at_place((gate_low, up_low), place)
        self.far = trade_mirrored(at_place((up_low, gate_low), place), 1)

    def hidden_second(self, main):
        return self.hidden.second(main)

    def hidden_third(self, main):
        return self.hidden.third(main)

    def grad_second(self, main):
        return self.grad.second(main)

    def grad_third(self, main):
        return self.grad.third(main)

    def act_second(self, main):
        main, self.act_far = tie(main, self.act_far)
        main, send = tie(main, jnp.concatenate([half_of(self.act, self.places[0], 1), self.act_far], axis=0))
        self.act_last = trade_mirrored(send, 2)
        return main

    def act_in(self, main):
        main, self.act_last = tie(main, self.act_last)
        return main

    def units_in(self, main):
        main, self.last = tie(main, self.last)
        return main

    def units_second(self, main):
        main, self.far = tie(main, self.far)
        other = 1 - self.places[1]
        main, send = tie(main, jnp.concatenate([half_of(self.keep, other, 1), half_of(self.far, other, 1)], axis=0))
        self.last = trade_mirrored(send, 2)
        return main

    def multiply(self, main):
        main, last, act_last = tie(main, self.last, self.act_last)
        sums = ffn_grad_rows(
            self.hidden.blocks,
            self.grad.blocks,
            (self.keep, self.far, last),
            (self.act, self.act_far, act_last),
            self.offload,
        )
        if not self.offload:
            return self.z_start(main, *sums)
        main, sums = tie(main, *sums)
        self.rows = lax.psum_scatter(sums, ("zh", "zl"), scatter_dimension=0, tiled=True)
        return main

    def landed(self, main):
        main, self.rows = tie(main, self.rows)
        return main

    def fix_first(self, main):
        second = self.places[1]
        rows = self.rows if self.offload else add_low(*self.part)
        unit_rows = rows.shape[0] // 3 * 2
        units = jnp.stack(quarters(rows[:unit_rows], 0, self.core)).reshape(2, 2, -1, rows.shape[1])
        main, send = tie(main, rows_at(units, 1, 1 - second))
        self.units, self.downs = rows_at(units, 1, second), rows[unit_rows:].reshape(2, -1, rows.shape[1])
        self.units_far = trade_mirrored(send, 2)
        return main

    def fix_second(self, main):
        first, second = self.places
        main, far = tie(main, self.units_far)
        units = ordered(second, self.units, far)
        self.own, send = (
            jnp.concatenate([rows_at(units, 0, which), rows_at(self.downs, 0, which)], axis=1)
            for which in (first, 1 - first)
        )
        main, send = tie(main, send)
        self.far = trade_mirrored(send, 1)
        return main

    def fix_in(self, main):
        main, self.far = tie(main, self.far)
        return main

    def finish(self):
        first = self.places[0]
        own, far = self.own.astype(F32), self.far.astype(F32)
        columns = own.shape[1] // 3 * 2
        gate = at_place((own[:, :columns], far[:, :columns]), first)
        up = at_place((far[:, :columns], own[:, :columns]), first)
        return gate, up, ordered(first, own[:, columns:], far[:, columns:])


class RowGrads(AlongZ):
    def __init__(self):
        self.lefts = [None, None]

    def left_known(self, index, left):
        self.lefts[index] = left, trade_mirrored(left, 1)

    def rights_known(self, first, second):
        self.cut = first.shape[1]
        right = jnp.concatenate([first, second], axis=1)
        self.rights = right, trade_mirrored(right, 1)

    def first_left_in(self, main):
        main, self.lefts[0] = tie(main, self.lefts[0])
        return main

    def second_left_in(self, main):
        main, self.lefts[1] = tie(main, self.lefts[1])
        return main

    def multiply(self, main):
        main, far, lefts = tie(main, self.rights[1], self.lefts)
        main, (send, keep) = tie(main, row_grad_rows(lefts, (self.rights[0], far), self.cut))
        self.part = keep, trade_mirrored(send, 2)
        return main

    def pair_done(self, main):
        keep, arrived = self.part
        main, arrived = tie(main, arrived)
        summed = add_low(keep, arrived).reshape(2, 2, -1, keep.shape[-1])
        here = lax.axis_index("zl")
        send, keep = (rows_at(summed, 1, which).reshape(-1, keep.shape[-1]) for which in (1 - here, here))
        return self.z_start(main, send, keep)

    def finish(self):
        keep, arrived = self.part
        summed = keep.astype(F32) + arrived.astype(F32)
        return summed[:, : self.cut], summed[:, self.cut :]


def plain_grad(left, right):
    return lax.psum_scatter(product_tn(left, right).astype(BF16), SEQ, scatter_dimension=0, tiled=True).astype(F32)


class PlainFfnGrads:
    def __init__(self, offload):
        pass

    def hidden_known(self, hidden):
        self.hidden = hidden

    def act_known(self, act):
        self.act = act

    def grad_known(self, grad):
        self.grad = grad

    def units_known(self, gate_low, up_low):
        self.units = gate_low, up_low

    def finish(self):
        gate, up = (plain_grad(self.hidden, unit) for unit in self.units)
        return gate, up, plain_grad(self.grad, self.act)


class PlainRowGrads:
    def __init__(self):
        self.lefts = [None, None]

    def left_known(self, index, left):
        self.lefts[index] = left

    def rights_known(self, *rights):
        self.rights = rights

    def finish(self):
        return tuple(plain_grad(left, right) for left, right in zip(self.lefts, self.rights))


def shards(
    tokens,
    doc_start,
    cotangent,
    mix_gain,
    in_proj,
    conv_taps,
    mix_proj,
    ffn_gain_a,
    gate_a,
    up_a,
    down_a,
    attn_gain,
    query_proj,
    key_proj,
    value_proj,
    attn_proj,
    query_gain,
    key_gain,
    ffn_gain_b,
    gate_b,
    up_b,
    down_b,
):
    streams, seq_rows, width = tokens.shape
    core = lax.axis_index("wsh")
    sequences = streams * lax.axis_size("wsh")
    token_count = streams * seq_rows
    head_width = query_gain.shape[0]
    groups = key_proj.shape[1] // head_width
    score_scale = head_width ** (-0.5)
    margin = conv_taps.shape[0] - 1
    half_width = width // 2
    chips = lax.axis_size(SEQ)
    chip = lax.axis_index(SEQ)
    positions = chip * seq_rows + jnp.arange(seq_rows, dtype=jnp.int32)
    paired = all(lax.axis_size(name) == 2 for name in SEQ)
    ffn_kind, rows_kind = (FfnGrads, RowGrads) if paired else (PlainFfnGrads, PlainRowGrads)
    ffn_a, ffn_b, mixer_rows, attn_rows = ffn_kind(True), ffn_kind(True), rows_kind(), rows_kind()

    def step(main, *events):
        if paired:
            for owner, name in events:
                main = getattr(owner, name)(main)
        return main

    frequency = ROPE_BASE ** (-(jnp.arange(0, head_width, 2, dtype=F32) / head_width))
    angles = positions.astype(F32)[:, None] * jnp.tile(frequency, 4)[None, :]
    tables = (jnp.cos(angles), jnp.sin(angles))
    query_gain_row = jnp.tile(query_gain, 2)[None, :]
    key_gain_row = jnp.tile(key_gain, 2)[None, :]

    def split_rows(weight, sent):
        return half_of(weight, core), half_of(swap_cores(sent), core)

    def out_product(left, pieces):
        return ordered(core, product(left, pieces[0]), product(left, pieces[1]))

    def out_product_back(grad, pieces):
        own = half_of(grad, core, 1)
        other = half_of(grad, 1 - core, 1)
        return product_nt(own, pieces[0]) + product_nt(other, pieces[1])

    def sum_cores(partial_rows):
        return half_of(partial_rows, core) + swap_cores(half_of(partial_rows, 1 - core))

    starts_far = swap_cores(doc_start)
    starts_here = jnp.concatenate(
        [jnp.where(core == 0, doc_start, starts_far), jnp.where(core == 0, starts_far, doc_start)], axis=0
    )
    in_far = swap_cores(in_proj)
    in_low, in_high = in_proj[:, :half_width], in_proj[:, 2 * half_width :]
    in_mid = in_far[:, half_width : 2 * half_width]

    grad_out = cotangent.reshape(token_count, width)
    down_low_b = gather_cores(grad_out.astype(BF16))
    flat_tokens = tokens.reshape(token_count, width)
    low_one = gather_cores(norm_rows(flat_tokens, mix_gain).astype(BF16))
    low_one, mix_far, down_a_far = tie(low_one, mix_proj, down_a)
    mix_pieces = split_rows(mix_proj, mix_far)
    down_a_pieces = split_rows(down_a, down_a_far)
    part_low = product(low_one, in_low)
    part_mid = product(low_one, in_mid)
    part_high = product(low_one, in_high)
    factor = jnp.where(core == 0, part_low, part_high)
    c_part = jnp.where(core == 0, part_high, part_low)
    gated = (part_mid * factor).reshape(sequences, seq_rows, half_width)
    edge_rows = lax.ppermute(gated[:, seq_rows - margin :, :], SEQ, [(i, i + 1) for i in range(chips - 1)])
    extended = jnp.concatenate([edge_rows, gated], axis=1)
    taps_here = half_of(conv_taps, core, 1)

    def convolve(extended_rows, taps_now):
        running = jnp.zeros_like(extended_rows[:, margin:])
        for tap_index in range(margin + 1):
            offset = margin - tap_index
            shifted = extended_rows[:, tap_index : tap_index + seq_rows]
            allowed = (positions[None, :] - offset >= starts_here)[:, :, None]
            running = running + jnp.where(allowed, shifted, 0.0) * taps_now[tap_index]
        return running

    mixed_conv = convolve(extended, taps_here).reshape(-1, half_width)
    mixer_low = (c_part * mixed_conv).astype(BF16)
    mixer_rows.left_known(1, low_one)
    resid_one = flat_tokens + sum_cores(out_product(mixer_low, mix_pieces))

    def ffn_units(grads, residual, gain_vec, gate_weight, up_weight):
        hidden_low = gather_cores(norm_rows(residual, gain_vec).astype(BF16))
        grads.hidden_known(hidden_low)
        gate_val = product(hidden_low, gate_weight)
        up_val = product(hidden_low, up_weight)
        act_low = gated_unit(gate_val, up_val).astype(BF16)
        grads.act_known(act_low)
        return gate_val, up_val, act_low

    gate_val_a, up_val_a, act_low_a = ffn_units(ffn_a, resid_one, ffn_gain_a, gate_a, up_a)
    resid_two = resid_one + sum_cores(out_product(act_low_a, down_a_pieces))

    low_three = gather_cores(norm_rows(resid_two, attn_gain).astype(BF16))
    low_three, attn_far, down_b_far = tie(low_three, attn_proj, down_b)
    attn_pieces = split_rows(attn_proj, attn_far)
    down_b_pieces = split_rows(down_b, down_b_far)
    attn_rows.left_known(1, low_three)
    query_raw = product(low_three, query_proj)
    key_raw = product(low_three, key_proj)
    value_raw = product(low_three, value_proj)
    packed = heads_forward(query_raw, key_raw, value_raw, starts_here, tables, query_gain_row, key_gain_row)

    team = SEQ if chips == sequences * groups else ("y", "x")
    rest = () if team == SEQ else ("zh", "zl")
    to_heads = partial(lax.all_to_all, axis_name=team, split_axis=0, concat_axis=0, tiled=True)
    packed = to_heads(packed)
    length = packed.shape[0] * seq_rows
    mixer_whole = gather_cores(mixer_low, 1)
    packed, mixer_whole, down_low_b = tie(packed, mixer_whole, down_low_b)
    packed = step(packed, (ffn_a, "hidden_second"))
    mixer_rows.left_known(0, mixer_whole)
    ffn_b.grad_known(down_low_b)
    if rest:
        kv = lax.all_gather(packed[:, :, LANES:], rest, axis=0, tiled=True)
        attended_low, attended_full, logs = attend(packed, kv, 0, rest, score_scale)
    else:
        attended_low = causal(packed, score_scale)

    def from_heads(block):
        back = to_heads(block.reshape(sequences * groups, seq_rows, -1))
        back = back.reshape(groups, sequences, seq_rows, -1)
        return jnp.transpose(back, (1, 2, 0, 3)).reshape(sequences * seq_rows, -1)

    attended_low = step(attended_low, (ffn_a, "act_second"), (ffn_b, "grad_second"))
    attn_low = from_heads(attended_low)
    grad_act_b = out_product_back(down_low_b, down_b_pieces)
    attn_low, grad_act_b = tie(attn_low, grad_act_b)
    attn_low = step(
        attn_low,
        (ffn_a, "hidden_third"),
        (mixer_rows, "second_left_in"),
    )
    resid_three = resid_two + sum_cores(out_product(attn_low, attn_pieces))
    gate_val_b, up_val_b, act_low_b = ffn_units(ffn_b, resid_three, ffn_gain_b, gate_b, up_b)

    def units_back(gate_val, up_val, grad_act):
        _, pull_unit = jax.vjp(gated_unit, gate_val, up_val)
        grad_gate_val, grad_up_val = pull_unit(grad_act)
        return grad_gate_val.astype(BF16), grad_up_val.astype(BF16)

    def norm_back(residual, gain_vec, partial_grad, grad_after):
        _, pull_norm = jax.vjp(norm_rows, residual, gain_vec)
        grad_resid, grad_gain = pull_norm(sum_cores(partial_grad))
        return grad_after + grad_resid, grad_gain

    gate_low, up_low = units_back(gate_val_b, up_val_b, grad_act_b)
    ffn_b.units_known(gate_low, up_low)
    gate_low = step(gate_low, (attn_rows, "second_left_in"), (mixer_rows, "first_left_in"))
    grad_three, grad_gain_b = norm_back(
        resid_three, ffn_gain_b, product_nt(gate_low, gate_b) + product_nt(up_low, up_b), grad_out
    )
    grad_attn_low = gather_cores(grad_three.astype(BF16))
    grad_heads = heads_grad(
        half_of(grad_attn_low, core, 1), half_of(grad_attn_low, 1 - core, 1), attn_pieces, sequences
    )
    grad_heads = to_heads(grad_heads).reshape(length, LANES)
    attn_whole = gather_cores(attn_low, 1)
    grad_heads, attn_whole = tie(grad_heads, attn_whole)
    attn_rows.left_known(0, attn_whole)
    grad_heads = step(
        grad_heads,
        (ffn_a, "act_in"),
        (ffn_b, "grad_third"),
        (ffn_b, "units_second"),
        (ffn_b, "act_second"),
        (ffn_b, "hidden_second"),
    )
    if not rest:
        query_grads, kv_grads = causal_back(packed, grad_heads, score_scale)
    else:
        query_grads, kv_grads = attend_back(packed, kv, 0, rest, grad_heads, attended_full, logs, score_scale)
        kv_grads = lax.psum_scatter(kv_grads, rest, scatter_dimension=0, tiled=True)
    query_grads = step(query_grads, (ffn_b, "units_in"), (ffn_b, "hidden_third"))
    packed_grads = jnp.concatenate([query_grads, kv_grads], axis=1)
    packed_grads = to_heads(packed_grads.reshape(sequences * groups, seq_rows, 2 * LANES))
    packed_grads = step(packed_grads, (ffn_b, "act_in"), (attn_rows, "first_left_in"), (ffn_b, "multiply"))
    query_back, key_back, value_back, query_term, key_term = heads_backward(
        packed_grads, query_raw, key_raw, tables, query_gain_row, key_gain_row
    )
    attn_rows.rights_known(
        half_of(grad_attn_low, core, 1), jnp.concatenate([query_back, key_back, value_back], axis=1)
    )
    grad_two, grad_attn_gain = norm_back(
        resid_two,
        attn_gain,
        product_nt(query_back, query_proj) + product_nt(key_back, key_proj) + product_nt(value_back, value_proj),
        grad_three,
    )

    down_low_a = gather_cores(grad_two.astype(BF16))
    ffn_a.grad_known(down_low_a)
    gate_low, up_low = units_back(gate_val_a, up_val_a, out_product_back(down_low_a, down_a_pieces))
    ffn_a.units_known(gate_low, up_low)
    gate_low = step(gate_low, (attn_rows, "multiply"), (ffn_a, "grad_second"))
    grad_one, grad_gain_a = norm_back(
        resid_one, ffn_gain_a, product_nt(gate_low, gate_a) + product_nt(up_low, up_a), grad_two
    )
    grad_one = step(grad_one, (ffn_a, "units_second"))
    grad_mix_low = gather_cores(grad_one.astype(BF16))
    grad_mixer = out_product_back(grad_mix_low, mix_pieces)
    grad_c_part = grad_mixer * mixed_conv
    grad_conv = (grad_mixer * c_part).reshape(sequences, seq_rows, half_width)
    _, pull_conv = jax.vjp(convolve, extended, taps_here)
    grad_extended, grad_taps = pull_conv(grad_conv)
    returned = lax.ppermute(grad_extended[:, :margin, :], SEQ, [(i + 1, i) for i in range(chips - 1)])
    grad_gated = grad_extended[:, margin:, :] + jnp.concatenate(
        [jnp.zeros((sequences, seq_rows - margin, half_width), F32), returned], axis=1
    )
    grad_gated = grad_gated.reshape(-1, half_width)
    grad_gated = step(grad_gated, (ffn_a, "units_in"), (ffn_a, "grad_third"), (ffn_a, "multiply"), (ffn_b, "landed"))
    grad_factor = grad_gated * part_mid
    mid_low = (grad_gated * factor).astype(BF16)
    low_low = jnp.where(core == 0, grad_factor, grad_c_part).astype(BF16)
    high_low = jnp.where(core == 0, grad_c_part, grad_factor).astype(BF16)
    mixer_rows.rights_known(
        half_of(grad_mix_low, core, 1), jnp.concatenate([low_low, swap_cores(mid_low), high_low], axis=1)
    )
    low_low = step(low_low, (attn_rows, "pair_done"))
    partial_one = product_nt(low_low, in_low) + product_nt(mid_low, in_mid) + product_nt(high_low, in_high)
    grad_tokens, grad_mix_gain = norm_back(flat_tokens, mix_gain, partial_one, grad_one)
    tokens_grad = grad_tokens.reshape(streams, seq_rows, width)
    grad_taps = lax.dynamic_update_slice_in_dim(jnp.zeros_like(conv_taps), grad_taps, core * half_width, 1)
    small = jnp.concatenate(
        [
            grad_mix_gain,
            grad_taps.reshape(-1),
            grad_gain_a,
            grad_attn_gain,
            grad_gain_b,
            query_term[0],
            key_term[0],
        ]
    )
    small = step(small, (ffn_b, "fix_first"))
    act_low_b, small = tie(act_low_b, small)
    output = resid_three + sum_cores(out_product(act_low_b, down_b_pieces))
    small = sum_everywhere(small, lambda own: step(own, (ffn_b, "fix_second"), (attn_rows, "z_second"), (mixer_rows, "multiply")))
    small = step(
        small,
        (mixer_rows, "pair_done"),
        (ffn_a, "landed"),
        (ffn_a, "fix_first"),
        (ffn_b, "fix_in"),
        (ffn_a, "fix_second"),
        (attn_rows, "z_done"),
    )
    gate_b_grad, up_b_grad, down_b_grad = ffn_b.finish()
    attn_grad, qkv_grad = attn_rows.finish()
    query_columns, key_columns = query_proj.shape[1], key_proj.shape[1]
    taps_end = width + conv_taps.size
    heads_at = taps_end + 3 * width

    def head_gain(offset):
        both = small[offset : offset + LANES]
        return both[:head_width] + both[head_width:]

    early = (
        output.reshape(streams, seq_rows, width),
        tokens_grad,
        small[:width],
        small[width:taps_end].reshape(conv_taps.shape),
        small[taps_end : taps_end + width],
        small[taps_end + width : taps_end + 2 * width],
        qkv_grad[:, :query_columns],
        qkv_grad[:, query_columns : query_columns + key_columns],
        qkv_grad[:, query_columns + key_columns :],
        attn_grad,
        head_gain(heads_at),
        head_gain(heads_at + LANES),
        small[taps_end + 2 * width : taps_end + 3 * width],
        gate_b_grad,
        up_b_grad,
        down_b_grad.T,
    )
    if paired:
        early = tie(*early)
    main, *early = early
    main = step(
        main,
        (mixer_rows, "z_second"),
        (ffn_a, "fix_in"),
        (mixer_rows, "z_done"),
    )
    mix_grad, proj_grad = mixer_rows.finish()
    gate_a_grad, up_a_grad, down_a_grad = ffn_a.finish()
    (
        tokens_grad,
        mix_gain_grad,
        taps_grad,
        gain_a_grad,
        attn_gain_grad,
        query_grad,
        key_grad,
        value_grad,
        attn_grad,
        query_gain_grad,
        key_gain_grad,
        gain_b_grad,
        gate_b_grad,
        up_b_grad,
        down_b_grad,
    ) = early
    return (
        main,
        tokens_grad,
        mix_gain_grad,
        proj_grad,
        taps_grad,
        mix_grad,
        gain_a_grad,
        gate_a_grad,
        up_a_grad,
        down_a_grad.T,
        attn_gain_grad,
        query_grad,
        key_grad,
        value_grad,
        attn_grad,
        query_gain_grad,
        key_gain_grad,
        gain_b_grad,
        gate_b_grad,
        up_b_grad,
        down_b_grad,
    )


def chip_grid(chips):
    along_z = math.gcd(4, chips)
    side = math.isqrt(chips // along_z)
    return along_z // 2, 2, chips // along_z // side, side


def solution(mesh):
    cores = mesh.shape["wsh"]
    grid = Mesh(mesh.devices.reshape(*chip_grid(mesh.shape["seq"]), cores), EVERY)
    tokens_spec = P("wsh", SEQ, None)
    columns = P(None, "wsh")
    grads = P(SEQ, "wsh")
    in_specs = (
        tokens_spec,
        P("wsh", SEQ),
        tokens_spec,
        P(),
        columns,
        P(),
        columns,
        P(),
        columns,
        columns,
        columns,
        P(),
        columns,
        columns,
        columns,
        columns,
        P(),
        P(),
        P(),
        columns,
        columns,
        columns,
    )
    out_specs = (
        tokens_spec,
        tokens_spec,
        P(),
        grads,
        P(),
        grads,
        P(),
        grads,
        grads,
        P("wsh", SEQ),
        P(),
        grads,
        grads,
        grads,
        grads,
        P(),
        P(),
        P(),
        grads,
        grads,
        P("wsh", SEQ),
    )
    return jax.shard_map(shards, mesh=grid, in_specs=in_specs, out_specs=out_specs, check_vma=False)
```

```python
from functools import partial
import math

import jax
import jax.numpy as jnp
from jax import lax
from jax.experimental import pallas as pl
from jax.experimental.pallas import tpu as pltpu
from jax.sharding import Mesh, PartitionSpec as P

EPS = 1e-05
ROPE_BASE = 1000000.0
MASKED = -1e30
START_PEAK = -1e25
SEQ = ("zh", "zl", "y", "x")
EVERY = SEQ + ("wsh",)
SWAP = [(0, 1), (1, 0)]
BF16 = jnp.bfloat16
F32 = jnp.float32
LANES = 128


def norm_rows(values, gain_vec):
    return values * lax.rsqrt(jnp.mean(values * values, axis=-1, keepdims=True) + EPS) * gain_vec


def product(left, right):
    return jnp.dot(left, right, preferred_element_type=F32)


def product_tn(left, right):
    return lax.dot_general(left, right, (((0,), (0,)), ((), ())), preferred_element_type=F32)


def product_nt(left, right):
    return lax.dot_general(left, right, (((1,), (1,)), ((), ())), preferred_element_type=F32)


def gated_unit(gate_val, up_val):
    return jax.nn.silu(gate_val) * up_val


def swap_cores(block):
    return lax.ppermute(block, "wsh", SWAP)


def gather_cores(block, axis=0):
    return lax.all_gather(block, "wsh", axis=axis, tiled=True)


def half_of(array, which, axis=0):
    size = array.shape[axis] // 2
    return lax.dynamic_slice_in_dim(array, which * size, size, axis)


def ordered(core, own, other):
    first = jnp.where(core == 0, own, other)
    second = jnp.where(core == 0, other, own)
    return jnp.concatenate([first, second], axis=-1)


def lane_of(shape):
    return lax.broadcasted_iota(jnp.int32, shape, 1)


def two_heads(block):
    return jnp.concatenate([block[:, :64], block[:, 64:]], axis=0)


def side_by_side(block):
    rows = block.shape[0] // 2
    return jnp.concatenate([block[:rows], block[rows:]], axis=1)


EXTRA = 16


def flat(block):
    return block[:, : block.shape[1] - EXTRA].reshape(-1, block.shape[2])


def places(packed_ref, offset):
    chips, padded, _ = packed_ref.shape
    rows = padded - EXTRA
    coded = packed_ref[:, rows, :].astype(F32)
    starts = coded[:, :64] * 64.0 + coded[:, 64:]
    diagonal = lax.broadcasted_iota(jnp.int32, (rows, rows), 0) == lane_of((rows, rows))
    columns = [
        jnp.sum(jnp.where(diagonal, starts[chip : chip + 1], 0.0), axis=1, keepdims=True) for chip in range(chips)
    ]
    starts = jnp.concatenate(columns * 2, axis=0).astype(jnp.int32)
    row = lax.broadcasted_iota(jnp.int32, (2 * chips * rows, 1), 0)
    row = jnp.where(row >= chips * rows, row - chips * rows, row)
    return starts, offset + pl.program_id(0) * chips * rows + row


def first_place(rest, length):
    return lax.axis_index(rest) * length if rest else 0


def lay_out(kv_ref, flat_ref):
    rows = kv_ref.shape[1] - EXTRA

    @pl.when(pl.program_id(0) == 0)
    def _():
        for chip in range(kv_ref.shape[0]):
            flat_ref[chip * rows : (chip + 1) * rows] = kv_ref[chip, :rows]


def attend_kernel(packed_ref, kv_ref, low_ref, full_ref, log_ref, flat_ref, *, rest, span, scale):
    lay_out(kv_ref, flat_ref)
    rows = low_ref.shape[0]
    offset = first_place(rest, rows * pl.num_programs(0))
    query = two_heads(flat(packed_ref[...]))
    starts, mine = places(packed_ref, offset)

    def advance(index, carried):
        peak, total, mixed = carried
        kv_block = flat_ref[pl.ds(pl.multiple_of(index * span, span), span), :]
        scores = product_nt(query, kv_block[:, :64]) * scale
        place = index * span + lane_of((1, span))
        scores = jnp.where((place >= starts) & (place <= mine), scores, MASKED)
        fresh_peak = jnp.maximum(peak, jnp.max(scores, axis=1, keepdims=True))
        shares = jnp.exp(scores - fresh_peak)
        keep = jnp.exp(peak - fresh_peak)
        total = total * keep + jnp.sum(shares, axis=1, keepdims=True)
        mixed = mixed * keep + product(shares.astype(BF16), kv_block[:, 64:])
        return fresh_peak, total, mixed

    last = (offset + (pl.program_id(0) + 1) * rows) // span
    peak, total, mixed = lax.fori_loop(
        0,
        last,
        advance,
        (
            jnp.full((2 * rows, 1), START_PEAK, F32),
            jnp.zeros((2 * rows, 1), F32),
            jnp.zeros((2 * rows, 64), F32),
        ),
    )
    attended = side_by_side(mixed / total)
    low_ref[...] = attended.astype(BF16)
    full_ref[...] = attended
    log_ref[...] = side_by_side(jnp.broadcast_to(peak + jnp.log(total), (2 * rows, 64)))


def attend_back_kernel(packed_ref, kv_ref, grad_ref, full_ref, log_ref, dq_ref, dkv_ref, sums_ref, flat_ref, *, rest, span, scale):
    lay_out(kv_ref, flat_ref)
    rows = grad_ref.shape[0]
    offset = first_place(rest, rows * pl.num_programs(0))
    query = two_heads(flat(packed_ref[...]))
    grad = two_heads(grad_ref[...])
    attended = two_heads(full_ref[...])
    logs = two_heads(log_ref[...])[:, :1]
    delta = jnp.sum(grad.astype(F32) * attended, axis=1, keepdims=True)
    starts, mine = places(packed_ref, offset)

    @pl.when(pl.program_id(0) == 0)
    def _():
        sums_ref[...] = jnp.zeros_like(sums_ref)

    def advance(index, query_grad):
        window = pl.ds(pl.multiple_of(index * span, span), span)
        kv_block = flat_ref[window, :]
        key, value = kv_block[:, :64], kv_block[:, 64:]
        scores = product_nt(query, key) * scale
        place = index * span + lane_of((1, span))
        scores = jnp.where((place >= starts) & (place <= mine), scores, MASKED)
        shares = jnp.exp(scores - logs)
        grad_scores = (shares * (product_nt(grad, value) - delta)).astype(BF16)
        key_grad = product_tn(grad_scores, query) * scale
        value_grad = product_tn(shares.astype(BF16), grad)
        sums_ref[window, :] += jnp.concatenate([key_grad, value_grad], axis=1)
        return query_grad + product(grad_scores, key)

    last = (offset + (pl.program_id(0) + 1) * rows) // span
    query_grad = lax.fori_loop(0, last, advance, jnp.zeros((2 * rows, 64), F32))
    dq_ref[...] = side_by_side(query_grad * scale).astype(BF16)

    @pl.when(pl.program_id(0) == pl.num_programs(0) - 1)
    def _():
        dkv_ref[...] = sums_ref[...].astype(BF16)


def rows_spec(rows, columns, column_block=0):
    return pl.BlockSpec((rows, columns), lambda index: (index, column_block))


def whole_spec(rows, columns, column_block=0):
    return pl.BlockSpec((rows, columns), lambda index: (0, column_block))


def attend_specs(packed, kv, kv_block):
    chips, padded, _ = packed.shape
    per_step = max(1, 256 // (padded - EXTRA))
    packed_spec = pl.BlockSpec((per_step, padded, LANES), lambda index: (index, 0, 0))
    kv_spec = pl.BlockSpec((kv.shape[0], padded, LANES), lambda index: (0, 0, kv_block))
    return chips // per_step, per_step * (padded - EXTRA), [packed_spec, kv_spec]


def attend(packed, kv, kv_block, rest, scale):
    steps, rows, specs = attend_specs(packed, kv, kv_block)
    length, keys = steps * rows, kv.shape[0] * (kv.shape[1] - EXTRA)
    return pl.pallas_call(
        partial(attend_kernel, rest=rest, span=rows, scale=scale),
        grid=(steps,),
        in_specs=specs,
        out_specs=[rows_spec(rows, LANES)] * 3,
        out_shape=[
            jax.ShapeDtypeStruct((length, LANES), BF16),
            jax.ShapeDtypeStruct((length, LANES), F32),
            jax.ShapeDtypeStruct((length, LANES), F32),
        ],
        scratch_shapes=[pltpu.VMEM((keys, LANES), BF16)],
        compiler_params=pltpu.CompilerParams(vmem_limit_bytes=24 << 20),
        cost_estimate=pl.CostEstimate(flops=4 * length * keys * 64, bytes_accessed=2 << 20, transcendentals=length * keys),
    )(packed, kv)


def attend_back(packed, kv, kv_block, rest, grad, full, logs, scale):
    steps, rows, specs = attend_specs(packed, kv, kv_block)
    length, keys = steps * rows, kv.shape[0] * (kv.shape[1] - EXTRA)
    return pl.pallas_call(
        partial(attend_back_kernel, rest=rest, span=rows, scale=scale),
        grid=(steps,),
        in_specs=specs + [rows_spec(rows, LANES)] * 3,
        out_specs=[rows_spec(rows, LANES), whole_spec(keys, LANES)],
        out_shape=[jax.ShapeDtypeStruct((length, LANES), BF16), jax.ShapeDtypeStruct((keys, LANES), BF16)],
        scratch_shapes=[pltpu.VMEM((keys, LANES), F32), pltpu.VMEM((keys, LANES), BF16)],
        compiler_params=pltpu.CompilerParams(vmem_limit_bytes=24 << 20),
        cost_estimate=pl.CostEstimate(flops=10 * length * keys * 64, bytes_accessed=3 << 20, transcendentals=length * keys),
    )(packed, kv, grad, full, logs)


def causal_blocks(packed_ref, scale):
    chips, padded, _ = packed_ref.shape
    rows = padded - EXTRA
    per_block = 256 // rows
    blocks = []
    for first in range(0, chips, per_block):
        packed = packed_ref[first : first + per_block]
        whole = flat(packed)
        coded = packed[:, rows, :LANES].astype(F32)
        starts = coded[:, :64] * 64.0 + coded[:, 64:]
        starts = jnp.concatenate([starts[chip : chip + 1] for chip in range(per_block)] * 2, axis=1)
        place = lane_of((1, 512)) % 256 + first * rows
        query = two_heads(whole[:, :LANES])
        query = (query.astype(F32) * scale).astype(BF16)
        blocks.append((query, whole[:, 128:192], whole[:, 192:], starts.astype(jnp.int32), place))
    return blocks


def causal_shares(blocks, index):
    query, _, _, starts, mine = blocks[index]
    scores = []
    for other in range(index + 1):
        key = blocks[other][1]
        place = lax.broadcasted_iota(jnp.int32, (256, 1), 0) + other * 256
        allowed = place >= starts
        if other == index:
            allowed = allowed & (place <= mine)
        scores.append(jnp.where(allowed, product_nt(key, query), MASKED))
    peak = jnp.max(scores[0], axis=0, keepdims=True)
    for block in scores[1:]:
        peak = jnp.maximum(peak, jnp.max(block, axis=0, keepdims=True))
    shares = [jnp.exp(block - peak) for block in scores]
    total = sum(jnp.sum(block, axis=0, keepdims=True) for block in shares)
    return shares, 1.0 / total


def causal_kernel(packed_ref, low_ref, *, scale):
    blocks = causal_blocks(packed_ref, scale)
    for index in range(len(blocks)):
        shares, inverse = causal_shares(blocks, index)
        mixed = 0.0
        for other, block in enumerate(shares):
            mixed = mixed + product_tn(blocks[other][2], block.astype(BF16))
        attended = (mixed * inverse).T
        low_ref[index * 256 : (index + 1) * 256] = side_by_side(attended).astype(BF16)


def causal_back_kernel(packed_ref, grad_ref, dq_ref, dkv_ref, sums_ref, *, scale):
    blocks = causal_blocks(packed_ref, scale)
    for index in range(len(blocks)):
        here = slice(index * 256, (index + 1) * 256)
        query = blocks[index][0]
        grad = two_heads(grad_ref[here])
        shares, inverse = causal_shares(blocks, index)
        shares = [block * inverse for block in shares]
        grad_shares = [product_nt(blocks[other][2], grad) for other in range(index + 1)]
        delta = sum(
            jnp.sum(share * grad_share, axis=0, keepdims=True) for share, grad_share in zip(shares, grad_shares)
        )
        query_grad = 0.0
        for other, (share, grad_share) in enumerate(zip(shares, grad_shares)):
            grad_scores = (share * (grad_share - delta)).astype(BF16)
            query_grad = query_grad + product_tn(blocks[other][1], grad_scores)
            parts = jnp.concatenate([product(grad_scores, query), product(share.astype(BF16), grad)], axis=1)
            there = slice(other * 256, (other + 1) * 256)
            if other == index:
                sums_ref[there] = parts
            else:
                sums_ref[there] += parts
        dq_ref[here] = side_by_side((query_grad * scale).T).astype(BF16)
    dkv_ref[...] = sums_ref[...].astype(BF16)


def causal(packed, scale):
    length = packed.shape[0] * (packed.shape[1] - EXTRA)
    return pl.pallas_call(
        partial(causal_kernel, scale=scale),
        out_shape=jax.ShapeDtypeStruct((length, LANES), BF16),
        compiler_params=pltpu.CompilerParams(vmem_limit_bytes=32 << 20),
        cost_estimate=pl.CostEstimate(flops=2 * length * length * 128, bytes_accessed=2 << 20, transcendentals=length * length),
    )(packed)


def causal_back(packed, grad, scale):
    length = grad.shape[0]
    return pl.pallas_call(
        partial(causal_back_kernel, scale=scale),
        out_shape=[jax.ShapeDtypeStruct((length, LANES), BF16)] * 2,
        scratch_shapes=[pltpu.VMEM((length, LANES), F32)],
        compiler_params=pltpu.CompilerParams(vmem_limit_bytes=32 << 20),
        cost_estimate=pl.CostEstimate(flops=5 * length * length * 128, bytes_accessed=3 << 20, transcendentals=length * length),
    )(packed, grad)


def heads_grad_kernel(own_ref, other_ref, own_piece_ref, other_piece_ref, out_ref):
    sums = product_nt(own_ref[...], own_piece_ref[...]) + product_nt(other_ref[...], other_piece_ref[...])
    out_ref[...] = sums.astype(BF16).reshape(out_ref.shape)


def heads_grad(own, other, pieces, sequences):
    tokens, columns = own.shape
    groups = pieces[0].shape[0] // LANES
    piece_spec = pl.BlockSpec((LANES, columns), lambda index: (index, 0))
    rows = tokens // sequences
    return pl.pallas_call(
        heads_grad_kernel,
        grid=(groups,),
        in_specs=[whole_spec(tokens, columns)] * 2 + [piece_spec] * 2,
        out_specs=pl.BlockSpec((sequences, rows, LANES), lambda index: (index, 0, 0)),
        out_shape=jax.ShapeDtypeStruct((groups * sequences, rows, LANES), BF16),
        compiler_params=pltpu.CompilerParams(vmem_limit_bytes=16 << 20),
    )(own, other, *pieces)


def head_means(values):
    low_lanes = lane_of(values.shape) < 64
    low_mean = jnp.sum(jnp.where(low_lanes, values, 0.0), axis=1, keepdims=True) * (1.0 / 64)
    high_mean = jnp.sum(jnp.where(low_lanes, 0.0, values), axis=1, keepdims=True) * (1.0 / 64)
    return jnp.where(low_lanes, low_mean, high_mean)


def turn(values, sign):
    lower = (lane_of(values.shape) % 64) < 32
    return jnp.where(lower, -sign * pltpu.roll(values, LANES - 32, 1), sign * pltpu.roll(values, 32, 1))


def head_forward(raw, gain, cosine, sine):
    unit = raw * lax.rsqrt(head_means(raw * raw) + EPS) * gain
    return (unit * cosine + turn(unit, 1.0) * sine).astype(BF16)


def head_backward(raw, gain, cosine, sine, grad):
    back = grad * cosine + turn(grad * sine, -1.0)
    scale = lax.rsqrt(head_means(raw * raw) + EPS)
    gain_term = jnp.sum(back * raw * scale, axis=0, keepdims=True)
    back = back * gain
    raw_grad = back * scale - raw * (scale * scale * scale) * head_means(back * raw)
    return raw_grad.astype(BF16), gain_term


def heads_kernel(query_ref, key_ref, value_ref, starts_ref, cos_ref, sin_ref, query_gain_ref, key_gain_ref, out_ref):
    rows = out_ref.shape[1] - EXTRA
    groups = key_ref.shape[1] // 64
    sequences = query_ref.shape[0] // rows
    cosine, sine = cos_ref[...], sin_ref[...]
    for place in range(sequences):
        span = pl.ds(place * rows, rows)
        starts = jnp.broadcast_to(starts_ref[place : place + 1], (EXTRA, LANES)).astype(BF16)
        for pair in range(groups // 2):
            lanes = pl.ds(pair * LANES, LANES)
            key = head_forward(key_ref[span, lanes], key_gain_ref[...], cosine, sine)
            value = value_ref[span, lanes].astype(BF16)
            for side in range(2):
                group = 2 * pair + side
                query = head_forward(
                    query_ref[span, pl.ds(group * LANES, LANES)], query_gain_ref[...], cosine, sine
                )
                half = slice(64 * side, 64 * side + 64)
                block = group * sequences + place
                out_ref[block, :rows, 0:LANES] = query
                out_ref[block, :rows, LANES : 2 * LANES] = jnp.concatenate([key[:, half], value[:, half]], axis=1)
                out_ref[block, rows:, 0:LANES] = starts
                out_ref[block, rows:, LANES : 2 * LANES] = starts


def heads_back_kernel(
    grad_ref,
    query_ref,
    key_ref,
    cos_ref,
    sin_ref,
    query_gain_ref,
    key_gain_ref,
    dq_ref,
    dk_ref,
    dv_ref,
    query_term_ref,
    key_term_ref,
):
    rows = grad_ref.shape[1]
    groups = key_ref.shape[1] // 64
    sequences = query_ref.shape[0] // rows
    cosine, sine = cos_ref[...], sin_ref[...]
    query_term = jnp.zeros((1, LANES), F32)
    key_term = jnp.zeros((1, LANES), F32)
    for place in range(sequences):
        span = pl.ds(place * rows, rows)
        for pair in range(groups // 2):
            lanes = pl.ds(pair * LANES, LANES)
            sides = [grad_ref[(2 * pair + side) * sequences + place, :, LANES : 2 * LANES] for side in range(2)]
            key_grad = jnp.concatenate([sides[0][:, :64], sides[1][:, :64]], axis=1).astype(F32)
            dv_ref[span, lanes] = jnp.concatenate([sides[0][:, 64:], sides[1][:, 64:]], axis=1)
            low, term = head_backward(key_ref[span, lanes], key_gain_ref[...], cosine, sine, key_grad)
            dk_ref[span, lanes] = low
            key_term = key_term + term
            for side in range(2):
                group = 2 * pair + side
                wide = pl.ds(group * LANES, LANES)
                query_grad = grad_ref[group * sequences + place, :, 0:LANES].astype(F32)
                low, term = head_backward(query_ref[span, wide], query_gain_ref[...], cosine, sine, query_grad)
                dq_ref[span, wide] = low
                query_term = query_term + term
    query_term_ref[...] = query_term
    key_term_ref[...] = key_term


def heads_forward(query, key, value, starts, tables, query_gain, key_gain):
    rows = starts.shape[1]
    blocks = starts.shape[0] * (key.shape[1] // 64)
    coded = jnp.concatenate([starts // 64, starts % 64], axis=1).astype(F32)
    return pl.pallas_call(
        heads_kernel,
        out_shape=jax.ShapeDtypeStruct((blocks, rows + EXTRA, 2 * LANES), BF16),
        compiler_params=pltpu.CompilerParams(vmem_limit_bytes=32 << 20),
    )(query, key, value, coded, *tables, query_gain, key_gain)


def heads_backward(grad, query, key, tables, query_gain, key_gain):
    return pl.pallas_call(
        heads_back_kernel,
        out_shape=[
            jax.ShapeDtypeStruct(query.shape, BF16),
            jax.ShapeDtypeStruct(key.shape, BF16),
            jax.ShapeDtypeStruct(key.shape, BF16),
            jax.ShapeDtypeStruct((1, LANES), F32),
            jax.ShapeDtypeStruct((1, LANES), F32),
        ],
        compiler_params=pltpu.CompilerParams(vmem_limit_bytes=32 << 20),
    )(grad, query, key, *tables, query_gain, key_gain)


def at_place(pieces, place):
    return jnp.where(place == 0, pieces[0], pieces[1])


def quarters(block, dim, core):
    size = block.shape[dim] // 4
    pieces = [lax.slice_in_dim(block, index * size, (index + 1) * size, axis=dim) for index in range(4)]
    return [
        pieces[0],
        jnp.where(core == 0, pieces[2], pieces[1]),
        jnp.where(core == 0, pieces[1], pieces[2]),
        pieces[3],
    ]


def places_here():
    core, x, y = lax.axis_index("wsh"), lax.axis_index("x"), lax.axis_index("y")
    return jnp.where(core == 0, x, y), jnp.where(core == 0, y, x)


def ffn_grad_kernel(meta_ref, *refs):
    hidden, grads = refs[:5], refs[5:10]
    keep_ref, far_ref, last_ref, act_ref, act_far_ref, act_last_ref = refs[10:16]
    outs = refs[16:]
    rows = keep_ref.shape[0]
    core, place = lax.axis_index("wsh"), places_here()[1]

    def tokens_of(left_refs):
        own, near, across, last, last_far = (left_ref[...] for left_ref in left_refs)
        halves = jnp.where(core == 0, last, last_far), jnp.where(core == 0, last_far, last)
        return own, near, across, jnp.concatenate(halves, axis=0)

    def lanes(block):
        pieces = quarters(block, 1, core)
        return jnp.concatenate([at_place(pieces[:2], place), at_place(pieces[2:], place)], axis=1)

    def total(lefts, own_ref, near_ref, pair_ref):
        sums = product_tn(lefts[0], own_ref[...]) + product_tn(lefts[1], near_ref[...])
        return sums + product_tn(lefts[2], pair_ref[:rows]) + product_tn(lefts[3], pair_ref[rows:])

    units = total(tokens_of(hidden), keep_ref, far_ref, last_ref).astype(BF16)
    downs = total([lanes(block) for block in tokens_of(grads)], act_ref, act_far_ref, act_last_ref).astype(BF16)
    unit_rows = units.shape[0]
    step, steps = pl.program_id(0), pl.num_programs(0)

    for place, out_ref in enumerate(outs):

        @pl.when(step * len(outs) // steps == place)
        def _(out_ref=out_ref):
            out_ref[:unit_rows] = units
            out_ref[unit_rows:] = downs


def ffn_grad_rows(hidden, grads, units, acts, whole):
    first, second = places_here()
    zl = lax.axis_index("zl")
    tokens, width = hidden[0].shape
    columns = units[2].shape[1]
    order = (0, 1, 2, 3) if whole else (1 - zl, 3 - zl, zl, 2 + zl)
    meta = jnp.stack([jnp.asarray(value, jnp.int32) for value in (*order, second, first)])

    def left_spec(block):
        return pl.BlockSpec((block.shape[0], width // 4), lambda index, meta_ref: (0, meta_ref[index]))

    def half_spec(position):
        return pl.BlockSpec((tokens, columns), lambda index, meta_ref: (0, meta_ref[position]))

    def full_spec(rows):
        return pl.BlockSpec((rows, columns), lambda index, meta_ref: (0, 0))

    out_rows = width // 4 + width // 8
    outs = 1 if whole else 2
    steps = 4 // outs

    def out_spec(place):
        return pl.BlockSpec((out_rows, columns), lambda index, meta_ref: (jnp.clip(index - place * steps, 0, steps - 1), 0))

    return pl.pallas_call(
        ffn_grad_kernel,
        grid_spec=pltpu.PrefetchScalarGridSpec(
            num_scalar_prefetch=1,
            grid=(4,),
            in_specs=[left_spec(block) for block in (*hidden, *grads)]
            + [half_spec(4), half_spec(4), full_spec(2 * tokens), half_spec(5), full_spec(tokens), full_spec(2 * tokens)],
            out_specs=[out_spec(place) for place in range(outs)],
        ),
        out_shape=[jax.ShapeDtypeStruct((steps * out_rows, columns), BF16)] * outs,
        compiler_params=pltpu.CompilerParams(vmem_limit_bytes=58 << 20),
        cost_estimate=pl.CostEstimate(
            flops=8 * tokens * 4 * out_rows * columns, bytes_accessed=14 << 20, transcendentals=0
        ),
    )(meta, *hidden, *grads, *units, *acts)


def row_kernel(a_ref, a_far_ref, b_ref, b_far_ref, right_ref, right_far_ref, send_ref, keep_ref, *, cut):
    core, (first, second) = lax.axis_index("wsh"), places_here()
    for left_ref, left_far_ref, span in ((a_ref, a_far_ref, slice(0, cut)), (b_ref, b_far_ref, slice(cut, None))):
        sums = product_tn(left_ref[...], right_ref[:, span]) + product_tn(left_far_ref[...], right_far_ref[:, span])
        pieces = quarters(sums, 0, core)
        pieces = [at_place(pieces[0::2], first), at_place(pieces[1::2], first)]
        keep_ref[:, span] = at_place(pieces, second).astype(BF16)
        send_ref[:, span] = at_place(pieces[::-1], second).astype(BF16)


def row_grad_rows(lefts, rights, cut):
    (a, a_far), (b, b_far) = lefts
    tokens, width = a.shape
    columns = rights[0].shape[1]
    out_rows = width // 16
    left_spec = pl.BlockSpec((tokens, width // 4), lambda index: (0, index))
    return pl.pallas_call(
        partial(row_kernel, cut=cut),
        grid=(4,),
        in_specs=[left_spec] * 4 + [whole_spec(tokens, columns)] * 2,
        out_specs=[rows_spec(out_rows, columns)] * 2,
        out_shape=[jax.ShapeDtypeStruct((4 * out_rows, columns), BF16)] * 2,
        compiler_params=pltpu.CompilerParams(vmem_limit_bytes=20 << 20),
        cost_estimate=pl.CostEstimate(flops=4 * tokens * width * columns, bytes_accessed=6 << 20, transcendentals=0),
    )(a, a_far, b, b_far, *rights)


def trade(block, axis):
    return lax.ppermute(block, axis, SWAP)


def trade_mirrored(block, stage):
    route = []
    for index in range(32):
        along_x = (index % 2 == 0) == (stage == 1)
        route.append((index, index ^ (2 if along_x else 4)))
    return lax.ppermute(block, EVERY, route)


def rows_at(blocks, axis, which):
    return lax.dynamic_index_in_dim(blocks, which, axis, keepdims=False)


def add_low(kept, arrived):
    return (kept.astype(F32) + arrived.astype(F32)).astype(BF16)


def tie(*values):
    return lax.optimization_barrier(values)


def sum_everywhere(vector, between):
    devices = lax.axis_size(EVERY)
    piece = -(-vector.size // (devices * LANES)) * LANES
    padded = jnp.pad(vector, (0, devices * piece - vector.size)).reshape(devices, 1, piece)
    turn_over = partial(lax.all_to_all, axis_name=EVERY, split_axis=0, concat_axis=0, tiled=True)
    own = between(jnp.sum(turn_over(padded), axis=0, keepdims=True))
    return turn_over(jnp.broadcast_to(own, (devices, 1, piece))).reshape(-1)


def mirrored_rows(shard, core):
    return jnp.stack(quarters(shard, 0, core)).reshape(2, 2, -1, shard.shape[1])


class AlongZ:
    def z_start(self, main, send, keep):
        main, send, keep = tie(main, send, keep)
        self.part = keep, trade(send, "zl")
        return main

    def z_second(self, main):
        keep, arrived = self.part
        main, arrived = tie(main, arrived)
        summed = add_low(keep, arrived).reshape(2, -1, keep.shape[-1])
        here = lax.axis_index("zh")
        send, keep = rows_at(summed, 0, 1 - here), rows_at(summed, 0, here)
        main, send, keep = tie(main, send, keep)
        self.part = keep, trade(send, "zh")
        return main

    def z_done(self, main):
        keep, arrived = self.part
        main, arrived = tie(main, arrived)
        self.part = keep, arrived
        return main


class FourChips:
    def __init__(self, own):
        self.own, self.near = own, trade_mirrored(own, 1)

    def second(self, main):
        main, near = tie(main, self.near)
        across = swap_cores(near)
        half = half_of(across, lax.axis_index("wsh"))
        main, half = tie(main, half)
        self.near, self.across, self.last = near, across, trade_mirrored(half, 1)
        return main

    def third(self, main):
        main, last = tie(main, self.last)
        self.blocks = self.own, self.near, self.across, last, swap_cores(last)
        return main


class FfnGrads(AlongZ):
    def __init__(self, offload):
        self.core, self.places, self.offload = lax.axis_index("wsh"), places_here(), offload

    def hidden_known(self, hidden):
        self.hidden = FourChips(hidden)

    def act_known(self, act):
        self.act = act
        self.act_far = trade_mirrored(half_of(act, 1 - self.places[0], 1), 1)

    def grad_known(self, grad):
        self.grad = FourChips(grad)

    def units_known(self, gate_low, up_low):
        place = self.places[0]
        self.keep = at_place((gate_low, up_low), place)
        self.far = trade_mirrored(at_place((up_low, gate_low), place), 1)

    def hidden_second(self, main):
        return self.hidden.second(main)

    def hidden_third(self, main):
        return self.hidden.third(main)

    def grad_second(self, main):
        return self.grad.second(main)

    def grad_third(self, main):
        return self.grad.third(main)

    def act_second(self, main):
        main, self.act_far = tie(main, self.act_far)
        main, send = tie(main, jnp.concatenate([half_of(self.act, self.places[0], 1), self.act_far], axis=0))
        self.act_last = trade_mirrored(send, 2)
        return main

    def act_in(self, main):
        main, self.act_last = tie(main, self.act_last)
        return main

    def units_in(self, main):
        main, self.last = tie(main, self.last)
        return main

    def units_second(self, main):
        main, self.far = tie(main, self.far)
        other = 1 - self.places[1]
        main, send = tie(main, jnp.concatenate([half_of(self.keep, other, 1), half_of(self.far, other, 1)], axis=0))
        self.last = trade_mirrored(send, 2)
        return main

    def multiply(self, main):
        main, last, act_last = tie(main, self.last, self.act_last)
        sums = ffn_grad_rows(
            self.hidden.blocks,
            self.grad.blocks,
            (self.keep, self.far, last),
            (self.act, self.act_far, act_last),
            self.offload,
        )
        if not self.offload:
            return self.z_start(main, *sums)
        main, sums = tie(main, *sums)
        self.rows = lax.psum_scatter(sums, ("zh", "zl"), scatter_dimension=0, tiled=True)
        return main

    def landed(self, main):
        main, self.rows = tie(main, self.rows)
        return main

    def fix_first(self, main):
        second = self.places[1]
        rows = self.rows if self.offload else add_low(*self.part)
        unit_rows = rows.shape[0] // 3 * 2
        units = jnp.stack(quarters(rows[:unit_rows], 0, self.core)).reshape(2, 2, -1, rows.shape[1])
        main, send = tie(main, rows_at(units, 1, 1 - second))
        self.units, self.downs = rows_at(units, 1, second), rows[unit_rows:].reshape(2, -1, rows.shape[1])
        self.units_far = trade_mirrored(send, 2)
        return main

    def fix_second(self, main):
        first, second = self.places
        main, far = tie(main, self.units_far)
        units = ordered(second, self.units, far)
        self.own, send = (
            jnp.concatenate([rows_at(units, 0, which), rows_at(self.downs, 0, which)], axis=1)
            for which in (first, 1 - first)
        )
        main, send = tie(main, send)
        self.far = trade_mirrored(send, 1)
        return main

    def fix_in(self, main):
        main, self.far = tie(main, self.far)
        return main

    def finish(self):
        first = self.places[0]
        own, far = self.own.astype(F32), self.far.astype(F32)
        columns = own.shape[1] // 3 * 2
        gate = at_place((own[:, :columns], far[:, :columns]), first)
        up = at_place((far[:, :columns], own[:, :columns]), first)
        return gate, up, ordered(first, own[:, columns:], far[:, columns:])


class RowGrads(AlongZ):
    def __init__(self):
        self.lefts = [None, None]

    def left_known(self, index, left):
        self.lefts[index] = left, trade_mirrored(left, 1)

    def rights_known(self, first, second):
        self.cut = first.shape[1]
        right = jnp.concatenate([first, second], axis=1)
        self.rights = right, trade_mirrored(right, 1)

    def first_left_in(self, main):
        main, self.lefts[0] = tie(main, self.lefts[0])
        return main

    def second_left_in(self, main):
        main, self.lefts[1] = tie(main, self.lefts[1])
        return main

    def multiply(self, main):
        main, far, lefts = tie(main, self.rights[1], self.lefts)
        main, (send, keep) = tie(main, row_grad_rows(lefts, (self.rights[0], far), self.cut))
        self.part = keep, trade_mirrored(send, 2)
        return main

    def pair_done(self, main):
        keep, arrived = self.part
        main, arrived = tie(main, arrived)
        summed = add_low(keep, arrived).reshape(2, 2, -1, keep.shape[-1])
        here = lax.axis_index("zl")
        send, keep = (rows_at(summed, 1, which).reshape(-1, keep.shape[-1]) for which in (1 - here, here))
        return self.z_start(main, send, keep)

    def finish(self):
        keep, arrived = self.part
        summed = keep.astype(F32) + arrived.astype(F32)
        return summed[:, : self.cut], summed[:, self.cut :]


def plain_grad(left, right):
    return lax.psum_scatter(product_tn(left, right).astype(BF16), SEQ, scatter_dimension=0, tiled=True).astype(F32)


class PlainFfnGrads:
    def __init__(self, offload):
        pass

    def hidden_known(self, hidden):
        self.hidden = hidden

    def act_known(self, act):
        self.act = act

    def grad_known(self, grad):
        self.grad = grad

    def units_known(self, gate_low, up_low):
        self.units = gate_low, up_low

    def finish(self):
        gate, up = (plain_grad(self.hidden, unit) for unit in self.units)
        return gate, up, plain_grad(self.grad, self.act)


class PlainRowGrads:
    def __init__(self):
        self.lefts = [None, None]

    def left_known(self, index, left):
        self.lefts[index] = left

    def rights_known(self, *rights):
        self.rights = rights

    def finish(self):
        return tuple(plain_grad(left, right) for left, right in zip(self.lefts, self.rights))


def shards(
    tokens,
    doc_start,
    cotangent,
    mix_gain,
    in_proj,
    conv_taps,
    mix_proj,
    ffn_gain_a,
    gate_a,
    up_a,
    down_a,
    attn_gain,
    query_proj,
    key_proj,
    value_proj,
    attn_proj,
    query_gain,
    key_gain,
    ffn_gain_b,
    gate_b,
    up_b,
    down_b,
):
    streams, seq_rows, width = tokens.shape
    core = lax.axis_index("wsh")
    sequences = streams * lax.axis_size("wsh")
    token_count = streams * seq_rows
    head_width = query_gain.shape[0]
    groups = key_proj.shape[1] // head_width
    score_scale = head_width ** (-0.5)
    margin = conv_taps.shape[0] - 1
    half_width = width // 2
    chips = lax.axis_size(SEQ)
    chip = lax.axis_index(SEQ)
    positions = chip * seq_rows + jnp.arange(seq_rows, dtype=jnp.int32)
    paired = all(lax.axis_size(name) == 2 for name in SEQ)
    ffn_kind, rows_kind = (FfnGrads, RowGrads) if paired else (PlainFfnGrads, PlainRowGrads)
    ffn_a, ffn_b, mixer_rows, attn_rows = ffn_kind(True), ffn_kind(True), rows_kind(), rows_kind()

    def step(main, *events):
        if paired:
            for owner, name in events:
                main = getattr(owner, name)(main)
        return main

    frequency = ROPE_BASE ** (-(jnp.arange(0, head_width, 2, dtype=F32) / head_width))
    angles = positions.astype(F32)[:, None] * jnp.tile(frequency, 4)[None, :]
    tables = (jnp.cos(angles), jnp.sin(angles))
    query_gain_row = jnp.tile(query_gain, 2)[None, :]
    key_gain_row = jnp.tile(key_gain, 2)[None, :]

    def split_rows(weight, sent):
        return half_of(weight, core), half_of(swap_cores(sent), core)

    def out_product(left, pieces):
        return ordered(core, product(left, pieces[0]), product(left, pieces[1]))

    def out_product_back(grad, pieces):
        own = half_of(grad, core, 1)
        other = half_of(grad, 1 - core, 1)
        return product_nt(own, pieces[0]) + product_nt(other, pieces[1])

    def sum_cores(partial_rows):
        return half_of(partial_rows, core) + swap_cores(half_of(partial_rows, 1 - core))

    starts_far = swap_cores(doc_start)
    starts_here = jnp.concatenate(
        [jnp.where(core == 0, doc_start, starts_far), jnp.where(core == 0, starts_far, doc_start)], axis=0
    )
    in_far = swap_cores(in_proj)
    in_low, in_high = in_proj[:, :half_width], in_proj[:, 2 * half_width :]
    in_mid = in_far[:, half_width : 2 * half_width]

    grad_out = cotangent.reshape(token_count, width)
    down_low_b = gather_cores(grad_out.astype(BF16))
    flat_tokens = tokens.reshape(token_count, width)
    low_one = gather_cores(norm_rows(flat_tokens, mix_gain).astype(BF16))
    low_one, mix_far, down_a_far = tie(low_one, mix_proj, down_a)
    mix_pieces = split_rows(mix_proj, mix_far)
    down_a_pieces = split_rows(down_a, down_a_far)
    part_low = product(low_one, in_low)
    part_mid = product(low_one, in_mid)
    part_high = product(low_one, in_high)
    factor = jnp.where(core == 0, part_low, part_high)
    c_part = jnp.where(core == 0, part_high, part_low)
    gated = (part_mid * factor).reshape(sequences, seq_rows, half_width)
    edge_rows = lax.ppermute(gated[:, seq_rows - margin :, :], SEQ, [(i, i + 1) for i in range(chips - 1)])
    extended = jnp.concatenate([edge_rows, gated], axis=1)
    taps_here = half_of(conv_taps, core, 1)

    def convolve(extended_rows, taps_now):
        running = jnp.zeros_like(extended_rows[:, margin:])
        for tap_index in range(margin + 1):
            offset = margin - tap_index
            shifted = extended_rows[:, tap_index : tap_index + seq_rows]
            allowed = (positions[None, :] - offset >= starts_here)[:, :, None]
            running = running + jnp.where(allowed, shifted, 0.0) * taps_now[tap_index]
        return running

    mixed_conv = convolve(extended, taps_here).reshape(-1, half_width)
    mixer_low = (c_part * mixed_conv).astype(BF16)
    mixer_rows.left_known(1, low_one)
    resid_one = flat_tokens + sum_cores(out_product(mixer_low, mix_pieces))

    def ffn_units(grads, residual, gain_vec, gate_weight, up_weight):
        hidden_low = gather_cores(norm_rows(residual, gain_vec).astype(BF16))
        grads.hidden_known(hidden_low)
        gate_val = product(hidden_low, gate_weight)
        up_val = product(hidden_low, up_weight)
        act_low = gated_unit(gate_val, up_val).astype(BF16)
        grads.act_known(act_low)
        return gate_val.astype(BF16), up_val.astype(BF16), act_low

    gate_val_a, up_val_a, act_low_a = ffn_units(ffn_a, resid_one, ffn_gain_a, gate_a, up_a)
    resid_two = resid_one + sum_cores(out_product(act_low_a, down_a_pieces))

    low_three = gather_cores(norm_rows(resid_two, attn_gain).astype(BF16))
    low_three, attn_far, down_b_far = tie(low_three, attn_proj, down_b)
    attn_pieces = split_rows(attn_proj, attn_far)
    down_b_pieces = split_rows(down_b, down_b_far)
    attn_rows.left_known(1, low_three)
    query_raw = product(low_three, query_proj)
    key_raw = product(low_three, key_proj)
    value_raw = product(low_three, value_proj)
    packed = heads_forward(query_raw, key_raw, value_raw, starts_here, tables, query_gain_row, key_gain_row)

    team = SEQ if chips == sequences * groups else ("y", "x")
    rest = () if team == SEQ else ("zh", "zl")
    to_heads = partial(lax.all_to_all, axis_name=team, split_axis=0, concat_axis=0, tiled=True)
    packed = to_heads(packed)
    length = packed.shape[0] * seq_rows
    grad_act_b = out_product_back(down_low_b, down_b_pieces)
    packed, down_low_b, grad_act_b = tie(packed, down_low_b, grad_act_b)
    packed = step(packed, (ffn_a, "hidden_second"))
    ffn_b.grad_known(down_low_b)
    if rest:
        kv = lax.all_gather(packed[:, :, LANES:], rest, axis=0, tiled=True)
        attended_low, attended_full, logs = attend(packed, kv, 0, rest, score_scale)
    else:
        attended_low = causal(packed, score_scale)

    def from_heads(block):
        back = to_heads(block.reshape(sequences * groups, seq_rows, -1))
        back = back.reshape(groups, sequences, seq_rows, -1)
        return jnp.transpose(back, (1, 2, 0, 3)).reshape(sequences * seq_rows, -1)

    attended_low = step(attended_low, (ffn_a, "act_second"), (ffn_b, "grad_second"))
    attn_low = from_heads(attended_low)
    mixer_whole = gather_cores(mixer_low, 1)
    attn_low, mixer_whole = tie(attn_low, mixer_whole)
    mixer_rows.left_known(0, mixer_whole)
    attn_low = step(
        attn_low,
        (ffn_a, "hidden_third"),
        (mixer_rows, "second_left_in"),
    )
    resid_three = resid_two + sum_cores(out_product(attn_low, attn_pieces))
    gate_val_b, up_val_b, act_low_b = ffn_units(ffn_b, resid_three, ffn_gain_b, gate_b, up_b)

    def units_back(gate_val, up_val, grad_act):
        _, pull_unit = jax.vjp(gated_unit, gate_val.astype(F32), up_val.astype(F32))
        grad_gate_val, grad_up_val = pull_unit(grad_act)
        return grad_gate_val.astype(BF16), grad_up_val.astype(BF16)

    def norm_back(residual, gain_vec, partial_grad, grad_after):
        _, pull_norm = jax.vjp(norm_rows, residual, gain_vec)
        grad_resid, grad_gain = pull_norm(sum_cores(partial_grad))
        return grad_after + grad_resid, grad_gain

    gate_low, up_low = units_back(gate_val_b, up_val_b, grad_act_b)
    ffn_b.units_known(gate_low, up_low)
    gate_low = step(gate_low, (attn_rows, "second_left_in"))
    grad_three, grad_gain_b = norm_back(
        resid_three, ffn_gain_b, product_nt(gate_low, gate_b) + product_nt(up_low, up_b), grad_out
    )
    grad_attn_low = gather_cores(grad_three.astype(BF16))
    grad_heads = heads_grad(
        half_of(grad_attn_low, core, 1), half_of(grad_attn_low, 1 - core, 1), attn_pieces, sequences
    )
    grad_heads = to_heads(grad_heads).reshape(length, LANES)
    attn_whole = gather_cores(attn_low, 1)
    grad_heads, attn_whole = tie(grad_heads, attn_whole)
    attn_rows.left_known(0, attn_whole)
    grad_heads = step(
        grad_heads,
        (ffn_a, "act_in"),
        (mixer_rows, "first_left_in"),
        (ffn_b, "grad_third"),
        (ffn_b, "units_second"),
        (ffn_b, "act_second"),
        (ffn_b, "hidden_second"),
    )
    if not rest:
        query_grads, kv_grads = causal_back(packed, grad_heads, score_scale)
    else:
        query_grads, kv_grads = attend_back(packed, kv, 0, rest, grad_heads, attended_full, logs, score_scale)
        kv_grads = lax.psum_scatter(kv_grads, rest, scatter_dimension=0, tiled=True)
    query_grads = step(query_grads, (ffn_b, "units_in"), (ffn_b, "hidden_third"))
    packed_grads = jnp.concatenate([query_grads, kv_grads], axis=1)
    packed_grads = to_heads(packed_grads.reshape(sequences * groups, seq_rows, 2 * LANES))
    packed_grads = step(packed_grads, (ffn_b, "act_in"), (attn_rows, "first_left_in"), (ffn_b, "multiply"))
    query_back, key_back, value_back, query_term, key_term = heads_backward(
        packed_grads, query_raw, key_raw, tables, query_gain_row, key_gain_row
    )
    attn_rows.rights_known(
        half_of(grad_attn_low, core, 1), jnp.concatenate([query_back, key_back, value_back], axis=1)
    )
    grad_two, grad_attn_gain = norm_back(
        resid_two,
        attn_gain,
        product_nt(query_back, query_proj) + product_nt(key_back, key_proj) + product_nt(value_back, value_proj),
        grad_three,
    )

    down_low_a = gather_cores(grad_two.astype(BF16))
    ffn_a.grad_known(down_low_a)
    gate_low, up_low = units_back(gate_val_a, up_val_a, out_product_back(down_low_a, down_a_pieces))
    ffn_a.units_known(gate_low, up_low)
    gate_low = step(gate_low, (attn_rows, "multiply"), (ffn_a, "grad_second"))
    grad_one, grad_gain_a = norm_back(
        resid_one, ffn_gain_a, product_nt(gate_low, gate_a) + product_nt(up_low, up_a), grad_two
    )
    grad_one = step(grad_one, (ffn_a, "units_second"))
    grad_mix_low = gather_cores(grad_one.astype(BF16))
    grad_mixer = out_product_back(grad_mix_low, mix_pieces)
    grad_c_part = grad_mixer * mixed_conv
    grad_conv = (grad_mixer * c_part).reshape(sequences, seq_rows, half_width)
    _, pull_conv = jax.vjp(convolve, extended, taps_here)
    grad_extended, grad_taps = pull_conv(grad_conv)
    returned = lax.ppermute(grad_extended[:, :margin, :], SEQ, [(i + 1, i) for i in range(chips - 1)])
    grad_gated = grad_extended[:, margin:, :] + jnp.concatenate(
        [jnp.zeros((sequences, seq_rows - margin, half_width), F32), returned], axis=1
    )
    grad_gated = grad_gated.reshape(-1, half_width)
    grad_gated = step(grad_gated, (ffn_a, "units_in"), (ffn_a, "grad_third"), (ffn_a, "multiply"), (ffn_b, "landed"))
    grad_factor = grad_gated * part_mid
    mid_low = (grad_gated * factor).astype(BF16)
    low_low = jnp.where(core == 0, grad_factor, grad_c_part).astype(BF16)
    high_low = jnp.where(core == 0, grad_c_part, grad_factor).astype(BF16)
    mixer_rows.rights_known(
        half_of(grad_mix_low, core, 1), jnp.concatenate([low_low, swap_cores(mid_low), high_low], axis=1)
    )
    low_low = step(low_low, (attn_rows, "pair_done"))
    partial_one = product_nt(low_low, in_low) + product_nt(mid_low, in_mid) + product_nt(high_low, in_high)
    grad_tokens, grad_mix_gain = norm_back(flat_tokens, mix_gain, partial_one, grad_one)
    tokens_grad = grad_tokens.reshape(streams, seq_rows, width)
    grad_taps = lax.dynamic_update_slice_in_dim(jnp.zeros_like(conv_taps), grad_taps, core * half_width, 1)
    small = jnp.concatenate(
        [
            grad_mix_gain,
            grad_taps.reshape(-1),
            grad_gain_a,
            grad_attn_gain,
            grad_gain_b,
            query_term[0],
            key_term[0],
        ]
    )
    small = step(small, (ffn_b, "fix_first"))
    act_low_b, small = tie(act_low_b, small)
    output = resid_three + sum_cores(out_product(act_low_b, down_b_pieces))
    small = sum_everywhere(small, lambda own: step(own, (ffn_b, "fix_second")))
    small = step(
        small,
        (mixer_rows, "multiply"),
        (ffn_b, "fix_in"),
        (attn_rows, "z_second"),
        (mixer_rows, "pair_done"),
        (ffn_a, "landed"),
        (ffn_a, "fix_first"),
        (mixer_rows, "z_second"),
        (ffn_a, "fix_second"),
        (attn_rows, "z_done"),
    )
    gate_b_grad, up_b_grad, down_b_grad = ffn_b.finish()
    attn_grad, qkv_grad = attn_rows.finish()
    query_columns, key_columns = query_proj.shape[1], key_proj.shape[1]
    taps_end = width + conv_taps.size
    heads_at = taps_end + 3 * width

    def head_gain(offset):
        both = small[offset : offset + LANES]
        return both[:head_width] + both[head_width:]

    early = (
        output.reshape(streams, seq_rows, width),
        tokens_grad,
        small[:width],
        small[width:taps_end].reshape(conv_taps.shape),
        small[taps_end : taps_end + width],
        small[taps_end + width : taps_end + 2 * width],
        qkv_grad[:, :query_columns],
        qkv_grad[:, query_columns : query_columns + key_columns],
        qkv_grad[:, query_columns + key_columns :],
        attn_grad,
        head_gain(heads_at),
        head_gain(heads_at + LANES),
        small[taps_end + 2 * width : taps_end + 3 * width],
        gate_b_grad,
        up_b_grad,
        down_b_grad.T,
    )
    if paired:
        early = tie(*early)
    main, *early = early
    main = step(
        main,
        (ffn_a, "fix_in"),
        (mixer_rows, "z_done"),
    )
    mix_grad, proj_grad = mixer_rows.finish()
    gate_a_grad, up_a_grad, down_a_grad = ffn_a.finish()
    (
        tokens_grad,
        mix_gain_grad,
        taps_grad,
        gain_a_grad,
        attn_gain_grad,
        query_grad,
        key_grad,
        value_grad,
        attn_grad,
        query_gain_grad,
        key_gain_grad,
        gain_b_grad,
        gate_b_grad,
        up_b_grad,
        down_b_grad,
    ) = early
    return (
        main,
        tokens_grad,
        mix_gain_grad,
        proj_grad,
        taps_grad,
        mix_grad,
        gain_a_grad,
        gate_a_grad,
        up_a_grad,
        down_a_grad.T,
        attn_gain_grad,
        query_grad,
        key_grad,
        value_grad,
        attn_grad,
        query_gain_grad,
        key_gain_grad,
        gain_b_grad,
        gate_b_grad,
        up_b_grad,
        down_b_grad,
    )


def chip_grid(chips):
    along_z = math.gcd(4, chips)
    side = math.isqrt(chips // along_z)
    return along_z // 2, 2, chips // along_z // side, side


def solution(mesh):
    cores = mesh.shape["wsh"]
    grid = Mesh(mesh.devices.reshape(*chip_grid(mesh.shape["seq"]), cores), EVERY)
    tokens_spec = P("wsh", SEQ, None)
    columns = P(None, "wsh")
    grads = P(SEQ, "wsh")
    in_specs = (
        tokens_spec,
        P("wsh", SEQ),
        tokens_spec,
        P(),
        columns,
        P(),
        columns,
        P(),
        columns,
        columns,
        columns,
        P(),
        columns,
        columns,
        columns,
        columns,
        P(),
        P(),
        P(),
        columns,
        columns,
        columns,
    )
    out_specs = (
        tokens_spec,
        tokens_spec,
        P(),
        grads,
        P(),
        grads,
        P(),
        grads,
        grads,
        P("wsh", SEQ),
        P(),
        grads,
        grads,
        grads,
        grads,
        P(),
        P(),
        P(),
        grads,
        grads,
        P("wsh", SEQ),
    )
    return jax.shard_map(shards, mesh=grid, in_specs=in_specs, out_specs=out_specs, check_vma=False)
```

```python
from functools import partial
import math

import jax
import jax.numpy as jnp
from jax import lax
from jax.experimental import pallas as pl
from jax.experimental.pallas import tpu as pltpu
from jax.sharding import Mesh, PartitionSpec as P

EPS = 1e-05
ROPE_BASE = 1000000.0
MASKED = -1e30
START_PEAK = -1e25
SEQ = ("zh", "zl", "y", "x")
EVERY = SEQ + ("wsh",)
SWAP = [(0, 1), (1, 0)]
BF16 = jnp.bfloat16
F32 = jnp.float32
LANES = 128


def norm_rows(values, gain_vec):
    return values * lax.rsqrt(jnp.mean(values * values, axis=-1, keepdims=True) + EPS) * gain_vec


def product(left, right):
    return jnp.dot(left, right, preferred_element_type=F32)


def product_tn(left, right):
    return lax.dot_general(left, right, (((0,), (0,)), ((), ())), preferred_element_type=F32)


def product_nt(left, right):
    return lax.dot_general(left, right, (((1,), (1,)), ((), ())), preferred_element_type=F32)


def gated_unit(gate_val, up_val):
    return jax.nn.silu(gate_val) * up_val


def swap_cores(block):
    return lax.ppermute(block, "wsh", SWAP)


def gather_cores(block, axis=0):
    return lax.all_gather(block, "wsh", axis=axis, tiled=True)


def half_of(array, which, axis=0):
    size = array.shape[axis] // 2
    return lax.dynamic_slice_in_dim(array, which * size, size, axis)


def ordered(core, own, other):
    first = jnp.where(core == 0, own, other)
    second = jnp.where(core == 0, other, own)
    return jnp.concatenate([first, second], axis=-1)


def lane_of(shape):
    return lax.broadcasted_iota(jnp.int32, shape, 1)


def two_heads(block):
    return jnp.concatenate([block[:, :64], block[:, 64:]], axis=0)


def side_by_side(block):
    rows = block.shape[0] // 2
    return jnp.concatenate([block[:rows], block[rows:]], axis=1)


EXTRA = 16


def flat(block):
    return block[:, : block.shape[1] - EXTRA].reshape(-1, block.shape[2])


def places(packed_ref, offset):
    chips, padded, _ = packed_ref.shape
    rows = padded - EXTRA
    coded = packed_ref[:, rows, :].astype(F32)
    starts = coded[:, :64] * 64.0 + coded[:, 64:]
    diagonal = lax.broadcasted_iota(jnp.int32, (rows, rows), 0) == lane_of((rows, rows))
    columns = [
        jnp.sum(jnp.where(diagonal, starts[chip : chip + 1], 0.0), axis=1, keepdims=True) for chip in range(chips)
    ]
    starts = jnp.concatenate(columns * 2, axis=0).astype(jnp.int32)
    row = lax.broadcasted_iota(jnp.int32, (2 * chips * rows, 1), 0)
    row = jnp.where(row >= chips * rows, row - chips * rows, row)
    return starts, offset + pl.program_id(0) * chips * rows + row


def first_place(rest, length):
    return lax.axis_index(rest) * length if rest else 0


def lay_out(kv_ref, flat_ref):
    rows = kv_ref.shape[1] - EXTRA

    @pl.when(pl.program_id(0) == 0)
    def _():
        for chip in range(kv_ref.shape[0]):
            flat_ref[chip * rows : (chip + 1) * rows] = kv_ref[chip, :rows]


def attend_kernel(packed_ref, kv_ref, low_ref, full_ref, log_ref, flat_ref, *, rest, span, scale):
    lay_out(kv_ref, flat_ref)
    rows = low_ref.shape[0]
    offset = first_place(rest, rows * pl.num_programs(0))
    query = two_heads(flat(packed_ref[...]))
    starts, mine = places(packed_ref, offset)

    def advance(index, carried):
        peak, total, mixed = carried
        kv_block = flat_ref[pl.ds(pl.multiple_of(index * span, span), span), :]
        scores = product_nt(query, kv_block[:, :64]) * scale
        place = index * span + lane_of((1, span))
        scores = jnp.where((place >= starts) & (place <= mine), scores, MASKED)
        fresh_peak = jnp.maximum(peak, jnp.max(scores, axis=1, keepdims=True))
        shares = jnp.exp(scores - fresh_peak)
        keep = jnp.exp(peak - fresh_peak)
        total = total * keep + jnp.sum(shares, axis=1, keepdims=True)
        mixed = mixed * keep + product(shares.astype(BF16), kv_block[:, 64:])
        return fresh_peak, total, mixed

    last = (offset + (pl.program_id(0) + 1) * rows) // span
    peak, total, mixed = lax.fori_loop(
        0,
        last,
        advance,
        (
            jnp.full((2 * rows, 1), START_PEAK, F32),
            jnp.zeros((2 * rows, 1), F32),
            jnp.zeros((2 * rows, 64), F32),
        ),
    )
    attended = side_by_side(mixed / total)
    low_ref[...] = attended.astype(BF16)
    full_ref[...] = attended
    log_ref[...] = side_by_side(jnp.broadcast_to(peak + jnp.log(total), (2 * rows, 64)))


def attend_back_kernel(packed_ref, kv_ref, grad_ref, full_ref, log_ref, dq_ref, dkv_ref, sums_ref, flat_ref, *, rest, span, scale):
    lay_out(kv_ref, flat_ref)
    rows = grad_ref.shape[0]
    offset = first_place(rest, rows * pl.num_programs(0))
    query = two_heads(flat(packed_ref[...]))
    grad = two_heads(grad_ref[...])
    attended = two_heads(full_ref[...])
    logs = two_heads(log_ref[...])[:, :1]
    delta = jnp.sum(grad.astype(F32) * attended, axis=1, keepdims=True)
    starts, mine = places(packed_ref, offset)

    @pl.when(pl.program_id(0) == 0)
    def _():
        sums_ref[...] = jnp.zeros_like(sums_ref)

    def advance(index, query_grad):
        window = pl.ds(pl.multiple_of(index * span, span), span)
        kv_block = flat_ref[window, :]
        key, value = kv_block[:, :64], kv_block[:, 64:]
        scores = product_nt(query, key) * scale
        place = index * span + lane_of((1, span))
        scores = jnp.where((place >= starts) & (place <= mine), scores, MASKED)
        shares = jnp.exp(scores - logs)
        grad_scores = (shares * (product_nt(grad, value) - delta)).astype(BF16)
        key_grad = product_tn(grad_scores, query) * scale
        value_grad = product_tn(shares.astype(BF16), grad)
        sums_ref[window, :] += jnp.concatenate([key_grad, value_grad], axis=1)
        return query_grad + product(grad_scores, key)

    last = (offset + (pl.program_id(0) + 1) * rows) // span
    query_grad = lax.fori_loop(0, last, advance, jnp.zeros((2 * rows, 64), F32))
    dq_ref[...] = side_by_side(query_grad * scale).astype(BF16)

    @pl.when(pl.program_id(0) == pl.num_programs(0) - 1)
    def _():
        dkv_ref[...] = sums_ref[...].astype(BF16)


def rows_spec(rows, columns, column_block=0):
    return pl.BlockSpec((rows, columns), lambda index: (index, column_block))


def whole_spec(rows, columns, column_block=0):
    return pl.BlockSpec((rows, columns), lambda index: (0, column_block))


def attend_specs(packed, kv, kv_block):
    chips, padded, _ = packed.shape
    per_step = max(1, 256 // (padded - EXTRA))
    packed_spec = pl.BlockSpec((per_step, padded, LANES), lambda index: (index, 0, 0))
    kv_spec = pl.BlockSpec((kv.shape[0], padded, LANES), lambda index: (0, 0, kv_block))
    return chips // per_step, per_step * (padded - EXTRA), [packed_spec, kv_spec]


def attend(packed, kv, kv_block, rest, scale):
    steps, rows, specs = attend_specs(packed, kv, kv_block)
    length, keys = steps * rows, kv.shape[0] * (kv.shape[1] - EXTRA)
    return pl.pallas_call(
        partial(attend_kernel, rest=rest, span=rows, scale=scale),
        grid=(steps,),
        in_specs=specs,
        out_specs=[rows_spec(rows, LANES)] * 3,
        out_shape=[
            jax.ShapeDtypeStruct((length, LANES), BF16),
            jax.ShapeDtypeStruct((length, LANES), F32),
            jax.ShapeDtypeStruct((length, LANES), F32),
        ],
        scratch_shapes=[pltpu.VMEM((keys, LANES), BF16)],
        compiler_params=pltpu.CompilerParams(vmem_limit_bytes=24 << 20),
        cost_estimate=pl.CostEstimate(flops=4 * length * keys * 64, bytes_accessed=2 << 20, transcendentals=length * keys),
    )(packed, kv)


def attend_back(packed, kv, kv_block, rest, grad, full, logs, scale):
    steps, rows, specs = attend_specs(packed, kv, kv_block)
    length, keys = steps * rows, kv.shape[0] * (kv.shape[1] - EXTRA)
    return pl.pallas_call(
        partial(attend_back_kernel, rest=rest, span=rows, scale=scale),
        grid=(steps,),
        in_specs=specs + [rows_spec(rows, LANES)] * 3,
        out_specs=[rows_spec(rows, LANES), whole_spec(keys, LANES)],
        out_shape=[jax.ShapeDtypeStruct((length, LANES), BF16), jax.ShapeDtypeStruct((keys, LANES), BF16)],
        scratch_shapes=[pltpu.VMEM((keys, LANES), F32), pltpu.VMEM((keys, LANES), BF16)],
        compiler_params=pltpu.CompilerParams(vmem_limit_bytes=24 << 20),
        cost_estimate=pl.CostEstimate(flops=10 * length * keys * 64, bytes_accessed=3 << 20, transcendentals=length * keys),
    )(packed, kv, grad, full, logs)


def causal_blocks(packed_ref, scale):
    chips, padded, _ = packed_ref.shape
    rows = padded - EXTRA
    per_block = 256 // rows
    blocks = []
    for first in range(0, chips, per_block):
        packed = packed_ref[first : first + per_block]
        whole = flat(packed)
        coded = packed[:, rows, :LANES].astype(F32)
        starts = coded[:, :64] * 64.0 + coded[:, 64:]
        starts = jnp.concatenate([starts[chip : chip + 1] for chip in range(per_block)] * 2, axis=1)
        place = lane_of((1, 512)) % 256 + first * rows
        query = two_heads(whole[:, :LANES])
        query = (query.astype(F32) * scale).astype(BF16)
        blocks.append((query, whole[:, 128:192], whole[:, 192:], starts.astype(jnp.int32), place))
    return blocks


def causal_shares(blocks, index):
    query, _, _, starts, mine = blocks[index]
    scores = []
    for other in range(index + 1):
        key = blocks[other][1]
        place = lax.broadcasted_iota(jnp.int32, (256, 1), 0) + other * 256
        allowed = place >= starts
        if other == index:
            allowed = allowed & (place <= mine)
        scores.append(jnp.where(allowed, product_nt(key, query), MASKED))
    peak = jnp.max(scores[0], axis=0, keepdims=True)
    for block in scores[1:]:
        peak = jnp.maximum(peak, jnp.max(block, axis=0, keepdims=True))
    shares = [jnp.exp(block - peak) for block in scores]
    total = sum(jnp.sum(block, axis=0, keepdims=True) for block in shares)
    return shares, 1.0 / total


def causal_kernel(packed_ref, low_ref, *, scale):
    blocks = causal_blocks(packed_ref, scale)
    for index in range(len(blocks)):
        shares, inverse = causal_shares(blocks, index)
        mixed = 0.0
        for other, block in enumerate(shares):
            mixed = mixed + product_tn(blocks[other][2], block.astype(BF16))
        attended = (mixed * inverse).T
        low_ref[index * 256 : (index + 1) * 256] = side_by_side(attended).astype(BF16)


def causal_back_kernel(packed_ref, grad_ref, dq_ref, dkv_ref, sums_ref, *, scale):
    blocks = causal_blocks(packed_ref, scale)
    for index in range(len(blocks)):
        here = slice(index * 256, (index + 1) * 256)
        query = blocks[index][0]
        grad = two_heads(grad_ref[here])
        shares, inverse = causal_shares(blocks, index)
        shares = [block * inverse for block in shares]
        grad_shares = [product_nt(blocks[other][2], grad) for other in range(index + 1)]
        delta = sum(
            jnp.sum(share * grad_share, axis=0, keepdims=True) for share, grad_share in zip(shares, grad_shares)
        )
        query_grad = 0.0
        for other, (share, grad_share) in enumerate(zip(shares, grad_shares)):
            grad_scores = (share * (grad_share - delta)).astype(BF16)
            query_grad = query_grad + product_tn(blocks[other][1], grad_scores)
            parts = jnp.concatenate([product(grad_scores, query), product(share.astype(BF16), grad)], axis=1)
            there = slice(other * 256, (other + 1) * 256)
            if other == index:
                sums_ref[there] = parts
            else:
                sums_ref[there] += parts
        dq_ref[here] = side_by_side((query_grad * scale).T).astype(BF16)
    dkv_ref[...] = sums_ref[...].astype(BF16)


def causal(packed, scale):
    length = packed.shape[0] * (packed.shape[1] - EXTRA)
    return pl.pallas_call(
        partial(causal_kernel, scale=scale),
        out_shape=jax.ShapeDtypeStruct((length, LANES), BF16),
        compiler_params=pltpu.CompilerParams(vmem_limit_bytes=32 << 20),
        cost_estimate=pl.CostEstimate(flops=2 * length * length * 128, bytes_accessed=2 << 20, transcendentals=length * length),
    )(packed)


def causal_back(packed, grad, scale):
    length = grad.shape[0]
    return pl.pallas_call(
        partial(causal_back_kernel, scale=scale),
        out_shape=[jax.ShapeDtypeStruct((length, LANES), BF16)] * 2,
        scratch_shapes=[pltpu.VMEM((length, LANES), F32)],
        compiler_params=pltpu.CompilerParams(vmem_limit_bytes=32 << 20),
        cost_estimate=pl.CostEstimate(flops=5 * length * length * 128, bytes_accessed=3 << 20, transcendentals=length * length),
    )(packed, grad)


def heads_grad_kernel(own_ref, other_ref, own_piece_ref, other_piece_ref, out_ref):
    sums = product_nt(own_ref[...], own_piece_ref[...]) + product_nt(other_ref[...], other_piece_ref[...])
    out_ref[...] = sums.astype(BF16).reshape(out_ref.shape)


def heads_grad(own, other, pieces, sequences):
    tokens, columns = own.shape
    groups = pieces[0].shape[0] // LANES
    piece_spec = pl.BlockSpec((LANES, columns), lambda index: (index, 0))
    rows = tokens // sequences
    return pl.pallas_call(
        heads_grad_kernel,
        grid=(groups,),
        in_specs=[whole_spec(tokens, columns)] * 2 + [piece_spec] * 2,
        out_specs=pl.BlockSpec((sequences, rows, LANES), lambda index: (index, 0, 0)),
        out_shape=jax.ShapeDtypeStruct((groups * sequences, rows, LANES), BF16),
        compiler_params=pltpu.CompilerParams(vmem_limit_bytes=16 << 20),
    )(own, other, *pieces)


def head_means(values):
    low_lanes = lane_of(values.shape) < 64
    low_mean = jnp.sum(jnp.where(low_lanes, values, 0.0), axis=1, keepdims=True) * (1.0 / 64)
    high_mean = jnp.sum(jnp.where(low_lanes, 0.0, values), axis=1, keepdims=True) * (1.0 / 64)
    return jnp.where(low_lanes, low_mean, high_mean)


def turn(values, sign):
    lower = (lane_of(values.shape) % 64) < 32
    return jnp.where(lower, -sign * pltpu.roll(values, LANES - 32, 1), sign * pltpu.roll(values, 32, 1))


def head_forward(raw, gain, cosine, sine):
    unit = raw * lax.rsqrt(head_means(raw * raw) + EPS) * gain
    return (unit * cosine + turn(unit, 1.0) * sine).astype(BF16)


def head_backward(raw, gain, cosine, sine, grad):
    back = grad * cosine + turn(grad * sine, -1.0)
    scale = lax.rsqrt(head_means(raw * raw) + EPS)
    gain_term = jnp.sum(back * raw * scale, axis=0, keepdims=True)
    back = back * gain
    raw_grad = back * scale - raw * (scale * scale * scale) * head_means(back * raw)
    return raw_grad.astype(BF16), gain_term


def heads_kernel(query_ref, key_ref, value_ref, starts_ref, cos_ref, sin_ref, query_gain_ref, key_gain_ref, out_ref):
    rows = out_ref.shape[1] - EXTRA
    groups = key_ref.shape[1] // 64
    sequences = query_ref.shape[0] // rows
    cosine, sine = cos_ref[...], sin_ref[...]
    for place in range(sequences):
        span = pl.ds(place * rows, rows)
        starts = jnp.broadcast_to(starts_ref[place : place + 1], (EXTRA, LANES)).astype(BF16)
        for pair in range(groups // 2):
            lanes = pl.ds(pair * LANES, LANES)
            key = head_forward(key_ref[span, lanes], key_gain_ref[...], cosine, sine)
            value = value_ref[span, lanes].astype(BF16)
            for side in range(2):
                group = 2 * pair + side
                query = head_forward(
                    query_ref[span, pl.ds(group * LANES, LANES)], query_gain_ref[...], cosine, sine
                )
                half = slice(64 * side, 64 * side + 64)
                block = group * sequences + place
                out_ref[block, :rows, 0:LANES] = query
                out_ref[block, :rows, LANES : 2 * LANES] = jnp.concatenate([key[:, half], value[:, half]], axis=1)
                out_ref[block, rows:, 0:LANES] = starts
                out_ref[block, rows:, LANES : 2 * LANES] = starts


def heads_back_kernel(
    grad_ref,
    query_ref,
    key_ref,
    cos_ref,
    sin_ref,
    query_gain_ref,
    key_gain_ref,
    dq_ref,
    dk_ref,
    dv_ref,
    query_term_ref,
    key_term_ref,
):
    rows = grad_ref.shape[1]
    groups = key_ref.shape[1] // 64
    sequences = query_ref.shape[0] // rows
    cosine, sine = cos_ref[...], sin_ref[...]
    query_term = jnp.zeros((1, LANES), F32)
    key_term = jnp.zeros((1, LANES), F32)
    for place in range(sequences):
        span = pl.ds(place * rows, rows)
        for pair in range(groups // 2):
            lanes = pl.ds(pair * LANES, LANES)
            sides = [grad_ref[(2 * pair + side) * sequences + place, :, LANES : 2 * LANES] for side in range(2)]
            key_grad = jnp.concatenate([sides[0][:, :64], sides[1][:, :64]], axis=1).astype(F32)
            dv_ref[span, lanes] = jnp.concatenate([sides[0][:, 64:], sides[1][:, 64:]], axis=1)
            low, term = head_backward(key_ref[span, lanes], key_gain_ref[...], cosine, sine, key_grad)
            dk_ref[span, lanes] = low
            key_term = key_term + term
            for side in range(2):
                group = 2 * pair + side
                wide = pl.ds(group * LANES, LANES)
                query_grad = grad_ref[group * sequences + place, :, 0:LANES].astype(F32)
                low, term = head_backward(query_ref[span, wide], query_gain_ref[...], cosine, sine, query_grad)
                dq_ref[span, wide] = low
                query_term = query_term + term
    query_term_ref[...] = query_term
    key_term_ref[...] = key_term


def heads_forward(query, key, value, starts, tables, query_gain, key_gain):
    rows = starts.shape[1]
    blocks = starts.shape[0] * (key.shape[1] // 64)
    coded = jnp.concatenate([starts // 64, starts % 64], axis=1).astype(F32)
    return pl.pallas_call(
        heads_kernel,
        out_shape=jax.ShapeDtypeStruct((blocks, rows + EXTRA, 2 * LANES), BF16),
        compiler_params=pltpu.CompilerParams(vmem_limit_bytes=32 << 20),
    )(query, key, value, coded, *tables, query_gain, key_gain)


def heads_backward(grad, query, key, tables, query_gain, key_gain):
    return pl.pallas_call(
        heads_back_kernel,
        out_shape=[
            jax.ShapeDtypeStruct(query.shape, BF16),
            jax.ShapeDtypeStruct(key.shape, BF16),
            jax.ShapeDtypeStruct(key.shape, BF16),
            jax.ShapeDtypeStruct((1, LANES), F32),
            jax.ShapeDtypeStruct((1, LANES), F32),
        ],
        compiler_params=pltpu.CompilerParams(vmem_limit_bytes=32 << 20),
    )(grad, query, key, *tables, query_gain, key_gain)


def at_place(pieces, place):
    return jnp.where(place == 0, pieces[0], pieces[1])


def quarters(block, dim, core):
    size = block.shape[dim] // 4
    pieces = [lax.slice_in_dim(block, index * size, (index + 1) * size, axis=dim) for index in range(4)]
    return [
        pieces[0],
        jnp.where(core == 0, pieces[2], pieces[1]),
        jnp.where(core == 0, pieces[1], pieces[2]),
        pieces[3],
    ]


def places_here():
    core, x, y = lax.axis_index("wsh"), lax.axis_index("x"), lax.axis_index("y")
    return jnp.where(core == 0, x, y), jnp.where(core == 0, y, x)


def ffn_grad_kernel(meta_ref, *refs):
    hidden, grads = refs[:5], refs[5:10]
    keep_ref, far_ref, last_ref, act_ref, act_far_ref, act_last_ref = refs[10:16]
    outs = refs[16:]
    rows = keep_ref.shape[0]
    core, place = lax.axis_index("wsh"), places_here()[1]

    def tokens_of(left_refs):
        own, near, across, last, last_far = (left_ref[...] for left_ref in left_refs)
        halves = jnp.where(core == 0, last, last_far), jnp.where(core == 0, last_far, last)
        return own, near, across, jnp.concatenate(halves, axis=0)

    def lanes(block):
        pieces = quarters(block, 1, core)
        return jnp.concatenate([at_place(pieces[:2], place), at_place(pieces[2:], place)], axis=1)

    def total(lefts, own_ref, near_ref, pair_ref):
        sums = product_tn(lefts[0], own_ref[...]) + product_tn(lefts[1], near_ref[...])
        return sums + product_tn(lefts[2], pair_ref[:rows]) + product_tn(lefts[3], pair_ref[rows:])

    units = total(tokens_of(hidden), keep_ref, far_ref, last_ref).astype(BF16)
    downs = total([lanes(block) for block in tokens_of(grads)], act_ref, act_far_ref, act_last_ref).astype(BF16)
    unit_rows = units.shape[0]
    step, steps = pl.program_id(0), pl.num_programs(0)

    for place, out_ref in enumerate(outs):

        @pl.when(step * len(outs) // steps == place)
        def _(out_ref=out_ref):
            out_ref[:unit_rows] = units
            out_ref[unit_rows:] = downs


def ffn_grad_rows(hidden, grads, units, acts, whole):
    first, second = places_here()
    zl = lax.axis_index("zl")
    tokens, width = hidden[0].shape
    columns = units[2].shape[1]
    order = (0, 1, 2, 3) if whole else (1 - zl, 3 - zl, zl, 2 + zl)
    meta = jnp.stack([jnp.asarray(value, jnp.int32) for value in (*order, second, first)])

    def left_spec(block):
        return pl.BlockSpec((block.shape[0], width // 4), lambda index, meta_ref: (0, meta_ref[index]))

    def half_spec(position):
        return pl.BlockSpec((tokens, columns), lambda index, meta_ref: (0, meta_ref[position]))

    def full_spec(rows):
        return pl.BlockSpec((rows, columns), lambda index, meta_ref: (0, 0))

    out_rows = width // 4 + width // 8
    outs = 1 if whole else 2
    steps = 4 // outs

    def out_spec(place):
        return pl.BlockSpec((out_rows, columns), lambda index, meta_ref: (jnp.clip(index - place * steps, 0, steps - 1), 0))

    return pl.pallas_call(
        ffn_grad_kernel,
        grid_spec=pltpu.PrefetchScalarGridSpec(
            num_scalar_prefetch=1,
            grid=(4,),
            in_specs=[left_spec(block) for block in (*hidden, *grads)]
            + [half_spec(4), half_spec(4), full_spec(2 * tokens), half_spec(5), full_spec(tokens), full_spec(2 * tokens)],
            out_specs=[out_spec(place) for place in range(outs)],
        ),
        out_shape=[jax.ShapeDtypeStruct((steps * out_rows, columns), BF16)] * outs,
        compiler_params=pltpu.CompilerParams(vmem_limit_bytes=58 << 20),
        cost_estimate=pl.CostEstimate(
            flops=8 * tokens * 4 * out_rows * columns, bytes_accessed=14 << 20, transcendentals=0
        ),
    )(meta, *hidden, *grads, *units, *acts)


def row_kernel(a_ref, a_far_ref, b_ref, b_far_ref, right_ref, right_far_ref, send_ref, keep_ref, *, cut):
    core, (first, second) = lax.axis_index("wsh"), places_here()
    for left_ref, left_far_ref, span in ((a_ref, a_far_ref, slice(0, cut)), (b_ref, b_far_ref, slice(cut, None))):
        sums = product_tn(left_ref[...], right_ref[:, span]) + product_tn(left_far_ref[...], right_far_ref[:, span])
        pieces = quarters(sums, 0, core)
        pieces = [at_place(pieces[0::2], first), at_place(pieces[1::2], first)]
        keep_ref[:, span] = at_place(pieces, second).astype(BF16)
        send_ref[:, span] = at_place(pieces[::-1], second).astype(BF16)


def row_grad_rows(lefts, rights, cut):
    (a, a_far), (b, b_far) = lefts
    tokens, width = a.shape
    columns = rights[0].shape[1]
    out_rows = width // 16
    left_spec = pl.BlockSpec((tokens, width // 4), lambda index: (0, index))
    return pl.pallas_call(
        partial(row_kernel, cut=cut),
        grid=(4,),
        in_specs=[left_spec] * 4 + [whole_spec(tokens, columns)] * 2,
        out_specs=[rows_spec(out_rows, columns)] * 2,
        out_shape=[jax.ShapeDtypeStruct((4 * out_rows, columns), BF16)] * 2,
        compiler_params=pltpu.CompilerParams(vmem_limit_bytes=20 << 20),
        cost_estimate=pl.CostEstimate(flops=4 * tokens * width * columns, bytes_accessed=6 << 20, transcendentals=0),
    )(a, a_far, b, b_far, *rights)


def trade(block, axis):
    return lax.ppermute(block, axis, SWAP)


def trade_mirrored(block, stage):
    route = []
    for index in range(32):
        along_x = (index % 2 == 0) == (stage == 1)
        route.append((index, index ^ (2 if along_x else 4)))
    return lax.ppermute(block, EVERY, route)


def rows_at(blocks, axis, which):
    return lax.dynamic_index_in_dim(blocks, which, axis, keepdims=False)


def add_low(kept, arrived):
    return (kept.astype(F32) + arrived.astype(F32)).astype(BF16)


def tie(*values):
    return lax.optimization_barrier(values)


def sum_everywhere(vector, between):
    devices = lax.axis_size(EVERY)
    piece = -(-vector.size // (devices * LANES)) * LANES
    padded = jnp.pad(vector, (0, devices * piece - vector.size)).reshape(devices, 1, piece)
    turn_over = partial(lax.all_to_all, axis_name=EVERY, split_axis=0, concat_axis=0, tiled=True)
    own = between(jnp.sum(turn_over(padded), axis=0, keepdims=True))
    return turn_over(jnp.broadcast_to(own, (devices, 1, piece))).reshape(-1)


def mirrored_rows(shard, core):
    return jnp.stack(quarters(shard, 0, core)).reshape(2, 2, -1, shard.shape[1])


class AlongZ:
    def z_start(self, main, send, keep):
        main, send, keep = tie(main, send, keep)
        self.part = keep, trade(send, "zl")
        return main

    def z_second(self, main):
        keep, arrived = self.part
        main, arrived = tie(main, arrived)
        summed = add_low(keep, arrived).reshape(2, -1, keep.shape[-1])
        here = lax.axis_index("zh")
        send, keep = rows_at(summed, 0, 1 - here), rows_at(summed, 0, here)
        main, send, keep = tie(main, send, keep)
        self.part = keep, trade(send, "zh")
        return main

    def z_done(self, main):
        keep, arrived = self.part
        main, arrived = tie(main, arrived)
        self.part = keep, arrived
        return main


class FourChips:
    def __init__(self, own):
        self.own, self.near = own, trade_mirrored(own, 1)

    def second(self, main):
        main, near = tie(main, self.near)
        across = swap_cores(near)
        half = half_of(across, lax.axis_index("wsh"))
        main, half = tie(main, half)
        self.near, self.across, self.last = near, across, trade_mirrored(half, 1)
        return main

    def third(self, main):
        main, last = tie(main, self.last)
        self.blocks = self.own, self.near, self.across, last, swap_cores(last)
        return main


class FfnGrads(AlongZ):
    def __init__(self, offload):
        self.core, self.places, self.offload = lax.axis_index("wsh"), places_here(), offload

    def hidden_known(self, hidden):
        self.hidden = FourChips(hidden)

    def act_known(self, act):
        self.act = act
        self.act_far = trade_mirrored(half_of(act, 1 - self.places[0], 1), 1)

    def grad_known(self, grad):
        self.grad = FourChips(grad)

    def units_known(self, gate_low, up_low):
        place = self.places[0]
        self.keep = at_place((gate_low, up_low), place)
        self.far = trade_mirrored(at_place((up_low, gate_low), place), 1)

    def hidden_second(self, main):
        return self.hidden.second(main)

    def hidden_third(self, main):
        return self.hidden.third(main)

    def grad_second(self, main):
        return self.grad.second(main)

    def grad_third(self, main):
        return self.grad.third(main)

    def act_second(self, main):
        main, self.act_far = tie(main, self.act_far)
        main, send = tie(main, jnp.concatenate([half_of(self.act, self.places[0], 1), self.act_far], axis=0))
        self.act_last = trade_mirrored(send, 2)
        return main

    def act_in(self, main):
        main, self.act_last = tie(main, self.act_last)
        return main

    def units_in(self, main):
        main, self.last = tie(main, self.last)
        return main

    def units_second(self, main):
        main, self.far = tie(main, self.far)
        other = 1 - self.places[1]
        main, send = tie(main, jnp.concatenate([half_of(self.keep, other, 1), half_of(self.far, other, 1)], axis=0))
        self.last = trade_mirrored(send, 2)
        return main

    def multiply(self, main):
        main, last, act_last = tie(main, self.last, self.act_last)
        sums = ffn_grad_rows(
            self.hidden.blocks,
            self.grad.blocks,
            (self.keep, self.far, last),
            (self.act, self.act_far, act_last),
            self.offload,
        )
        if not self.offload:
            return self.z_start(main, *sums)
        main, sums = tie(main, *sums)
        self.rows = lax.psum_scatter(sums, ("zh", "zl"), scatter_dimension=0, tiled=True)
        return main

    def landed(self, main):
        main, self.rows = tie(main, self.rows)
        return main

    def fix_first(self, main):
        second = self.places[1]
        rows = self.rows if self.offload else add_low(*self.part)
        unit_rows = rows.shape[0] // 3 * 2
        units = jnp.stack(quarters(rows[:unit_rows], 0, self.core)).reshape(2, 2, -1, rows.shape[1])
        main, send = tie(main, rows_at(units, 1, 1 - second))
        self.units, self.downs = rows_at(units, 1, second), rows[unit_rows:].reshape(2, -1, rows.shape[1])
        self.units_far = trade_mirrored(send, 2)
        return main

    def fix_second(self, main):
        first, second = self.places
        main, far = tie(main, self.units_far)
        units = ordered(second, self.units, far)
        self.own, send = (
            jnp.concatenate([rows_at(units, 0, which), rows_at(self.downs, 0, which)], axis=1)
            for which in (first, 1 - first)
        )
        main, send = tie(main, send)
        self.far = trade_mirrored(send, 1)
        return main

    def fix_in(self, main):
        main, self.far = tie(main, self.far)
        return main

    def finish(self):
        first = self.places[0]
        own, far = self.own.astype(F32), self.far.astype(F32)
        columns = own.shape[1] // 3 * 2
        gate = at_place((own[:, :columns], far[:, :columns]), first)
        up = at_place((far[:, :columns], own[:, :columns]), first)
        return gate, up, ordered(first, own[:, columns:], far[:, columns:])


class RowGrads(AlongZ):
    def __init__(self):
        self.lefts = [None, None]

    def left_known(self, index, left):
        self.lefts[index] = left, trade_mirrored(left, 1)

    def rights_known(self, first, second):
        self.cut = first.shape[1]
        right = jnp.concatenate([first, second], axis=1)
        self.rights = right, trade_mirrored(right, 1)

    def first_left_in(self, main):
        main, self.lefts[0] = tie(main, self.lefts[0])
        return main

    def second_left_in(self, main):
        main, self.lefts[1] = tie(main, self.lefts[1])
        return main

    def multiply(self, main):
        main, far, lefts = tie(main, self.rights[1], self.lefts)
        main, (send, keep) = tie(main, row_grad_rows(lefts, (self.rights[0], far), self.cut))
        self.part = keep, trade_mirrored(send, 2)
        return main

    def pair_done(self, main):
        keep, arrived = self.part
        main, arrived = tie(main, arrived)
        summed = add_low(keep, arrived).reshape(2, 2, -1, keep.shape[-1])
        here = lax.axis_index("zl")
        send, keep = (rows_at(summed, 1, which).reshape(-1, keep.shape[-1]) for which in (1 - here, here))
        return self.z_start(main, send, keep)

    def finish(self):
        keep, arrived = self.part
        summed = keep.astype(F32) + arrived.astype(F32)
        return summed[:, : self.cut], summed[:, self.cut :]


def plain_grad(left, right):
    return lax.psum_scatter(product_tn(left, right).astype(BF16), SEQ, scatter_dimension=0, tiled=True).astype(F32)


class PlainFfnGrads:
    def __init__(self, offload):
        pass

    def hidden_known(self, hidden):
        self.hidden = hidden

    def act_known(self, act):
        self.act = act

    def grad_known(self, grad):
        self.grad = grad

    def units_known(self, gate_low, up_low):
        self.units = gate_low, up_low

    def finish(self):
        gate, up = (plain_grad(self.hidden, unit) for unit in self.units)
        return gate, up, plain_grad(self.grad, self.act)


class PlainRowGrads:
    def __init__(self):
        self.lefts = [None, None]

    def left_known(self, index, left):
        self.lefts[index] = left

    def rights_known(self, *rights):
        self.rights = rights

    def finish(self):
        return tuple(plain_grad(left, right) for left, right in zip(self.lefts, self.rights))


def shards(
    tokens,
    doc_start,
    cotangent,
    mix_gain,
    in_proj,
    conv_taps,
    mix_proj,
    ffn_gain_a,
    gate_a,
    up_a,
    down_a,
    attn_gain,
    query_proj,
    key_proj,
    value_proj,
    attn_proj,
    query_gain,
    key_gain,
    ffn_gain_b,
    gate_b,
    up_b,
    down_b,
):
    streams, seq_rows, width = tokens.shape
    core = lax.axis_index("wsh")
    sequences = streams * lax.axis_size("wsh")
    token_count = streams * seq_rows
    head_width = query_gain.shape[0]
    groups = key_proj.shape[1] // head_width
    score_scale = head_width ** (-0.5)
    margin = conv_taps.shape[0] - 1
    half_width = width // 2
    chips = lax.axis_size(SEQ)
    chip = lax.axis_index(SEQ)
    positions = chip * seq_rows + jnp.arange(seq_rows, dtype=jnp.int32)
    paired = all(lax.axis_size(name) == 2 for name in SEQ)
    ffn_kind, rows_kind = (FfnGrads, RowGrads) if paired else (PlainFfnGrads, PlainRowGrads)
    ffn_a, ffn_b, mixer_rows, attn_rows = ffn_kind(True), ffn_kind(True), rows_kind(), rows_kind()

    def step(main, *events):
        if paired:
            for owner, name in events:
                main = getattr(owner, name)(main)
        return main

    frequency = ROPE_BASE ** (-(jnp.arange(0, head_width, 2, dtype=F32) / head_width))
    angles = positions.astype(F32)[:, None] * jnp.tile(frequency, 4)[None, :]
    tables = (jnp.cos(angles), jnp.sin(angles))
    query_gain_row = jnp.tile(query_gain, 2)[None, :]
    key_gain_row = jnp.tile(key_gain, 2)[None, :]

    def split_rows(weight, sent):
        return half_of(weight, core), half_of(swap_cores(sent), core)

    def out_product(left, pieces):
        return ordered(core, product(left, pieces[0]), product(left, pieces[1]))

    def out_product_back(grad, pieces):
        own = half_of(grad, core, 1)
        other = half_of(grad, 1 - core, 1)
        return product_nt(own, pieces[0]) + product_nt(other, pieces[1])

    def sum_cores(partial_rows):
        arrived = swap_cores(half_of(partial_rows, 1 - core).astype(BF16))
        return half_of(partial_rows, core) + arrived.astype(F32)

    starts_far = swap_cores(doc_start)
    starts_here = jnp.concatenate(
        [jnp.where(core == 0, doc_start, starts_far), jnp.where(core == 0, starts_far, doc_start)], axis=0
    )
    in_far = swap_cores(in_proj)
    in_low, in_high = in_proj[:, :half_width], in_proj[:, 2 * half_width :]
    in_mid = in_far[:, half_width : 2 * half_width]

    grad_out = cotangent.reshape(token_count, width)
    down_low_b = gather_cores(grad_out.astype(BF16))
    flat_tokens = tokens.reshape(token_count, width)
    low_one = gather_cores(norm_rows(flat_tokens, mix_gain).astype(BF16))
    low_one, mix_far, down_a_far = tie(low_one, mix_proj, down_a)
    mix_pieces = split_rows(mix_proj, mix_far)
    down_a_pieces = split_rows(down_a, down_a_far)
    part_low = product(low_one, in_low)
    part_mid = product(low_one, in_mid)
    part_high = product(low_one, in_high)
    factor = jnp.where(core == 0, part_low, part_high)
    c_part = jnp.where(core == 0, part_high, part_low)
    gated = (part_mid * factor).reshape(sequences, seq_rows, half_width)
    edge_rows = lax.ppermute(gated[:, seq_rows - margin :, :], SEQ, [(i, i + 1) for i in range(chips - 1)])
    extended = jnp.concatenate([edge_rows, gated], axis=1)
    taps_here = half_of(conv_taps, core, 1)

    def convolve(extended_rows, taps_now):
        running = jnp.zeros_like(extended_rows[:, margin:])
        for tap_index in range(margin + 1):
            offset = margin - tap_index
            shifted = extended_rows[:, tap_index : tap_index + seq_rows]
            allowed = (positions[None, :] - offset >= starts_here)[:, :, None]
            running = running + jnp.where(allowed, shifted, 0.0) * taps_now[tap_index]
        return running

    mixed_conv = convolve(extended, taps_here).reshape(-1, half_width)
    mixer_low = (c_part * mixed_conv).astype(BF16)
    mixer_rows.left_known(1, low_one)
    resid_one = flat_tokens + sum_cores(out_product(mixer_low, mix_pieces))

    def ffn_units(grads, residual, gain_vec, gate_weight, up_weight):
        hidden_low = gather_cores(norm_rows(residual, gain_vec).astype(BF16))
        grads.hidden_known(hidden_low)
        gate_val = product(hidden_low, gate_weight)
        up_val = product(hidden_low, up_weight)
        act_low = gated_unit(gate_val, up_val).astype(BF16)
        grads.act_known(act_low)
        return gate_val.astype(BF16), up_val.astype(BF16), act_low

    gate_val_a, up_val_a, act_low_a = ffn_units(ffn_a, resid_one, ffn_gain_a, gate_a, up_a)
    resid_two = resid_one + sum_cores(out_product(act_low_a, down_a_pieces))

    low_three = gather_cores(norm_rows(resid_two, attn_gain).astype(BF16))
    low_three, attn_far, down_b_far = tie(low_three, attn_proj, down_b)
    attn_pieces = split_rows(attn_proj, attn_far)
    down_b_pieces = split_rows(down_b, down_b_far)
    attn_rows.left_known(1, low_three)
    query_raw = product(low_three, query_proj)
    key_raw = product(low_three, key_proj)
    value_raw = product(low_three, value_proj)
    packed = heads_forward(query_raw, key_raw, value_raw, starts_here, tables, query_gain_row, key_gain_row)

    team = SEQ if chips == sequences * groups else ("y", "x")
    rest = () if team == SEQ else ("zh", "zl")
    to_heads = partial(lax.all_to_all, axis_name=team, split_axis=0, concat_axis=0, tiled=True)
    packed = to_heads(packed)
    length = packed.shape[0] * seq_rows
    grad_act_b = out_product_back(down_low_b, down_b_pieces)
    packed, down_low_b, grad_act_b = tie(packed, down_low_b, grad_act_b)
    packed = step(packed, (ffn_a, "hidden_second"))
    ffn_b.grad_known(down_low_b)
    if rest:
        kv = lax.all_gather(packed[:, :, LANES:], rest, axis=0, tiled=True)
        attended_low, attended_full, logs = attend(packed, kv, 0, rest, score_scale)
    else:
        attended_low = causal(packed, score_scale)

    def from_heads(block):
        back = to_heads(block.reshape(sequences * groups, seq_rows, -1))
        back = back.reshape(groups, sequences, seq_rows, -1)
        return jnp.transpose(back, (1, 2, 0, 3)).reshape(sequences * seq_rows, -1)

    attended_low = step(attended_low, (ffn_a, "act_second"), (ffn_b, "grad_second"))
    attn_low = from_heads(attended_low)
    mixer_whole = gather_cores(mixer_low, 1)
    attn_low, mixer_whole = tie(attn_low, mixer_whole)
    mixer_rows.left_known(0, mixer_whole)
    attn_low = step(
        attn_low,
        (ffn_a, "hidden_third"),
        (mixer_rows, "second_left_in"),
    )
    resid_three = resid_two + sum_cores(out_product(attn_low, attn_pieces))
    gate_val_b, up_val_b, act_low_b = ffn_units(ffn_b, resid_three, ffn_gain_b, gate_b, up_b)

    def units_back(gate_val, up_val, grad_act):
        _, pull_unit = jax.vjp(gated_unit, gate_val.astype(F32), up_val.astype(F32))
        grad_gate_val, grad_up_val = pull_unit(grad_act)
        return grad_gate_val.astype(BF16), grad_up_val.astype(BF16)

    def norm_back(residual, gain_vec, partial_grad, grad_after):
        _, pull_norm = jax.vjp(norm_rows, residual, gain_vec)
        grad_resid, grad_gain = pull_norm(sum_cores(partial_grad))
        return grad_after + grad_resid, grad_gain

    gate_low, up_low = units_back(gate_val_b, up_val_b, grad_act_b)
    ffn_b.units_known(gate_low, up_low)
    gate_low = step(gate_low, (attn_rows, "second_left_in"))
    grad_three, grad_gain_b = norm_back(
        resid_three, ffn_gain_b, product_nt(gate_low, gate_b) + product_nt(up_low, up_b), grad_out
    )
    grad_attn_low = gather_cores(grad_three.astype(BF16))
    grad_heads = heads_grad(
        half_of(grad_attn_low, core, 1), half_of(grad_attn_low, 1 - core, 1), attn_pieces, sequences
    )
    grad_heads = to_heads(grad_heads).reshape(length, LANES)
    attn_whole = gather_cores(attn_low, 1)
    grad_heads, attn_whole = tie(grad_heads, attn_whole)
    attn_rows.left_known(0, attn_whole)
    grad_heads = step(
        grad_heads,
        (ffn_a, "act_in"),
        (mixer_rows, "first_left_in"),
        (ffn_b, "grad_third"),
        (ffn_b, "units_second"),
        (ffn_b, "act_second"),
        (ffn_b, "hidden_second"),
    )
    if not rest:
        query_grads, kv_grads = causal_back(packed, grad_heads, score_scale)
    else:
        query_grads, kv_grads = attend_back(packed, kv, 0, rest, grad_heads, attended_full, logs, score_scale)
        kv_grads = lax.psum_scatter(kv_grads, rest, scatter_dimension=0, tiled=True)
    query_grads = step(query_grads, (ffn_b, "units_in"), (ffn_b, "hidden_third"))
    packed_grads = jnp.concatenate([query_grads, kv_grads], axis=1)
    packed_grads = to_heads(packed_grads.reshape(sequences * groups, seq_rows, 2 * LANES))
    packed_grads = step(packed_grads, (ffn_b, "act_in"), (attn_rows, "first_left_in"), (ffn_b, "multiply"))
    query_back, key_back, value_back, query_term, key_term = heads_backward(
        packed_grads, query_raw, key_raw, tables, query_gain_row, key_gain_row
    )
    attn_rows.rights_known(
        half_of(grad_attn_low, core, 1), jnp.concatenate([query_back, key_back, value_back], axis=1)
    )
    grad_two, grad_attn_gain = norm_back(
        resid_two,
        attn_gain,
        product_nt(query_back, query_proj) + product_nt(key_back, key_proj) + product_nt(value_back, value_proj),
        grad_three,
    )

    down_low_a = gather_cores(grad_two.astype(BF16))
    ffn_a.grad_known(down_low_a)
    gate_low, up_low = units_back(gate_val_a, up_val_a, out_product_back(down_low_a, down_a_pieces))
    ffn_a.units_known(gate_low, up_low)
    gate_low = step(gate_low, (attn_rows, "multiply"), (ffn_a, "grad_second"))
    grad_one, grad_gain_a = norm_back(
        resid_one, ffn_gain_a, product_nt(gate_low, gate_a) + product_nt(up_low, up_a), grad_two
    )
    grad_one = step(grad_one, (ffn_a, "units_second"))
    grad_mix_low = gather_cores(grad_one.astype(BF16))
    grad_mixer = out_product_back(grad_mix_low, mix_pieces)
    grad_c_part = grad_mixer * mixed_conv
    grad_conv = (grad_mixer * c_part).reshape(sequences, seq_rows, half_width)
    _, pull_conv = jax.vjp(convolve, extended, taps_here)
    grad_extended, grad_taps = pull_conv(grad_conv)
    returned = lax.ppermute(grad_extended[:, :margin, :], SEQ, [(i + 1, i) for i in range(chips - 1)])
    grad_gated = grad_extended[:, margin:, :] + jnp.concatenate(
        [jnp.zeros((sequences, seq_rows - margin, half_width), F32), returned], axis=1
    )
    grad_gated = grad_gated.reshape(-1, half_width)
    grad_gated = step(grad_gated, (ffn_a, "units_in"), (ffn_a, "grad_third"), (ffn_a, "multiply"), (ffn_b, "landed"))
    grad_factor = grad_gated * part_mid
    mid_low = (grad_gated * factor).astype(BF16)
    low_low = jnp.where(core == 0, grad_factor, grad_c_part).astype(BF16)
    high_low = jnp.where(core == 0, grad_c_part, grad_factor).astype(BF16)
    mixer_rows.rights_known(
        half_of(grad_mix_low, core, 1), jnp.concatenate([low_low, swap_cores(mid_low), high_low], axis=1)
    )
    low_low = step(low_low, (attn_rows, "pair_done"))
    partial_one = product_nt(low_low, in_low) + product_nt(mid_low, in_mid) + product_nt(high_low, in_high)
    grad_tokens, grad_mix_gain = norm_back(flat_tokens, mix_gain, partial_one, grad_one)
    tokens_grad = grad_tokens.reshape(streams, seq_rows, width)
    grad_taps = lax.dynamic_update_slice_in_dim(jnp.zeros_like(conv_taps), grad_taps, core * half_width, 1)
    small = jnp.concatenate(
        [
            grad_mix_gain,
            grad_taps.reshape(-1),
            grad_gain_a,
            grad_attn_gain,
            grad_gain_b,
            query_term[0],
            key_term[0],
        ]
    )
    small = step(small, (ffn_b, "fix_first"))
    act_low_b, small = tie(act_low_b, small)
    output = resid_three + sum_cores(out_product(act_low_b, down_b_pieces))
    small = sum_everywhere(small, lambda own: step(own, (ffn_b, "fix_second")))
    small = step(
        small,
        (mixer_rows, "multiply"),
        (ffn_b, "fix_in"),
        (attn_rows, "z_second"),
        (mixer_rows, "pair_done"),
        (ffn_a, "landed"),
        (ffn_a, "fix_first"),
        (mixer_rows, "z_second"),
        (ffn_a, "fix_second"),
        (attn_rows, "z_done"),
    )
    gate_b_grad, up_b_grad, down_b_grad = ffn_b.finish()
    attn_grad, qkv_grad = attn_rows.finish()
    query_columns, key_columns = query_proj.shape[1], key_proj.shape[1]
    taps_end = width + conv_taps.size
    heads_at = taps_end + 3 * width

    def head_gain(offset):
        both = small[offset : offset + LANES]
        return both[:head_width] + both[head_width:]

    early = (
        output.reshape(streams, seq_rows, width),
        tokens_grad,
        small[:width],
        small[width:taps_end].reshape(conv_taps.shape),
        small[taps_end : taps_end + width],
        small[taps_end + width : taps_end + 2 * width],
        qkv_grad[:, :query_columns],
        qkv_grad[:, query_columns : query_columns + key_columns],
        qkv_grad[:, query_columns + key_columns :],
        attn_grad,
        head_gain(heads_at),
        head_gain(heads_at + LANES),
        small[taps_end + 2 * width : taps_end + 3 * width],
        gate_b_grad,
        up_b_grad,
        down_b_grad.T,
    )
    if paired:
        early = tie(*early)
    main, *early = early
    main = step(
        main,
        (ffn_a, "fix_in"),
        (mixer_rows, "z_done"),
    )
    mix_grad, proj_grad = mixer_rows.finish()
    gate_a_grad, up_a_grad, down_a_grad = ffn_a.finish()
    (
        tokens_grad,
        mix_gain_grad,
        taps_grad,
        gain_a_grad,
        attn_gain_grad,
        query_grad,
        key_grad,
        value_grad,
        attn_grad,
        query_gain_grad,
        key_gain_grad,
        gain_b_grad,
        gate_b_grad,
        up_b_grad,
        down_b_grad,
    ) = early
    return (
        main,
        tokens_grad,
        mix_gain_grad,
        proj_grad,
        taps_grad,
        mix_grad,
        gain_a_grad,
        gate_a_grad,
        up_a_grad,
        down_a_grad.T,
        attn_gain_grad,
        query_grad,
        key_grad,
        value_grad,
        attn_grad,
        query_gain_grad,
        key_gain_grad,
        gain_b_grad,
        gate_b_grad,
        up_b_grad,
        down_b_grad,
    )


def chip_grid(chips):
    along_z = math.gcd(4, chips)
    side = math.isqrt(chips // along_z)
    return along_z // 2, 2, chips // along_z // side, side


def solution(mesh):
    cores = mesh.shape["wsh"]
    grid = Mesh(mesh.devices.reshape(*chip_grid(mesh.shape["seq"]), cores), EVERY)
    tokens_spec = P("wsh", SEQ, None)
    columns = P(None, "wsh")
    grads = P(SEQ, "wsh")
    in_specs = (
        tokens_spec,
        P("wsh", SEQ),
        tokens_spec,
        P(),
        columns,
        P(),
        columns,
        P(),
        columns,
        columns,
        columns,
        P(),
        columns,
        columns,
        columns,
        columns,
        P(),
        P(),
        P(),
        columns,
        columns,
        columns,
    )
    out_specs = (
        tokens_spec,
        tokens_spec,
        P(),
        grads,
        P(),
        grads,
        P(),
        grads,
        grads,
        P("wsh", SEQ),
        P(),
        grads,
        grads,
        grads,
        grads,
        P(),
        P(),
        P(),
        grads,
        grads,
        P("wsh", SEQ),
    )
    return jax.shard_map(shards, mesh=grid, in_specs=in_specs, out_specs=out_specs, check_vma=False)
```
